128 devices in a mesh: rep: 4 (over y_hi, core), grp: 16 (over z, x), tp: 2 (over y_lo).
Axes of the slice: x: 4, y: 4 (y_hi: 2, y_lo: 2; y = y_hi * 2 + y_lo), z: 4, core: 2. Of those that a mesh axis runs over, the one named last changes fastest.
Arguments:
- tokens: bfloat16 [8, 2048, 2048], P('rep', 'grp'), may hold values from -6 to 6
- cotangent: bfloat16 [8, 2048, 2048], P('rep', 'grp'), may hold values from -6 to 6
- offsets: int32 [8, 16], P('rep'), may hold values from 0 to 1920, as said below
- w_query: float32 [2048, 2048], P('grp', 'tp'), may hold values from -0.125 to 0.125
- moment_query: float32 [2048, 2048], P('grp', 'tp'), may hold values from -112 to 112
- square_query: float32 [2048, 2048], P('grp', 'tp'), may hold values from 1310.72 to 9175.04
- w_keyval: float32 [2048, 2, 256], P('grp', None, 'tp'), may hold values from -0.125 to 0.125
- moment_keyval: float32 [2048, 2, 256], P('grp', None, 'tp'), may hold values from -112 to 112
- square_keyval: float32 [2048, 2, 256], P('grp', None, 'tp'), may hold values from 1310.72 to 9175.04
- w_out: float32 [2048, 2048], P('grp', 'tp'), may hold values from -4 to 4
- moment_out: float32 [2048, 2048], P('grp', 'tp'), may hold values from -4 to 4
- square_out: float32 [2048, 2048], P('grp', 'tp'), may hold values from 1.28 to 8.96
- w_gateup: float32 [2048, 2, 5632], P('grp', None, 'tp'), may hold values from -0.125 to 0.125
- moment_gateup: float32 [2048, 2, 5632], P('grp', None, 'tp'), may hold values from -28 to 28
- square_gateup: float32 [2048, 2, 5632], P('grp', None, 'tp'), may hold values from 72.0896 to 507.904
- w_down: float32 [2048, 5632], P('grp', 'tp'), may hold values from -0.078125 to 0.078125
- moment_down: float32 [2048, 5632], P('grp', 'tp'), may hold values from -48 to 48
- square_down: float32 [2048, 5632], P('grp', 'tp'), may hold values from 235.9296 to 1638.4
- norm_gains: float32 [2048, 2], P('grp'), may hold values from 0.5 to 1.5
- moment_gains: float32 [2048, 2], P('grp'), may hold values from -96 to 96
- square_gains: float32 [2048, 2], P('grp'), may hold values from 950.272 to 6553.6
Outputs:
- layer_out: bfloat16 [8, 2048, 2048], P('rep', 'grp')
- input_grad: float32 [8, 2048, 2048], P('rep', 'grp')
- new_query: float32 [2048, 2048], P('grp', 'tp')
- new_moment_query: float32 [2048, 2048], P('grp', 'tp')
- new_square_query: float32 [2048, 2048], P('grp', 'tp')
- new_keyval: float32 [2048, 2, 256], P('grp', None, 'tp')
- new_moment_keyval: float32 [2048, 2, 256], P('grp', None, 'tp')
- new_square_keyval: float32 [2048, 2, 256], P('grp', None, 'tp')
- new_out: float32 [2048, 2048], P('grp', 'tp')
- new_moment_out: float32 [2048, 2048], P('grp', 'tp')
- new_square_out: float32 [2048, 2048], P('grp', 'tp')
- new_gateup: float32 [2048, 2, 5632], P('grp', None, 'tp')
- new_moment_gateup: float32 [2048, 2, 5632], P('grp', None, 'tp')
- new_square_gateup: float32 [2048, 2, 5632], P('grp', None, 'tp')
- new_down: float32 [2048, 5632], P('grp', 'tp')
- new_moment_down: float32 [2048, 5632], P('grp', 'tp')
- new_square_down: float32 [2048, 5632], P('grp', 'tp')
- new_gains: float32 [2048, 2], P('grp')
- new_moment_gains: float32 [2048, 2], P('grp')
- new_square_gains: float32 [2048, 2], P('grp')
The draws below stay inside these ranges and needn't reach their ends.
Inputs may be any that keep to these rules, and one draw needn't show every extreme that they name: `offsets`: in each row the entries are the multiples 0, 128, ..., 1920, each once, in an order drawn per sequence.
All inputs are finite; a program needn't handle non-finite values.
Results may differ from the reference program's by a relative error of at most 0.024.
Values may be sent and summed in bfloat16 or wider, within the bound.
No kernel may reach another device: no remote copies, remote signals or barrier semaphores. Data moves between devices by JAX's collectives and lax.ppermute only.
A program may use at most 320 MiB of HBM per device.

```python
import math
import jax
import jax.numpy as jnp
from jax import lax

D = 2048
HEADS = 32
KV_HEADS = 4
HEAD_DIM = 64
FF = 5632
LENGTH = 2048
STEP = 10
SPAN = 128
BATCH = 8
TOKENS = 16384


def draw_offsets(key, part):
    key = jax.random.fold_in(key, 11)
    blocks = LENGTH // SPAN
    row_keys = jax.random.split(key, BATCH)
    orders = jax.vmap(lambda row_key: jax.random.permutation(row_key, blocks))(row_keys)
    return (orders * SPAN).astype(jnp.int32)


def steps_of(own_key, shape, cuts, smallest, largest):
    level = 1.0
    for dim, blocks in cuts:
        draws = jax.random.uniform(jax.random.fold_in(jax.random.fold_in(own_key, 6), dim), (blocks,), jnp.float32, smallest / len(cuts), largest / len(cuts))
        level = level * jnp.repeat(jnp.exp(draws), shape[dim] // blocks).reshape((-1,) + (1,) * (len(shape) - 1 - dim))
    return level


def bell_draw(stream_key, dims, scale, limit, shards=(), held_as=jnp.bfloat16):
    level = steps_of(stream_key, dims, shards, -0.22, 0.18) if shards else 1.0
    array = jax.random.normal(stream_key, dims, jnp.float32) * scale * level
    return jnp.minimum(jnp.maximum(array, -limit), limit).astype(held_as)


def setup_inputs(seed: int = 0) -> dict:
    arg_keys = jax.random.split(jax.random.key(seed), 22)
    tokens = bell_draw(arg_keys[0], (BATCH, LENGTH, D), 1.0, 6.0, ((0, 4), (1, 16)))
    cotangent = bell_draw(arg_keys[1], (BATCH, LENGTH, D), 1.0, 6.0, ((0, 4), (1, 16)))
    offsets = draw_offsets(jax.random.fold_in(arg_keys[21], 71), 0)
    w_query = bell_draw(arg_keys[3], (D, HEADS * HEAD_DIM), D ** -0.5, 0.125, ((0, 16), (1, 2)), jnp.float32)
    moment_query = bell_draw(arg_keys[4], (D, HEADS * HEAD_DIM), (0.15 * TOKENS ** 0.5), 112.0, ((0, 16), (1, 2)), jnp.float32)
    square_query = jnp.clip(jnp.exp(math.log(9175.04) - 1.9459102 * jax.random.uniform(arg_keys[5], (D, HEADS * HEAD_DIM), jnp.float32) ** steps_of(arg_keys[5], (D, HEADS * HEAD_DIM), ((0, 16), (1, 2)), -0.2, 0.2)), 1310.72, 9175.04)
    w_keyval = bell_draw(arg_keys[6], (D, 2, KV_HEADS * HEAD_DIM), D ** -0.5, 0.125, ((0, 16), (2, 2)), jnp.float32)
    moment_keyval = bell_draw(arg_keys[7], (D, 2, KV_HEADS * HEAD_DIM), (0.15 * TOKENS ** 0.5), 112.0, ((0, 16), (2, 2)), jnp.float32)
    square_keyval = jnp.clip(jnp.exp(math.log(9175.04) - 1.9459102 * jax.random.uniform(arg_keys[8], (D, 2, KV_HEADS * HEAD_DIM), jnp.float32) ** steps_of(arg_keys[8], (D, 2, KV_HEADS * HEAD_DIM), ((0, 16), (2, 2)), -0.2, 0.2)), 1310.72, 9175.04)
    w_out = bell_draw(arg_keys[9], (D, HEADS * HEAD_DIM), (max(1, 2 * D // LENGTH)) ** -0.5, 4.0, ((0, 16), (1, 2)), jnp.float32)
    moment_out = bell_draw(arg_keys[10], (D, HEADS * HEAD_DIM), (0.22 * (TOKENS // LENGTH) ** 0.5), 4.0, ((0, 16), (1, 2)), jnp.float32)
    square_out = jnp.clip(jnp.exp(math.log(8.96) - 1.9459102 * jax.random.uniform(arg_keys[11], (D, HEADS * HEAD_DIM), jnp.float32) ** steps_of(arg_keys[11], (D, HEADS * HEAD_DIM), ((0, 16), (1, 2)), -0.2, 0.2)), 1.28, 8.96)
    w_gateup = bell_draw(arg_keys[12], (D, 2, FF), D ** -0.5, 0.125, ((0, 16), (2, 2)), jnp.float32)
    moment_gateup = bell_draw(arg_keys[13], (D, 2, FF), (0.037 * TOKENS ** 0.5), 28.0, ((0, 16), (2, 2)), jnp.float32)
    square_gateup = jnp.clip(jnp.exp(math.log(507.904) - 1.9523827 * jax.random.uniform(arg_keys[14], (D, 2, FF), jnp.float32) ** steps_of(arg_keys[14], (D, 2, FF), ((0, 16), (2, 2)), -0.2, 0.2)), 72.0896, 507.904)
    w_down = bell_draw(arg_keys[15], (D, FF), FF ** -0.5, 0.078125, ((0, 16), (1, 2)), jnp.float32)
    moment_down = bell_draw(arg_keys[16], (D, FF), (0.066 * TOKENS ** 0.5), 48.0, ((0, 16), (1, 2)), jnp.float32)
    square_down = jnp.clip(jnp.exp(math.log(1638.4) - 1.937942 * jax.random.uniform(arg_keys[17], (D, FF), jnp.float32) ** steps_of(arg_keys[17], (D, FF), ((0, 16), (1, 2)), -0.2, 0.2)), 235.9296, 1638.4)
    norm_gains = jnp.clip(1.0 + 0.1 * jax.random.normal(arg_keys[18], (D, 2), jnp.float32), 0.5, 1.5)
    moment_gains = bell_draw(arg_keys[19], (D, 2), (0.13 * TOKENS ** 0.5), 96.0, ((0, 16),), jnp.float32)
    square_gains = jnp.clip(jnp.exp(math.log(6553.6) - 1.9310216 * jax.random.uniform(arg_keys[20], (D, 2), jnp.float32) ** steps_of(arg_keys[20], (D, 2), ((0, 16),), -0.2, 0.2)), 950.272, 6553.6)
    return {"tokens": tokens, "cotangent": cotangent, "offsets": offsets, "w_query": w_query, "moment_query": moment_query, "square_query": square_query, "w_keyval": w_keyval, "moment_keyval": moment_keyval, "square_keyval": square_keyval, "w_out": w_out, "moment_out": moment_out, "square_out": square_out, "w_gateup": w_gateup, "moment_gateup": moment_gateup, "square_gateup": square_gateup, "w_down": w_down, "moment_down": moment_down, "square_down": square_down, "norm_gains": norm_gains, "moment_gains": moment_gains, "square_gains": square_gains}


@jax.custom_vjp
def low(v):
    return lax.optimization_barrier(v.astype(jnp.bfloat16)).astype(jnp.float32)

@jax.custom_vjp
def low_back(v):
    return v

def low_keep(v):
    return (low(v), None)

def low_pass(kept, grad):
    return (grad,)

def back_keep(v):
    return (v, None)

def back_low(kept, grad):
    return (low(grad),)
low.defvjp(low_keep, low_pass)
low_back.defvjp(back_keep, back_low)
norm_epsilon = 1e-05
rope_base = 10000.0
neg_large = -1e+30
beta_first = 0.9
beta_second = 0.95
adam_epsilon = 1e-08
decay_rate = 0.1

def hdot(left, right):
    return jnp.dot(left, right, precision=lax.Precision.HIGHEST, preferred_element_type=jnp.float32)

def rms_gain(values, gain):
    return values * lax.rsqrt(lax.optimization_barrier(jnp.mean(values * values, axis=-1, keepdims=True)) + norm_epsilon) * gain

def rope_tables(positions):
    half_dim = HEAD_DIM // 2
    inverse = rope_base ** (-2.0 * jnp.arange(half_dim, dtype=jnp.float32) / HEAD_DIM)
    angles = positions.astype(jnp.float32)[:, None] * inverse[None, :]
    return (jnp.cos(angles)[:, None, :], jnp.sin(angles)[:, None, :])

def rotate(vector, cosine_table, sine_table):
    half_dim = vector.shape[-1] // 2
    first_half = vector[..., :half_dim]
    second_half = vector[..., half_dim:]
    return jnp.concatenate([first_half * cosine_table - second_half * sine_table, second_half * cosine_table + first_half * sine_table], axis=-1)

def layer(inputs, positions, w_query, w_keyval, w_out, w_gateup, w_down, norm_gains):
    seq_len = inputs.shape[0]
    head_ratio = HEADS // KV_HEADS
    gains = low(norm_gains)
    h_one = low(rms_gain(inputs, gains[:, 0]))
    query_pre = low_back(hdot(h_one, low(w_query))).reshape(seq_len, HEADS, HEAD_DIM)
    key_pre = low_back(hdot(h_one, low(w_keyval[:, 0]))).reshape(seq_len, KV_HEADS, HEAD_DIM)
    values = low(low_back(hdot(h_one, low(w_keyval[:, 1])))).reshape(seq_len, KV_HEADS, HEAD_DIM)
    cosine_table, sine_table = rope_tables(positions)
    queries = low(rotate(query_pre, cosine_table, sine_table) * HEAD_DIM ** (-0.5))
    keys = low(rotate(key_pre, cosine_table, sine_table))
    allowed = positions[None, :] <= positions[:, None]
    grouped = queries.reshape(seq_len, KV_HEADS, head_ratio, HEAD_DIM).transpose(1, 2, 0, 3)

    def one_head(pieces):
        query_group, key_head, value_head = pieces
        scores = low_back(jnp.einsum('gqd,kd->gqk', query_group, key_head, precision=lax.Precision.HIGHEST))
        scores = jnp.where(allowed[None], scores, neg_large)
        attn_probs = low(jax.nn.softmax(scores, axis=-1))
        return low(low_back(jnp.einsum('gqk,kd->gqd', attn_probs, value_head, precision=lax.Precision.HIGHEST)))
    mixed_heads = lax.map(jax.checkpoint(one_head), (grouped, keys.transpose(1, 0, 2), values.transpose(1, 0, 2)))
    mixed_heads = mixed_heads.transpose(2, 0, 1, 3).reshape(seq_len, HEADS * HEAD_DIM)
    attn_branch = low_back(lax.dot_general(mixed_heads, low(w_out), (((1,), (1,)), ((), ())), precision=lax.Precision.HIGHEST, preferred_element_type=jnp.float32))
    middle = inputs + attn_branch
    h_two = low(rms_gain(middle, gains[:, 1]))
    gate_pre = low_back(hdot(h_two, low(w_gateup[:, 0])))
    up_value = low_back(hdot(h_two, low(w_gateup[:, 1])))
    hidden = low(jax.nn.silu(gate_pre) * up_value)
    mlp_branch = low_back(lax.dot_general(hidden, low(w_down), (((1,), (1,)), ((), ())), precision=lax.Precision.HIGHEST, preferred_element_type=jnp.float32))
    return middle + mlp_branch

def adamw(weight, moment, square, grad, rate, decay):
    moment = beta_first * moment + (1.0 - beta_first) * grad
    square = beta_second * square + (1.0 - beta_second) * grad * grad
    fix_first = 1.0 - beta_first ** STEP
    fix_second = 1.0 - beta_second ** STEP
    update = moment / fix_first / (jnp.sqrt(square / fix_second) + adam_epsilon)
    return (weight * (1.0 - rate * decay) - rate * update, moment, square)

def reference(tokens, cotangent, offsets, w_query, moment_query, square_query, w_keyval, moment_keyval, square_keyval, w_out, moment_out, square_out, w_gateup, moment_gateup, square_gateup, w_down, moment_down, square_down, norm_gains, moment_gains, square_gains):
    weights = (w_query, w_keyval, w_out, w_gateup, w_down, norm_gains)
    steps_in = jnp.arange(SPAN, dtype=jnp.int32)
    positions_all = (offsets[:, :, None] + steps_in[None, None, :]).reshape(BATCH, LENGTH).astype(jnp.int32)

    def one_sequence(totals, pieces):
        seq_tokens, seq_cot, seq_pos = pieces

        def forward(inputs, *params):
            return layer(inputs, seq_pos, *params)
        result, pullback = jax.vjp(forward, seq_tokens.astype(jnp.float32), *weights)
        grads = pullback(seq_cot.astype(jnp.float32))
        return (jax.tree.map(jnp.add, totals, tuple(grads[1:])), (result.astype(jnp.bfloat16), grads[0]))
    zeros = tuple((jnp.zeros(weight.shape, jnp.float32) for weight in weights))
    totals, (layer_out, input_grad) = lax.scan(one_sequence, zeros, (tokens, cotangent, positions_all))
    grad_query, grad_keyval, grad_out, grad_gateup, grad_down, grad_gains = totals
    rate_wide = 2.0 * D ** (-0.5)
    rate_out = 2.0 * max(1, 2 * D // LENGTH) ** (-0.5)
    rate_down = 2.0 * FF ** (-0.5)
    new_query, new_moment_query, new_square_query = adamw(w_query, moment_query, square_query, grad_query, rate_wide, decay_rate)
    new_keyval, new_moment_keyval, new_square_keyval = adamw(w_keyval, moment_keyval, square_keyval, grad_keyval, rate_wide, decay_rate)
    new_out, new_moment_out, new_square_out = adamw(w_out, moment_out, square_out, grad_out, rate_out, decay_rate)
    new_gateup, new_moment_gateup, new_square_gateup = adamw(w_gateup, moment_gateup, square_gateup, grad_gateup, rate_wide, decay_rate)
    new_down, new_moment_down, new_square_down = adamw(w_down, moment_down, square_down, grad_down, rate_down, decay_rate)
    new_gains, new_moment_gains, new_square_gains = adamw(norm_gains, moment_gains, square_gains, grad_gains, 1.0, 0.0)
    return (layer_out, input_grad, new_query, new_moment_query, new_square_query, new_keyval, new_moment_keyval, new_square_keyval, new_out, new_moment_out, new_square_out, new_gateup, new_moment_gateup, new_square_gateup, new_down, new_moment_down, new_square_down, new_gains, new_moment_gains, new_square_gains)
```

```python
import functools

import jax
import jax.numpy as jnp
from jax import lax
from jax.experimental import pallas as pl
from jax.experimental.pallas import tpu as pltpu
from jax.sharding import PartitionSpec as P

D = 2048
HEAD_DIM = 64
FF = 5632
LENGTH = 2048
STEP = 10
GROUP = 16
SPAN = 128
TILE = 128

norm_epsilon = 1e-05
rope_base = 10000.0
neg_large = -1e30
beta_first = 0.9
beta_second = 0.95
adam_epsilon = 1e-08
decay_rate = 0.1

bf16 = jnp.bfloat16
f32 = jnp.float32

VMEM_LIMIT = 56 * 1024 * 1024

CORE_SWAP = [(0, 1), (1, 0), (2, 3), (3, 2)]
REPLICA_SWAP = [(0, 2), (1, 3), (2, 0), (3, 1)]
TP_SWAP = [(0, 1), (1, 0)]


def params():
    return pltpu.CompilerParams(vmem_limit_bytes=VMEM_LIMIT)


def dot_nn(left, right):
    return lax.dot_general(left, right, (((1,), (0,)), ((), ())), preferred_element_type=f32)


def dot_nt(left, right):
    return lax.dot_general(left, right, (((1,), (1,)), ((), ())), preferred_element_type=f32)


def dot_tn(left, right):
    return lax.dot_general(left, right, (((0,), (0,)), ((), ())), preferred_element_type=f32)


def adamw(weight, moment, square, grad, rate, decay):
    moment = beta_first * moment + (1.0 - beta_first) * grad
    square = beta_second * square + (1.0 - beta_second) * grad * grad
    fix_first = 1.0 - beta_first**STEP
    fix_second = 1.0 - beta_second**STEP
    update = moment / fix_first / (jnp.sqrt(square / fix_second) + adam_epsilon)
    return (weight * (1.0 - rate * decay) - rate * update, moment, square)


def norm_back(upstream, gain, normed, scale):
    weighted = upstream * gain
    return scale * (weighted - normed * jnp.mean(weighted * normed, axis=-1, keepdims=True))


def partner(values):
    lane = lax.broadcasted_iota(jnp.int32, values.shape, 1)
    up = pltpu.roll(values, 96, 1)
    down = pltpu.roll(values, 32, 1)
    return jnp.where(lane % HEAD_DIM < HEAD_DIM // 2, up, down)


def row_of(block):
    return jnp.concatenate([block[i : i + 1, :] for i in range(GROUP)], axis=1)


def project_kernel(x_ref, wq_ref, wkv_ref, gain_ref, cos_ref, sin_ref, h_ref, q_ref, kv_ref):
    x = x_ref[...].astype(f32)
    scale = lax.rsqrt(jnp.mean(x * x, axis=-1, keepdims=True) + norm_epsilon)
    gain = row_of(gain_ref[:, 0, :].astype(f32))
    h = (x * scale * gain).astype(bf16)
    h_ref[...] = h
    cos = cos_ref[...]
    sin = sin_ref[...]
    lane = lax.broadcasted_iota(jnp.int32, (SPAN, 128), 1)
    low_half = lane < HEAD_DIM
    query = dot_nn(h, wq_ref[...].reshape(D, 512))
    for pair in range(4):
        block = query[:, pair * 128 : (pair + 1) * 128]
        turned = (block * cos + partner(block) * sin) * (HEAD_DIM**-0.5)
        q_ref[2 * pair] = jnp.where(low_half, turned, 0.0).astype(bf16)
        q_ref[2 * pair + 1] = jnp.where(
            low_half, pltpu.roll(turned, HEAD_DIM, 1), 0.0
        ).astype(bf16)
    keyval = dot_nn(h, wkv_ref[...].reshape(D, 128))
    turned = keyval * cos + partner(keyval) * sin
    kv_ref[...] = jnp.where(low_half, turned, keyval).astype(bf16)


def project(x, attn_full, cos, sin):
    rows = x.shape[0]
    row = lambda i: (i, 0)
    return pl.pallas_call(
        project_kernel,
        grid=(rows // SPAN,),
        in_specs=[
            pl.BlockSpec((SPAN, D), row),
            pl.BlockSpec((GROUP, 128, 512), lambda i: (0, 0, 0)),
            pl.BlockSpec((GROUP, 128, 128), lambda i: (0, 0, 8)),
            pl.BlockSpec((GROUP, 16, 128), lambda i: (0, 8, 0)),
            pl.BlockSpec((SPAN, 128), row),
            pl.BlockSpec((SPAN, 128), row),
        ],
        out_specs=[
            pl.BlockSpec((SPAN, D), row),
            pl.BlockSpec((8, SPAN, 128), lambda i: (0, i, 0)),
            pl.BlockSpec((SPAN, 128), row),
        ],
        out_shape=[
            jax.ShapeDtypeStruct((rows, D), bf16),
            jax.ShapeDtypeStruct((8, rows, 128), bf16),
            jax.ShapeDtypeStruct((rows, 128), bf16),
        ],
        compiler_params=params(),
        name="project",
    )(x, attn_full, attn_full, attn_full, cos, sin)


CHUNK = 512


def causal_offsets():
    key = lax.broadcasted_iota(jnp.int32, (128, 256), 0)
    query = lax.broadcasted_iota(jnp.int32, (128, 256), 1) % SPAN
    return key - query


def attend_kernel(off_ref, place_ref, q_ref, kv_ref, wo_ref, o_ref, lse_ref, part_ref, kvt, score):
    seq = pl.program_id(0)
    kv = kv_ref[...].reshape(LENGTH, 128)
    kvt[...] = kv.T
    own = off_ref[seq, place_ref[0]]
    differ = causal_offsets()

    def pair_step(pair, carry):
        q = q_ref[pl.ds(2 * pair, 2)].reshape(256, 128)
        top = jnp.full((1, 256), neg_large, f32)
        for c in range(LENGTH // CHUNK):
            raw = dot_nt(kv_ref[4 * c : 4 * c + 4].reshape(CHUNK, 128), q)
            for j in range(CHUNK // 128):
                block = raw[j * 128 : (j + 1) * 128]
                block = jnp.where(differ <= own - off_ref[seq, 4 * c + j], block, neg_large)
                score[c * CHUNK + j * 128 : c * CHUNK + (j + 1) * 128, :] = block
                top = jnp.maximum(top, jnp.max(block, axis=0, keepdims=True))
        total = jnp.zeros((1, 256), f32)
        mixed = jnp.zeros((128, 256), f32)
        for c in range(LENGTH // CHUNK):
            weight = jnp.exp(score[c * CHUNK : (c + 1) * CHUNK, :] - top)
            total = total + jnp.sum(weight, axis=0, keepdims=True)
            mixed = mixed + dot_nn(kvt[:, c * CHUNK : (c + 1) * CHUNK], weight.astype(bf16))
        out = (mixed[HEAD_DIM:, :] / total).T
        o_ref[pair] = jnp.concatenate([out[:SPAN], out[SPAN:]], axis=1).astype(bf16)
        lse = top + jnp.log(total)
        lse_ref[0, pl.ds(pair, 1), :] = lse
        return carry

    lax.fori_loop(0, 4, pair_step, 0)
    heads = jnp.concatenate([o_ref[i] for i in range(4)], axis=1)
    part_ref[...] = dot_nt(heads, wo_ref[...].reshape(D, 512)).astype(bf16)


def attend(offsets, place, q, kv_all, attn_full):
    rows = q.shape[1]
    seqs = rows // SPAN
    grid_spec = pltpu.PrefetchScalarGridSpec(
        num_scalar_prefetch=2,
        grid=(seqs,),
        in_specs=[
            pl.BlockSpec((8, SPAN, 128), lambda i, *_: (0, i, 0)),
            pl.BlockSpec((GROUP, SPAN, 128), lambda i, *_: (0, i, 0)),
            pl.BlockSpec((GROUP, 128, 512), lambda i, *_: (0, 0, 1)),
        ],
        out_specs=[
            pl.BlockSpec((4, SPAN, 128), lambda i, *_: (0, i, 0)),
            pl.BlockSpec((1, 4, 256), lambda i, *_: (i, 0, 0)),
            pl.BlockSpec((SPAN, D), lambda i, *_: (i, 0)),
        ],
        scratch_shapes=[pltpu.VMEM((128, LENGTH), bf16), pltpu.VMEM((LENGTH, 256), f32)],
    )
    return pl.pallas_call(
        attend_kernel,
        grid_spec=grid_spec,
        out_shape=[
            jax.ShapeDtypeStruct((4, rows, 128), bf16),
            jax.ShapeDtypeStruct((seqs, 4, 256), f32),
            jax.ShapeDtypeStruct((rows, D), bf16),
        ],
        compiler_params=params(),
        name="attend",
    )(offsets, place, q, kv_all, attn_full)


def mlp_kernel(h_ref, dy_ref, w_ref, side_ref, out_ref, back_ref, out_sum, back_sum):
    step = pl.program_id(0)

    @pl.when(step == 0)
    def _():
        out_sum[...] = jnp.zeros_like(out_sum)
        back_sum[...] = jnp.zeros_like(back_sum)

    w_gu = w_ref[:, : 2 * TILE]
    w_d = w_ref[:, 2 * TILE :]
    both = dot_nn(h_ref[...], w_gu)
    upstream = dot_nn(dy_ref[...], w_d)
    gate = both[:, :TILE]
    up = both[:, TILE:]
    sigmoid = jax.nn.sigmoid(gate)
    active = gate * sigmoid
    hidden = (active * up).astype(bf16)
    d_gate = (upstream * up * (sigmoid * (1.0 + gate * (1.0 - sigmoid)))).astype(bf16)
    d_up = (upstream * active).astype(bf16)
    d_both = jnp.concatenate([d_gate, d_up], axis=1)
    side_ref[:, : 2 * TILE] = d_both
    side_ref[:, 2 * TILE :] = hidden
    out_sum[...] += dot_nt(hidden, w_d)
    back_sum[...] += dot_nt(d_both, w_gu)

    @pl.when(step == pl.num_programs(0) - 1)
    def _():
        out_ref[...] = out_sum[...].astype(bf16)
        back_ref[...] = back_sum[...].astype(bf16)


def mlp(h, dy, w_full):
    rows = h.shape[0]
    width = 3 * TILE
    steps = w_full.shape[1] // width
    whole = pl.BlockSpec((rows, D), lambda i: (0, 0))
    return pl.pallas_call(
        mlp_kernel,
        grid=(steps,),
        in_specs=[whole, whole, pl.BlockSpec((D, width), lambda i: (0, i))],
        out_specs=[pl.BlockSpec((rows, width), lambda i: (0, i)), whole, whole],
        out_shape=[
            jax.ShapeDtypeStruct((rows, steps * width), bf16),
            jax.ShapeDtypeStruct((rows, D), bf16),
            jax.ShapeDtypeStruct((rows, D), bf16),
        ],
        scratch_shapes=[pltpu.VMEM((rows, D), f32), pltpu.VMEM((rows, D), f32)],
        compiler_params=params(),
        name="mlp",
    )(h, dy, w_full)


def mlp_grads_kernel(h_ref, dy_ref, side_ref, out_ref):
    out_ref[:, : 2 * TILE] = dot_nn(h_ref[...], side_ref[:, : 2 * TILE]).astype(bf16)
    out_ref[:, 2 * TILE :] = dot_nn(dy_ref[...], side_ref[:, 2 * TILE :]).astype(bf16)


def mlp_grads(h_t, dy_t, side):
    rows = side.shape[0]
    width = 3 * TILE
    steps = side.shape[1] // width
    whole = pl.BlockSpec((D, rows), lambda i: (0, 0))
    return pl.pallas_call(
        mlp_grads_kernel,
        grid=(steps,),
        in_specs=[whole, whole, pl.BlockSpec((rows, width), lambda i: (0, i))],
        out_specs=pl.BlockSpec((D, width), lambda i: (0, i)),
        out_shape=jax.ShapeDtypeStruct((D, steps * width), bf16),
        compiler_params=params(),
        name="mlp_grads",
    )(h_t, dy_t, side)


def attend_back_kernel(
    off_ref, place_ref, da_ref, wo_ref, q_ref, kv_ref, o_ref, lse_ref, cos_ref, sin_ref,
    dq_ref, dkv_ref, kvt, d_heads, dkv,
):
    seq = pl.program_id(0)
    kvt[...] = kv_ref[...].reshape(LENGTH, 128).T
    dkv[...] = jnp.zeros_like(dkv)
    d_all = dot_nn(da_ref[...], wo_ref[...].reshape(D, 512))
    for pair in range(4):
        d_heads[pair] = d_all[:, pair * 128 : (pair + 1) * 128].astype(bf16).astype(f32)
    own = off_ref[seq, place_ref[0]]
    differ = causal_offsets()
    lane = lax.broadcasted_iota(jnp.int32, (SPAN, 128), 1)
    high_half = lane >= HEAD_DIM
    cos = cos_ref[...]
    sin = sin_ref[...]

    def pair_step(pair, carry):
        q = q_ref[pl.ds(2 * pair, 2)].reshape(256, 128)
        d_out = d_heads[pair]
        first = jnp.where(high_half, pltpu.roll(d_out, HEAD_DIM, 1), 0.0).astype(bf16)
        second = jnp.where(high_half, d_out, 0.0).astype(bf16)
        d_o = jnp.concatenate([first, second], axis=0)
        dots = (d_out * o_ref[pair].astype(f32)).T
        inner = jnp.concatenate(
            [
                jnp.sum(dots[:HEAD_DIM], axis=0, keepdims=True),
                jnp.sum(dots[HEAD_DIM:], axis=0, keepdims=True),
            ],
            axis=1,
        )
        lse = lse_ref[0, pl.ds(pair, 1), :]
        d_query = jnp.zeros((128, 256), f32)
        for c in range(LENGTH // CHUNK):
            kv = kv_ref[4 * c : 4 * c + 4].reshape(CHUNK, 128)
            raw = dot_nt(kv, q)
            parts = []
            for j in range(CHUNK // 128):
                block = raw[j * 128 : (j + 1) * 128]
                parts.append(
                    jnp.where(differ <= own - off_ref[seq, 4 * c + j], block, neg_large)
                )
            prob = jnp.exp(jnp.concatenate(parts, axis=0) - lse)
            d_prob = dot_nt(kv, d_o)
            d_score = (prob * (d_prob - inner)).astype(bf16)
            span = slice(c * CHUNK, (c + 1) * CHUNK)
            dkv[span, :] += dot_nn(d_score, q) + dot_nn(prob.astype(bf16), d_o)
            d_query = d_query + dot_nn(kvt[:, span], d_score)
        turned = d_query[:HEAD_DIM, :].T
        block = jnp.concatenate([turned[:SPAN], turned[SPAN:]], axis=1)
        block = (block * cos - partner(block) * sin) * (HEAD_DIM**-0.5)
        dq_ref[pair] = block.astype(bf16)
        return carry

    lax.fori_loop(0, 4, pair_step, 0)
    dkv_ref[...] = dkv[...].astype(bf16).reshape(GROUP, SPAN, 128)


def attend_back(offsets, place, da, attn_full, q, kv_all, o, lse, cos, sin):
    rows = da.shape[0]
    seqs = rows // SPAN
    grid_spec = pltpu.PrefetchScalarGridSpec(
        num_scalar_prefetch=2,
        grid=(seqs,),
        in_specs=[
            pl.BlockSpec((SPAN, D), lambda i, *_: (i, 0)),
            pl.BlockSpec((GROUP, 128, 512), lambda i, *_: (0, 0, 1)),
            pl.BlockSpec((8, SPAN, 128), lambda i, *_: (0, i, 0)),
            pl.BlockSpec((GROUP, SPAN, 128), lambda i, *_: (0, i, 0)),
            pl.BlockSpec((4, SPAN, 128), lambda i, *_: (0, i, 0)),
            pl.BlockSpec((1, 4, 256), lambda i, *_: (i, 0, 0)),
            pl.BlockSpec((SPAN, 128), lambda i, *_: (i, 0)),
            pl.BlockSpec((SPAN, 128), lambda i, *_: (i, 0)),
        ],
        out_specs=[
            pl.BlockSpec((4, SPAN, 128), lambda i, *_: (0, i, 0)),
            pl.BlockSpec((GROUP, SPAN, 128), lambda i, *_: (0, i, 0)),
        ],
        scratch_shapes=[
            pltpu.VMEM((128, LENGTH), bf16),
            pltpu.VMEM((4, SPAN, 128), f32),
            pltpu.VMEM((LENGTH, 128), f32),
        ],
    )
    return pl.pallas_call(
        attend_back_kernel,
        grid_spec=grid_spec,
        out_shape=[
            jax.ShapeDtypeStruct((4, rows, 128), bf16),
            jax.ShapeDtypeStruct((GROUP, rows, 128), bf16),
        ],
        compiler_params=params(),
        name="attend_back",
    )(offsets, place, da, attn_full, q, kv_all, o, lse, cos, sin)


def project_back_kernel(
    dq_ref, dkv_ref, wq_ref, wkv_ref, x_ref, cos_ref, sin_ref, dh_ref, right_ref, gain_ref
):
    lane = lax.broadcasted_iota(jnp.int32, (SPAN, 128), 1)
    total = jnp.sum(dkv_ref[...].astype(f32), axis=0)
    turned = total * cos_ref[...] - partner(total) * sin_ref[...]
    d_kv = jnp.where(lane < HEAD_DIM, turned, total).astype(bf16)
    d_q = jnp.concatenate([dq_ref[i] for i in range(4)], axis=1)
    right_ref[:, :512] = d_q
    right_ref[:, 512:] = d_kv
    d_h = dot_nt(d_q, wq_ref[...].reshape(D, 512)) + dot_nt(d_kv, wkv_ref[...].reshape(D, 128))
    dh_ref[...] = d_h.astype(bf16)
    x = x_ref[...].astype(f32)
    scale = lax.rsqrt(jnp.mean(x * x, axis=-1, keepdims=True) + norm_epsilon)
    terms = (d_h * (x * scale)).reshape(SPAN // 8, 8, D).sum(axis=0)

    @pl.when(pl.program_id(0) == 0)
    def _():
        gain_ref[...] = jnp.zeros_like(gain_ref)

    gain_ref[...] += terms


def project_back(dq, dkv, attn_full, x, cos, sin):
    rows = x.shape[0]
    row = lambda i: (i, 0)
    return pl.pallas_call(
        project_back_kernel,
        grid=(rows // SPAN,),
        in_specs=[
            pl.BlockSpec((4, SPAN, 128), lambda i: (0, i, 0)),
            pl.BlockSpec((GROUP, SPAN, 128), lambda i: (0, i, 0)),
            pl.BlockSpec((GROUP, 128, 512), lambda i: (0, 0, 0)),
            pl.BlockSpec((GROUP, 128, 128), lambda i: (0, 0, 8)),
            pl.BlockSpec((SPAN, D), row),
            pl.BlockSpec((SPAN, 128), row),
            pl.BlockSpec((SPAN, 128), row),
        ],
        out_specs=[
            pl.BlockSpec((SPAN, D), row),
            pl.BlockSpec((SPAN, 640), row),
            pl.BlockSpec((8, D), lambda i: (0, 0)),
        ],
        out_shape=[
            jax.ShapeDtypeStruct((rows, D), bf16),
            jax.ShapeDtypeStruct((rows, 640), bf16),
            jax.ShapeDtypeStruct((8, D), f32),
        ],
        compiler_params=params(),
        name="project_back",
    )(dq, dkv, attn_full, attn_full, x, cos, sin)


def attn_grads_kernel(h_ref, right_ref, da_ref, o_ref, gain_ref, out_ref):
    first = dot_tn(h_ref[...], right_ref[...]).astype(bf16)
    heads = jnp.concatenate([o_ref[i] for i in range(4)], axis=1)
    out_ref[0, :128, :512] = first[:, :512]
    out_ref[0, :128, 512:1024] = dot_tn(da_ref[...], heads).astype(bf16)
    out_ref[0, :128, 1024:] = first[:, 512:]
    out_ref[0, 128:, :] = jnp.zeros((16, 1152), bf16)
    out_ref[0, 128:, :128] = gain_ref[...].astype(bf16)


def attn_grads(h, right, da, o, gains):
    rows = h.shape[0]
    column = lambda g: (0, g)
    return pl.pallas_call(
        attn_grads_kernel,
        grid=(GROUP,),
        in_specs=[
            pl.BlockSpec((rows, 128), column),
            pl.BlockSpec((rows, 640), lambda g: (0, 0)),
            pl.BlockSpec((rows, 128), column),
            pl.BlockSpec((4, rows, 128), lambda g: (0, 0, 0)),
            pl.BlockSpec((16, 128), column),
        ],
        out_specs=pl.BlockSpec((1, 144, 1152), lambda g: (g, 0, 0)),
        out_shape=jax.ShapeDtypeStruct((GROUP, 144, 1152), bf16),
        compiler_params=params(),
        name="attn_grads",
    )(h, right, da, o, gains)


def pack_kernel(core_ref, gu_ref, d_ref, out_ref):
    out_ref[:, :TILE] = gu_ref[:, 0, :].astype(bf16)
    out_ref[:, TILE : 2 * TILE] = gu_ref[:, 1, :].astype(bf16)
    out_ref[:, 2 * TILE :] = d_ref[...].astype(bf16)


def pack_mlp(core, w_gateup, w_down):
    rows, units = w_down.shape
    tiles = units // 2 // TILE
    grid_spec = pltpu.PrefetchScalarGridSpec(
        num_scalar_prefetch=1,
        grid=(tiles,),
        in_specs=[
            pl.BlockSpec((rows, 2, TILE), lambda i, core: (0, 0, core[0] * tiles + i)),
            pl.BlockSpec((rows, TILE), lambda i, core: (0, core[0] * tiles + i)),
        ],
        out_specs=pl.BlockSpec((rows, 3 * TILE), lambda i, core: (0, i)),
    )
    return pl.pallas_call(
        pack_kernel,
        grid_spec=grid_spec,
        out_shape=jax.ShapeDtypeStruct((rows, tiles * 3 * TILE), bf16),
        compiler_params=params(),
        name="pack_mlp",
    )(core, w_gateup, w_down)


def mlp_adam_kernel(
    core_ref, own_ref, other_ref, wg, mg, sg, wd, md, sd, wg_o, mg_o, sg_o, wd_o, md_o, sd_o,
    *, tiles, rate_wide, rate_down,
):
    mine = pl.program_id(0) // tiles == core_ref[0]
    grad = jnp.where(mine, own_ref[...].astype(f32), other_ref[...].astype(f32))
    for i in range(2):
        new = adamw(
            wg[:, i, :], mg[:, i, :], sg[:, i, :], grad[:, i * TILE : (i + 1) * TILE],
            rate_wide, decay_rate,
        )
        wg_o[:, i, :], mg_o[:, i, :], sg_o[:, i, :] = new
    new = adamw(wd[...], md[...], sd[...], grad[:, 2 * TILE :], rate_down, decay_rate)
    wd_o[...], md_o[...], sd_o[...] = new


def mlp_adam(core, own, other, gateup, down, rate_wide, rate_down):
    rows, units = down[0].shape
    tiles = units // 2 // TILE
    wide = pl.BlockSpec((rows, 2, TILE), lambda i, core: (0, 0, i))
    flat = pl.BlockSpec((rows, TILE), lambda i, core: (0, i))
    grad = pl.BlockSpec((rows, 3 * TILE), lambda i, core: (0, i % tiles))
    grid_spec = pltpu.PrefetchScalarGridSpec(
        num_scalar_prefetch=1,
        grid=(2 * tiles,),
        in_specs=[grad, grad] + [wide] * 3 + [flat] * 3,
        out_specs=[wide] * 3 + [flat] * 3,
    )
    shapes = [jax.ShapeDtypeStruct(gateup[0].shape, f32)] * 3
    shapes += [jax.ShapeDtypeStruct(down[0].shape, f32)] * 3
    return pl.pallas_call(
        functools.partial(
            mlp_adam_kernel, tiles=tiles, rate_wide=rate_wide, rate_down=rate_down
        ),
        grid_spec=grid_spec,
        out_shape=shapes,
        compiler_params=params(),
        name="mlp_adam",
    )(core, own, other, *gateup, *down)


def swap_core(values):
    return lax.ppermute(values, "rep", CORE_SWAP)


def swap_replica(values):
    return lax.ppermute(values, "rep", REPLICA_SWAP)


def swap_tp(values):
    return lax.ppermute(values, "tp", TP_SWAP)


def sum_shares(part, own_rows):
    from_core = swap_core(part[own_rows:])
    share = (part[:own_rows].astype(f32) + from_core.astype(f32)).astype(bf16)
    return share.astype(f32) + swap_tp(share).astype(f32)


def on_device(
    tokens,
    cotangent,
    offsets,
    w_query,
    moment_query,
    square_query,
    w_keyval,
    moment_keyval,
    square_keyval,
    w_out,
    moment_out,
    square_out,
    w_gateup,
    moment_gateup,
    square_gateup,
    w_down,
    moment_down,
    square_down,
    norm_gains,
    moment_gains,
    square_gains,
):
    sequences, own_len, width = tokens.shape
    own_rows = sequences * own_len
    core = lax.axis_index("rep") % 2
    core_list = core.reshape(1).astype(jnp.int32)
    place = lax.axis_index("grp").reshape(1).astype(jnp.int32)
    first_core = core == 0

    def half(values):
        size = values.shape[-1] // 2
        return jnp.where(first_core, values[..., :size], values[..., size:])

    def whole(own, other):
        return jnp.concatenate(
            [jnp.where(first_core, own, other), jnp.where(first_core, other, own)], axis=-1
        )

    keyval_half = half(w_keyval)
    attn_pack = jnp.concatenate(
        [half(w_query), half(w_out), keyval_half[:, 0], keyval_half[:, 1]], axis=1
    ).astype(bf16)
    gain_rows = jnp.pad(norm_gains.astype(bf16).T, ((0, 14), (0, 1024)))
    attn_pack = jnp.concatenate([attn_pack, gain_rows], axis=0)
    attn_full = lax.all_gather(attn_pack, "grp", axis=0, tiled=False)
    mlp_full = lax.all_gather(pack_mlp(core_list, w_gateup, w_down), "grp", axis=0, tiled=True)

    x_own = tokens.reshape(own_rows, width)
    dy_own = cotangent.reshape(own_rows, width)
    x_all = jnp.concatenate([x_own, swap_core(x_own)], axis=0)
    dy_all = jnp.concatenate([dy_own, swap_core(dy_own)], axis=0)
    offsets_all = jnp.concatenate([offsets, swap_core(offsets)], axis=0)
    steps_in = jnp.arange(own_len, dtype=jnp.int32)
    starts = lax.dynamic_slice_in_dim(offsets_all, place[0], 1, 1)
    positions = (starts + steps_in[None, :]).reshape(2 * own_rows)
    half_dim = HEAD_DIM // 2
    inverse = rope_base ** (-2.0 * jnp.arange(half_dim, dtype=f32) / HEAD_DIM)
    angles = positions.astype(f32)[:, None] * inverse[None, :]
    cos_part = jnp.cos(angles)
    sin_part = jnp.sin(angles)
    cos = jnp.concatenate([cos_part] * 4, axis=1)
    sin = jnp.concatenate([-sin_part, sin_part] * 2, axis=1)

    h_one, q, kv = project(x_all, attn_full, cos, sin)
    kv_all = lax.all_to_all(
        jnp.broadcast_to(kv[None], (GROUP,) + kv.shape), "grp", 0, 0, tiled=False
    )
    o, lse, attn_part = attend(offsets_all, place, q, kv_all, attn_full)
    gains = attn_full[:, 128:130, :128].astype(f32)
    gain_one = gains[:, 0].reshape(1, width)
    gain_two = gains[:, 1].reshape(1, width)

    x_low = x_own.astype(f32)
    middle = x_low + sum_shares(attn_part, own_rows)
    scale_two = lax.rsqrt(jnp.mean(middle * middle, axis=-1, keepdims=True) + norm_epsilon)
    normed_two = middle * scale_two
    h_two_own = (normed_two * gain_two).astype(bf16)
    h_two = jnp.concatenate([h_two_own, swap_core(h_two_own)], axis=0)
    side, out_part, back_part = mlp(h_two, dy_all, mlp_full)
    mlp_sums = mlp_grads(h_two.T, dy_all.T, side)
    mlp_own = lax.psum_scatter(mlp_sums, "grp", scatter_dimension=0, tiled=True)

    grad_h_two = sum_shares(back_part, own_rows)
    grad_gain_two = jnp.sum(grad_h_two * normed_two, axis=0)
    grad_middle = dy_own.astype(f32) + norm_back(grad_h_two, gain_two, normed_two, scale_two)
    da_own = grad_middle.astype(bf16)
    da = jnp.concatenate([da_own, swap_core(da_own)], axis=0)
    layer_out = (middle + sum_shares(out_part, own_rows)).astype(bf16)

    dq, dkv_part = attend_back(offsets_all, place, da, attn_full, q, kv_all, o, lse, cos, sin)
    dkv = lax.all_to_all(dkv_part, "grp", 0, 0, tiled=False)
    dh_part, right, gain_terms = project_back(dq, dkv, attn_full, x_all, cos, sin)
    grad_gain_one = jnp.sum(gain_terms, axis=0)
    gain_grads = jnp.stack([grad_gain_one, 0.5 * grad_gain_two], axis=0)
    gain_grads = jnp.pad(gain_grads, ((0, 14), (0, 0)))
    attn_sums = lax.all_to_all(attn_grads(h_one, right, da, o, gain_grads), "grp", 0, 0)
    attn_own = jnp.sum(attn_sums.astype(f32), axis=0).astype(bf16)

    grad_h_one = sum_shares(dh_part, own_rows)
    scale_one = lax.rsqrt(jnp.mean(x_low * x_low, axis=-1, keepdims=True) + norm_epsilon)
    input_grad = grad_middle + norm_back(grad_h_one, gain_one, x_low * scale_one, scale_one)

    def over_replicas(values):
        return (values.astype(f32) + swap_replica(values).astype(f32)).astype(bf16)

    mlp_total = over_replicas(mlp_own)
    mlp_other = swap_core(mlp_total)
    attn_total = over_replicas(attn_own)
    attn_other = swap_core(attn_total)
    own = attn_total[:128].astype(f32)
    other = attn_other[:128].astype(f32)
    grad_wq = whole(own[:, :512], other[:, :512])
    grad_wo = whole(own[:, 512:1024], other[:, 512:1024])
    grad_wkv = jnp.stack(
        [
            whole(own[:, 1024:1088], other[:, 1024:1088]),
            whole(own[:, 1088:], other[:, 1088:]),
        ],
        axis=1,
    )
    gain_share = attn_total[128:130, :128].astype(f32) + attn_other[128:130, :128].astype(f32)
    grad_gains = (gain_share + swap_tp(gain_share)).T

    rate_wide = 2.0 * D ** (-0.5)
    rate_out = 2.0 * max(1, 2 * D // LENGTH) ** (-0.5)
    rate_down = 2.0 * FF ** (-0.5)
    new_query = adamw(w_query, moment_query, square_query, grad_wq, rate_wide, decay_rate)
    new_keyval = adamw(w_keyval, moment_keyval, square_keyval, grad_wkv, rate_wide, decay_rate)
    new_out = adamw(w_out, moment_out, square_out, grad_wo, rate_out, decay_rate)
    new_mlp = mlp_adam(
        core_list,
        mlp_total,
        mlp_other,
        (w_gateup, moment_gateup, square_gateup),
        (w_down, moment_down, square_down),
        rate_wide,
        rate_down,
    )
    new_gains = adamw(norm_gains, moment_gains, square_gains, grad_gains, 1.0, 0.0)
    return (
        layer_out.reshape(tokens.shape),
        input_grad.reshape(tokens.shape),
        *new_query,
        *new_keyval,
        *new_out,
        *new_mlp,
        *new_gains,
    )


def solution(mesh):
    rows = P("rep", "grp", None)
    flat = P("grp", "tp")
    deep = P("grp", None, "tp")
    states = (flat,) * 3 + (deep,) * 3 + (flat,) * 3 + (deep,) * 3 + (flat,) * 3
    states += (P("grp", None),) * 3
    return jax.shard_map(
        on_device,
        mesh=mesh,
        in_specs=(rows, rows, P("rep", None)) + states,
        out_specs=(rows, rows) + states,
        check_vma=False,
    )
```

```python
import functools

import jax
import jax.numpy as jnp
from jax import lax
from jax.experimental import pallas as pl
from jax.experimental.layout import Layout, with_layout_constraint
from jax.experimental.pallas import tpu as pltpu
from jax.sharding import PartitionSpec as P

D = 2048
HEAD_DIM = 64
FF = 5632
LENGTH = 2048
STEP = 10
GROUP = 16
SPAN = 128
TILE = 256

norm_epsilon = 1e-05
rope_base = 10000.0
neg_large = -1e30
beta_first = 0.9
beta_second = 0.95
adam_epsilon = 1e-08
decay_rate = 0.1

bf16 = jnp.bfloat16
f32 = jnp.float32

VMEM_LIMIT = 63 * 1024 * 1024

CORE_SWAP = [(0, 1), (1, 0), (2, 3), (3, 2)]
REPLICA_SWAP = [(0, 2), (1, 3), (2, 0), (3, 1)]
TP_SWAP = [(0, 1), (1, 0)]
CORE_TP_SWAP = [(2 * r + t, 2 * (r ^ 1) + (1 - t)) for r in range(4) for t in range(2)]
BOTH_SWAP = [(2 * r + t, 2 * (r ^ 2) + (1 - t)) for r in range(4) for t in range(2)]


def struct(shape, dtype):
    return jax.ShapeDtypeStruct(shape, dtype)


def kernel_call(
    kernel, *, name, out_shape, grid=(), in_specs=None, out_specs=None, scratch_shapes=(), prefetch=0,
    after=(),
):
    first = prefetch + len(in_specs)

    def body(*refs):
        kernel(*refs[:first], *refs[first + len(after) :])

    grid_spec = pltpu.PrefetchScalarGridSpec(
        num_scalar_prefetch=prefetch,
        grid=grid,
        in_specs=list(in_specs) + [pl.BlockSpec(memory_space=pl.ANY)] * len(after),
        out_specs=out_specs,
        scratch_shapes=list(scratch_shapes),
    )
    call = pl.pallas_call(
        body,
        grid_spec=grid_spec,
        out_shape=out_shape,
        compiler_params=pltpu.CompilerParams(vmem_limit_bytes=VMEM_LIMIT),
        name=name,
    )
    return lambda *args: call(*args, *after)


def dot_nn(left, right):
    return lax.dot_general(left, right, (((1,), (0,)), ((), ())), preferred_element_type=f32)


def dot_nt(left, right):
    return lax.dot_general(left, right, (((1,), (1,)), ((), ())), preferred_element_type=f32)


def dot_tn(left, right):
    return lax.dot_general(left, right, (((0,), (0,)), ((), ())), preferred_element_type=f32)


def adamw(weight, moment, square, grad, rate, decay):
    moment = beta_first * moment + (1.0 - beta_first) * grad
    square = beta_second * square + (1.0 - beta_second) * grad * grad
    fix_first = 1.0 - beta_first**STEP
    fix_second = 1.0 - beta_second**STEP
    update = moment / fix_first / (jnp.sqrt(square / fix_second) + adam_epsilon)
    return (weight * (1.0 - rate * decay) - rate * update, moment, square)


def norm_back(upstream, gain, normed, scale):
    weighted = upstream * gain
    return scale * (weighted - normed * jnp.mean(weighted * normed, axis=-1, keepdims=True))


def partner(values):
    lane = lax.broadcasted_iota(jnp.int32, values.shape, 1)
    up = pltpu.roll(values, 96, 1)
    down = pltpu.roll(values, 32, 1)
    return jnp.where(lane % HEAD_DIM < HEAD_DIM // 2, up, down)


def row_of(block):
    return jnp.concatenate([block[i : i + 1, :] for i in range(GROUP)], axis=1)


def rms_scale(values):
    return lax.rsqrt(jnp.mean(values * values, axis=-1, keepdims=True) + norm_epsilon)


def gain_row(gain_ref, index):
    return row_of(gain_ref[:, index, :].astype(f32))


GAIN_SPEC = pl.BlockSpec((GROUP, 16, 128), lambda *_: (0, 8, 0))
WQ_SPEC = pl.BlockSpec((D, 512), lambda *_: (0, 0))
WO_SPEC = pl.BlockSpec((D, 512), lambda *_: (0, 1))
WKV_SPEC = pl.BlockSpec((GROUP, 128, 128), lambda *_: (0, 0, 0))
ROWS_SPEC = pl.BlockSpec((SPAN, D), lambda *_: (0, 0))


def half_of(place, k):
    return place[1] if k == 0 else 1 - place[1]


def seq_spec(k):
    return pl.BlockSpec((1, SPAN, D), lambda *ids: (half_of(ids[-1], k), 0, 0))


def turn_spec(k):
    return pl.BlockSpec((SPAN, 128), lambda i, *refs: (2 * half_of(refs[-1], k) + i, 0))


def whole_spec(shape):
    return pl.BlockSpec(shape, lambda *_: (0,) * len(shape))


def pack_attn_kernel(core_ref, wq_ref, wo_ref, wkv_ref, gain_ref, wide_ref, kv_ref, copies_ref):
    lane = lax.broadcasted_iota(jnp.int32, (128, 128), 1)
    low_half = lane < HEAD_DIM
    first_core = core_ref[0] == 0
    key = jnp.where(first_core, wkv_ref[:, 0, :], pltpu.roll(wkv_ref[:, 0, :], HEAD_DIM, 1))
    value = jnp.where(first_core, pltpu.roll(wkv_ref[:, 1, :], HEAD_DIM, 1), wkv_ref[:, 1, :])
    kv = jnp.where(low_half, key, value).astype(bf16)
    wide_ref[:, :512] = wq_ref[...].astype(bf16)
    wide_ref[:, 512:] = wo_ref[...].astype(bf16)
    kv_ref[...] = kv
    gains = jnp.concatenate([gain_ref[...], jnp.zeros((14, 128), f32)], axis=0).astype(bf16)
    for g in range(GROUP):
        copies_ref[g, :128, :] = kv
        copies_ref[g, 128:, :] = gains


def pack_attn(core, w_query, w_out, w_keyval, gains):
    rows = w_query.shape[0]
    half = pl.BlockSpec((rows, 512), lambda i, core: (0, core[0]))
    shapes = [(rows, 1024), (rows, 128), (GROUP, rows + 16, 128)]
    return kernel_call(
        pack_attn_kernel,
        prefetch=1,
        grid=(1,),
        in_specs=[half, half, whole_spec(w_keyval.shape), whole_spec(gains.shape)],
        out_specs=[whole_spec(shape) for shape in shapes],
        out_shape=[struct(shape, bf16) for shape in shapes],
        name="pack_attn",
    )(core, w_query, w_out, w_keyval, gains)


def project_kv_kernel(
    place_ref, own_ref, other_ref, wkv_ref, gain_ref, cos_ref, sin_ref, h_ref, turned_ref, kv_ref
):
    mine = pl.program_id(0) == 0
    x = jnp.where(mine, own_ref[0].astype(f32), other_ref[0].astype(f32))
    h = (x * rms_scale(x) * gain_row(gain_ref, 0)).astype(bf16)
    h_ref[...] = h
    low_half = lax.broadcasted_iota(jnp.int32, (SPAN, 128), 1) < HEAD_DIM
    keyval = dot_nn(h, wkv_ref[...].reshape(D, 128))
    turned = keyval * cos_ref[...] + partner(keyval) * sin_ref[...]
    kv = jnp.where(low_half, turned, keyval).astype(bf16)
    kv_ref[...] = jnp.broadcast_to(kv[None], (GROUP, SPAN, 128))
    turned_ref[...] = h.T


def project_kv(k, place, x_own, x_other, kv_full, cos, sin, after=()):
    return kernel_call(
        project_kv_kernel,
        prefetch=1,
        grid=(2,),
        in_specs=[seq_spec(k), seq_spec(k), WKV_SPEC, GAIN_SPEC, turn_spec(k), turn_spec(k)],
        out_specs=[
            pl.BlockSpec((SPAN, D), lambda i, *_: (i, 0)),
            pl.BlockSpec((D, SPAN), lambda i, *_: (0, i)),
            pl.BlockSpec((GROUP, SPAN, 128), lambda i, *_: (0, i, 0)),
        ],
        out_shape=[
            struct((2 * SPAN, D), bf16),
            struct((D, 2 * SPAN), bf16),
            struct((GROUP, 2 * SPAN, 128), bf16),
        ],
        after=after,
        name="project_kv",
    )(place, x_own, x_other, kv_full, kv_full, cos, sin)


def project_q_kernel(place_ref, h_ref, wq_ref, cos_ref, sin_ref, q_ref):
    cos = cos_ref[...]
    sin = sin_ref[...]
    low_half = lax.broadcasted_iota(jnp.int32, (SPAN, 128), 1) < HEAD_DIM
    query = dot_nn(h_ref[...], wq_ref[...])
    for pair in range(4):
        block = query[:, pair * 128 : (pair + 1) * 128]
        turned = (block * cos + partner(block) * sin) * (HEAD_DIM**-0.5)
        q_ref[2 * pair] = jnp.where(low_half, turned, 0.0).astype(bf16)
        q_ref[2 * pair + 1] = jnp.where(
            low_half, pltpu.roll(turned, HEAD_DIM, 1), 0.0
        ).astype(bf16)


def project_q(k, place, h, wide_full, cos, sin, after=()):
    return kernel_call(
        project_q_kernel,
        prefetch=1,
        grid=(2,),
        in_specs=[pl.BlockSpec((SPAN, D), lambda i, *_: (i, 0)), WQ_SPEC, turn_spec(k), turn_spec(k)],
        out_specs=pl.BlockSpec((8, SPAN, 128), lambda i, *_: (0, i, 0)),
        out_shape=struct((8, 2 * SPAN, 128), bf16),
        after=after,
        name="project_q",
    )(place, h, wide_full, cos, sin)


CHUNK = 512
BACK_CHUNK = 1024


def causal_offsets():
    key = lax.broadcasted_iota(jnp.int32, (128, 256), 0)
    query = lax.broadcasted_iota(jnp.int32, (128, 256), 1) % SPAN
    return key - query


def masked(raw, differ, own, off_ref, seq, c):
    parts = []
    blocks = raw.shape[0] // 128
    for j in range(blocks):
        allowed = differ <= own - off_ref[seq, blocks * c + j]
        parts.append(jnp.where(allowed, raw[j * 128 : (j + 1) * 128], neg_large))
    return jnp.concatenate(parts, axis=0)


def attend_kernel(
    off_ref, place_ref, q_ref, kv_ref, wo_ref, o_ref, lse_ref, own_ref, other_ref, kvt, scores, *, k
):
    step = pl.program_id(0)
    seq = 2 * half_of(place_ref, k) + step
    kvt[...] = kv_ref[...].reshape(LENGTH, 128).T
    own = off_ref[seq, place_ref[0]]
    differ = causal_offsets()
    blocks = CHUNK // 128

    for pair in range(4):
        q = q_ref[2 * pair : 2 * pair + 2].reshape(256, 128)
        top = jnp.full((1, 256), neg_large, f32)
        for c in range(LENGTH // CHUNK):
            raw = dot_nt(kv_ref[blocks * c : blocks * (c + 1)].reshape(CHUNK, 128), q)
            score = masked(raw, differ, own, off_ref, seq, c)
            scores[pair % 2, c * CHUNK : (c + 1) * CHUNK, :] = score
            top = jnp.maximum(top, jnp.max(score, axis=0, keepdims=True))
        total = jnp.zeros((1, 256), f32)
        mixed = jnp.zeros((128, 256), f32)
        for c in range(LENGTH // CHUNK):
            weight = jnp.exp(scores[pair % 2, c * CHUNK : (c + 1) * CHUNK, :] - top)
            total = total + jnp.sum(weight, axis=0, keepdims=True)
            mixed = mixed + dot_nn(kvt[:, c * CHUNK : (c + 1) * CHUNK], weight.astype(bf16))
        out = (mixed[HEAD_DIM:, :] / total).T
        o_ref[pair] = jnp.concatenate([out[:SPAN], out[SPAN:]], axis=1).astype(bf16)
        lse_ref[0, pair : pair + 1, :] = top + jnp.log(total)

    heads = jnp.concatenate([o_ref[i] for i in range(4)], axis=1)
    part = dot_nt(heads, wo_ref[...]).astype(bf16)

    @pl.when(step == 0)
    def _():
        own_ref[...] = part

    @pl.when(step == 1)
    def _():
        other_ref[...] = part


def attend(k, offsets, place, q, kv_all, wo_full, after=()):
    grid_spec = dict(
        prefetch=2,
        grid=(2,),
        in_specs=[
            pl.BlockSpec((8, SPAN, 128), lambda i, *_: (0, i, 0)),
            pl.BlockSpec((GROUP, SPAN, 128), lambda i, *_: (0, i, 0)),
            WO_SPEC,
        ],
        out_specs=[
            pl.BlockSpec((4, SPAN, 128), lambda i, *_: (0, i, 0)),
            pl.BlockSpec((1, 4, 256), lambda i, *_: (i, 0, 0)),
            ROWS_SPEC,
            ROWS_SPEC,
        ],
        scratch_shapes=[pltpu.VMEM((128, LENGTH), bf16), pltpu.VMEM((2, LENGTH, 256), f32)],
    )
    return kernel_call(
        functools.partial(attend_kernel, k=k),
        **grid_spec,
        out_shape=[
            struct((4, 2 * SPAN, 128), bf16),
            struct((2, 4, 256), f32),
            struct((SPAN, D), bf16),
            struct((SPAN, D), bf16),
        ],
        after=after,
        name="attend",
    )(offsets, place, q, kv_all, wo_full)


def share_kernel(own_ref, other_ref, out_ref):
    out_ref[...] = (own_ref[...].astype(f32) + other_ref[...].astype(f32)).astype(bf16)


def add_low(first, second, after=()):
    rows, width = first.shape
    block = pl.BlockSpec((128, width), lambda i: (i, 0))
    return kernel_call(
        share_kernel,
        grid=(rows // 128,),
        in_specs=[block, block],
        out_specs=block,
        out_shape=struct(first.shape, bf16),
        after=after,
        name="add_low",
    )(first, second)


def middle_kernel(place_ref, x_ref, one_ref, two_ref, gain_ref, mid_ref, h_ref):
    total = one_ref[...].astype(f32) + two_ref[...].astype(f32)
    mid = x_ref[0].astype(f32) + total
    mid_ref[...] = mid
    h_ref[...] = (mid * rms_scale(mid) * gain_row(gain_ref, 1)).astype(bf16)


def middle(place, x_own, one, two, attn_full):
    return kernel_call(
        middle_kernel,
        prefetch=1,
        grid=(1,),
        in_specs=[seq_spec(0), ROWS_SPEC, ROWS_SPEC, GAIN_SPEC],
        out_specs=[ROWS_SPEC, ROWS_SPEC],
        out_shape=[struct((SPAN, D), f32), struct((SPAN, D), bf16)],
        name="middle",
    )(place, x_own, one, two, attn_full)


def sum_rows(refs):
    return sum(ref[...].astype(f32) for ref in refs)


def middle_back_kernel(place_ref, p0, p1, p2, p3, mid_ref, dy_ref, gain_ref, da_ref):
    upstream = sum_rows((p0, p1, p2, p3))
    mid = mid_ref[...]
    scale = rms_scale(mid)
    d_norm = norm_back(upstream, gain_row(gain_ref, 1), mid * scale, scale)
    da_ref[...] = (dy_ref[0].astype(f32) + d_norm).astype(bf16)


def middle_back(place, parts, mid, dy_own, attn_full, after=()):
    return kernel_call(
        middle_back_kernel,
        prefetch=1,
        grid=(1,),
        in_specs=[ROWS_SPEC] * 5 + [seq_spec(0), GAIN_SPEC],
        out_specs=ROWS_SPEC,
        out_shape=struct((SPAN, D), bf16),
        after=after,
        name="middle_back",
    )(place, *parts, mid, dy_own, attn_full)


def layer_part_kernel(mid_ref, p0, p1, p2, p3, out_ref):
    out_ref[...] = (mid_ref[...] + sum_rows((p0, p1, p2, p3))).astype(bf16)


def layer_part(mid, parts, after=()):
    return kernel_call(
        layer_part_kernel,
        grid=(1,),
        in_specs=[ROWS_SPEC] * 5,
        out_specs=ROWS_SPEC,
        out_shape=struct((SPAN, D), bf16),
        after=after,
        name="layer_part",
    )(mid, *parts)


def layer_out_kernel(place_ref, mine_ref, other_ref, out_ref):
    out_ref[half_of(place_ref, 0)] = mine_ref[...]
    out_ref[half_of(place_ref, 1)] = other_ref[...]


def layer_out_of(place, mine, other, after=()):
    return kernel_call(
        layer_out_kernel,
        prefetch=1,
        grid=(1,),
        in_specs=[ROWS_SPEC, ROWS_SPEC],
        out_specs=whole_spec((2, SPAN, D)),
        out_shape=struct((2, SPAN, D), bf16),
        after=after,
        name="layer_out",
    )(place, mine, other)


def input_grad_kernel(place_ref, da0, da1, share, received, x_ref, gain_ref, out_ref):
    gain = gain_row(gain_ref, 0)
    for k, da_ref in enumerate((da0, da1)):
        here = slice(k * SPAN, (k + 1) * SPAN)
        there = slice((1 - k) * SPAN, (2 - k) * SPAN)
        upstream = share[here, :].astype(f32) + received[there, :].astype(f32)
        m = half_of(place_ref, k)
        x = x_ref[m].astype(f32)
        scale = rms_scale(x)
        out_ref[m] = da_ref[...].astype(f32) + norm_back(upstream, gain, x * scale, scale)


def input_grad_of(place, das, share, received, x_own, attn_full, after=()):
    both = whole_spec((2 * SPAN, D))
    seqs = whole_spec((2, SPAN, D))
    return kernel_call(
        input_grad_kernel,
        prefetch=1,
        grid=(1,),
        in_specs=[ROWS_SPEC, ROWS_SPEC, both, both, seqs, GAIN_SPEC],
        out_specs=seqs,
        out_shape=struct((2, SPAN, D), f32),
        after=after,
        name="input_grad",
    )(place, *das, share, received, x_own, attn_full)


PACK_ROWS = 16
ALL_ROWS = 8 * SPAN
SMALL = 128
WINDOW_TILES = 6
WIDTH = 3 * WINDOW_TILES * SMALL
WINDOW_STARTS = (0, 6, 11, 16)
FIRST_OWN = (0, 6, 12, 17, 22)


def window_start(quarter):
    return jnp.where(quarter < 2, 6 * quarter, 5 * quarter + 1)


def packed_column(tile, kind):
    return 3 * TILE * (tile // 2) + TILE * kind + SMALL * (tile % 2)


def transpose_kernel(place_ref, *refs):
    parts, out_ref = refs[:-1], refs[-1]
    for k in range(2):
        for i, ref in enumerate(parts):
            start = (len(parts) * k + i) * SPAN
            out_ref[:, start : start + SPAN] = ref[half_of(place_ref, k)].T


def transposed(place, parts, after=()):
    seqs = pl.BlockSpec((2, SPAN, 512), lambda i, *_: (0, 0, i))
    return kernel_call(
        transpose_kernel,
        prefetch=1,
        grid=(D // 512,),
        in_specs=[seqs] * 4,
        out_specs=pl.BlockSpec((512, ALL_ROWS), lambda i, *_: (i, 0)),
        out_shape=struct((D, ALL_ROWS), bf16),
        after=after,
        name="transposed",
    )(place, *parts)


def mlp_kernel(place_ref, *refs):
    h_parts, dy_parts, dyt_ref, w_ref = refs[:8], refs[8:12], refs[12], refs[13]
    side_ref, sum_ref, h, ht, dy, dyt, sems = refs[14:]
    step = pl.program_id(0)

    def part_copies():
        copies = []
        for i, ref in enumerate(h_parts):
            spot = h.at[i * SPAN : (i + 1) * SPAN]
            copies.append(pltpu.make_async_copy(ref, spot, sems.at[i]))
        for k in range(2):
            for i, ref in enumerate(dy_parts):
                number = 4 * k + i
                spot = dy.at[number * SPAN : (number + 1) * SPAN]
                source = ref.at[half_of(place_ref, k)]
                copies.append(pltpu.make_async_copy(source, spot, sems.at[8 + number]))
        return copies

    turned_copy = pltpu.make_async_copy(dyt_ref, dyt, sems.at[16])

    @pl.when(step == 0)
    def _():
        copies = part_copies()
        for copy in copies:
            copy.start()
        turned_copy.start()
        for copy in copies:
            copy.wait()

    for start in range(0, ALL_ROWS, 256):
        rows = slice(start, start + 256)
        both = dot_nn(h[rows, :], w_ref[:, : 2 * TILE])
        upstream = dot_nn(dy[rows, :], w_ref[:, 2 * TILE :])
        gate = both[:, :TILE]
        up = both[:, TILE:]
        sigmoid = jax.nn.sigmoid(gate)
        active = gate * sigmoid
        side_ref[rows, :TILE] = (
            upstream * up * (sigmoid * (1.0 + gate * (1.0 - sigmoid)))
        ).astype(bf16)
        side_ref[rows, TILE : 2 * TILE] = (upstream * active).astype(bf16)
        side_ref[rows, 2 * TILE :] = (active * up).astype(bf16)

    @pl.when(step == 0)
    def _():
        ht[...] = h[...].T
        turned_copy.wait()

    sum_ref[:, : 2 * TILE] = dot_nn(ht[...], side_ref[:, : 2 * TILE]).astype(bf16)
    sum_ref[:, 2 * TILE :] = dot_nn(dyt[...], side_ref[:, 2 * TILE :]).astype(bf16)


def mlp(place, h_parts, dy_parts, dy_t, w_full, after=()):
    width = 3 * TILE
    return kernel_call(
        mlp_kernel,
        prefetch=1,
        grid=(WIDTH // width,),
        in_specs=[pl.BlockSpec(memory_space=pl.ANY)] * 13
        + [pl.BlockSpec((D, width), lambda i, *_: (0, i))],
        out_specs=[
            pl.BlockSpec((ALL_ROWS, width), lambda i, *_: (0, i)),
            pl.BlockSpec((D, width), lambda i, *_: (0, i)),
        ],
        out_shape=[struct((ALL_ROWS, WIDTH), bf16), struct((D, WIDTH), bf16)],
        scratch_shapes=[
            pltpu.VMEM((ALL_ROWS, D), bf16),
            pltpu.VMEM((D, ALL_ROWS), bf16),
            pltpu.VMEM((ALL_ROWS, D), bf16),
            pltpu.VMEM((D, ALL_ROWS), bf16),
            pltpu.SemaphoreType.DMA((17,)),
        ],
        after=after,
        name="mlp",
    )(place, *h_parts, *dy_parts, dy_t, w_full)


def mlp_back_kernel(side_ref, w_ref, *outs, first, count):
    total = jnp.zeros((ALL_ROWS, w_ref.shape[0]), f32)
    for column in range(0, WIDTH, 3 * TILE):
        span = slice(column + first * TILE, column + (first + count) * TILE)
        total = total + dot_nt(side_ref[:, span], w_ref[:, span])
    for out, i in zip(outs, range(8)):
        out[...] = total[i * SPAN : (i + 1) * SPAN].astype(bf16)


def mlp_back(side, w_full, first, count, after=()):
    return kernel_call(
        functools.partial(mlp_back_kernel, first=first, count=count),
        grid=(D // 512,),
        in_specs=[whole_spec((ALL_ROWS, WIDTH)), pl.BlockSpec((512, WIDTH), lambda i: (i, 0))],
        out_specs=[pl.BlockSpec((SPAN, 512), lambda i: (0, i))] * 8,
        out_shape=[struct((SPAN, D), bf16)] * 8,
        after=after,
        name="mlp_back",
    )(side, w_full)


def quad_kernel(*refs):
    for i in range(4):
        total = refs[2 * i][...].astype(f32) + refs[2 * i + 1][...].astype(f32)
        refs[8 + i][...] = total.astype(bf16)


def add_quads(pairs, after=()):
    block = pl.BlockSpec((64, D), lambda i: (i, 0))
    return kernel_call(
        quad_kernel,
        grid=(SPAN // 64,),
        in_specs=[block] * 8,
        out_specs=[block] * 4,
        out_shape=[struct((SPAN, D), bf16)] * 4,
        after=after,
        name="add_quads",
    )(*[value for pair in pairs for value in pair])


def attend_back_kernel(
    off_ref, place_ref, own_ref, other_ref, wo_ref, q_ref, kv_ref, o_ref, lse_ref, cos_ref,
    sin_ref, dq_ref, dkv_ref, kvt, d_heads, dkv, *, k,
):
    step = pl.program_id(0)
    seq = 2 * half_of(place_ref, k) + step
    kvt[...] = kv_ref[...].reshape(LENGTH, 128).T
    dkv[...] = jnp.zeros_like(dkv)
    d_out_rows = jnp.where(step == 0, own_ref[...].astype(f32), other_ref[...].astype(f32))
    d_all = dot_nn(d_out_rows.astype(bf16), wo_ref[...])
    for pair in range(4):
        d_heads[pair] = d_all[:, pair * 128 : (pair + 1) * 128].astype(bf16).astype(f32)
    own = off_ref[seq, place_ref[0]]
    differ = causal_offsets()
    lane = lax.broadcasted_iota(jnp.int32, (SPAN, 128), 1)
    high_half = lane >= HEAD_DIM
    cos = cos_ref[...]
    sin = sin_ref[...]
    blocks = BACK_CHUNK // 128

    for pair in range(4):
        q = q_ref[2 * pair : 2 * pair + 2].reshape(256, 128)
        d_out = d_heads[pair]
        first = jnp.where(high_half, pltpu.roll(d_out, HEAD_DIM, 1), 0.0).astype(bf16)
        second = jnp.where(high_half, d_out, 0.0).astype(bf16)
        d_o = jnp.concatenate([first, second], axis=0)
        dots = (d_out * o_ref[pair].astype(f32)).T
        inner = jnp.concatenate(
            [
                jnp.sum(dots[:HEAD_DIM], axis=0, keepdims=True),
                jnp.sum(dots[HEAD_DIM:], axis=0, keepdims=True),
            ],
            axis=1,
        )
        lse = lse_ref[0, pair : pair + 1, :]
        d_query = jnp.zeros((128, 256), f32)
        for c in range(LENGTH // BACK_CHUNK):
            kv = kv_ref[blocks * c : blocks * (c + 1)].reshape(BACK_CHUNK, 128)
            score = masked(dot_nt(kv, q), differ, own, off_ref, seq, c)
            prob = jnp.exp(score - lse)
            d_prob = dot_nt(kv, d_o)
            d_score = (prob * (d_prob - inner)).astype(bf16)
            span = slice(c * BACK_CHUNK, (c + 1) * BACK_CHUNK)
            dkv[span, :] += dot_nn(d_score, q) + dot_nn(prob.astype(bf16), d_o)
            d_query = d_query + dot_nn(kvt[:, span], d_score)
        turned = d_query[:HEAD_DIM, :].T
        block = jnp.concatenate([turned[:SPAN], turned[SPAN:]], axis=1)
        block = (block * cos - partner(block) * sin) * (HEAD_DIM**-0.5)
        dq_ref[pair] = block.astype(bf16)

    dkv_ref[...] = dkv[...].astype(bf16).reshape(GROUP, SPAN, 128)


def attend_back(k, offsets, place, da_own, da_other, wo_full, q, kv_all, o, lse, cos, sin, after=()):
    turn = turn_spec(k)
    heads = pl.BlockSpec((4, SPAN, 128), lambda i, *_: (0, i, 0))
    group = pl.BlockSpec((GROUP, SPAN, 128), lambda i, *_: (0, i, 0))
    grid_spec = dict(
        prefetch=2,
        grid=(2,),
        in_specs=[
            ROWS_SPEC,
            ROWS_SPEC,
            WO_SPEC,
            pl.BlockSpec((8, SPAN, 128), lambda i, *_: (0, i, 0)),
            group,
            heads,
            pl.BlockSpec((1, 4, 256), lambda i, *_: (i, 0, 0)),
            turn,
            turn,
        ],
        out_specs=[heads, group],
        scratch_shapes=[
            pltpu.VMEM((128, LENGTH), bf16),
            pltpu.VMEM((4, SPAN, 128), f32),
            pltpu.VMEM((LENGTH, 128), f32),
        ],
    )
    return kernel_call(
        functools.partial(attend_back_kernel, k=k),
        **grid_spec,
        out_shape=[
            struct((4, 2 * SPAN, 128), bf16),
            struct((GROUP, 2 * SPAN, 128), bf16),
        ],
        after=after,
        name="attend_back",
    )(offsets, place, da_own, da_other, wo_full, q, kv_all, o, lse, cos, sin)


def out_grads_kernel(a0, a1, a2, a3, o0_ref, o1_ref, out_ref):
    heads = jnp.concatenate(
        [jnp.concatenate([ref[i] for i in range(4)], axis=1) for ref in (o0_ref, o1_ref)],
        axis=0,
    )
    rows = jnp.concatenate([ref[...] for ref in (a0, a1, a2, a3)], axis=0)
    out_ref[...] = dot_tn(rows, heads).astype(bf16)


def out_grads(da_parts, o_parts, after=()):
    return kernel_call(
        out_grads_kernel,
        grid=(4,),
        in_specs=[pl.BlockSpec((SPAN, 512), lambda i: (0, i))] * 4
        + [whole_spec((4, 2 * SPAN, 128))] * 2,
        out_specs=pl.BlockSpec((512, 512), lambda i: (i, 0)),
        out_shape=struct((D, 512), bf16),
        after=after,
        name="out_grads",
    )(*da_parts, *o_parts)


def right_kernel(place_ref, dkv_ref, cos_ref, sin_ref, out_ref):
    lane = lax.broadcasted_iota(jnp.int32, (SPAN, 128), 1)
    total = jnp.sum(dkv_ref[...].astype(f32), axis=0)
    turned = total * cos_ref[...] - partner(total) * sin_ref[...]
    out_ref[...] = jnp.where(lane < HEAD_DIM, turned, total).astype(bf16)


def right_side(k, place, dkv, cos, sin, after=()):
    return kernel_call(
        right_kernel,
        prefetch=1,
        grid=(2,),
        in_specs=[
            pl.BlockSpec((GROUP, SPAN, 128), lambda i, *_: (0, i, 0)),
            turn_spec(k),
            turn_spec(k),
        ],
        out_specs=pl.BlockSpec((SPAN, 128), lambda i, *_: (i, 0)),
        out_shape=struct((2 * SPAN, 128), bf16),
        after=after,
        name="right_side",
    )(place, dkv, cos, sin)


def query_grads_kernel(place_ref, h0_ref, h1_ref, q0_ref, q1_ref, *outs):
    rights = [jnp.concatenate([ref[i] for i in range(4)], axis=1) for ref in (q0_ref, q1_ref)]
    for step in range(4):
        for z in range(4):
            owner = z * 4 + (place_ref[0] + step) % 4
            rows = pl.ds(pl.multiple_of(owner * 128, 128), 128)
            total = dot_nn(h0_ref[rows, :], rights[0]) + dot_nn(h1_ref[rows, :], rights[1])
            outs[step][z] = total.astype(bf16)


def query_grads(place, h_turned, dqs, after=()):
    args = (*h_turned, *dqs)
    shape = (4, 128, 512)
    return kernel_call(
        query_grads_kernel,
        prefetch=1,
        grid=(1,),
        in_specs=[whole_spec(arg.shape) for arg in args],
        out_specs=[whole_spec(shape)] * 4,
        out_shape=[struct(shape, bf16)] * 4,
        after=after,
        name="query_grads",
    )(place, *args)


def line_sum_kernel(place_ref, e0, e1, e2, e3, *outs):
    for step in range(4):
        z = (place_ref[0] // 4 + step) % 4
        outs[step][...] = sum(ref[z].astype(f32) for ref in (e0, e1, e2, e3)).astype(bf16)


def line_sums(place, terms, after=()):
    shape = terms[0].shape[1:]
    return kernel_call(
        line_sum_kernel,
        prefetch=1,
        grid=(1,),
        in_specs=[whole_spec(term.shape) for term in terms],
        out_specs=[whole_spec(shape)] * 4,
        out_shape=[struct(shape, bf16)] * 4,
        after=after,
        name="line_sums",
    )(place, *terms)


def final_sums_kernel(e0, e1, e2, e3, out_ref, kv_ref, sum_ref):
    sum_ref[:, :512] = sum_rows((e0, e1, e2, e3)).astype(bf16)
    sum_ref[:, 512:1024] = out_ref[...]
    sum_ref[:, 1024:] = jnp.sum(kv_ref[...].astype(f32), axis=0).astype(bf16)


def final_sums(q_terms, out_own, kv_terms, after=()):
    args = (*q_terms, out_own, kv_terms)
    return kernel_call(
        final_sums_kernel,
        grid=(1,),
        in_specs=[whole_spec(arg.shape) for arg in args],
        out_specs=whole_spec((128, 1152)),
        out_shape=struct((128, 1152), bf16),
        after=after,
        name="final_sums",
    )(*args)


def torus_shift(dz, dx):
    return [
        (z * 4 + x, ((z + dz) % 4) * 4 + (x + dx) % 4) for z in range(4) for x in range(4)
    ]


def along_x(values, step):
    return lax.ppermute(values, "grp", torus_shift(0, step))


def along_z(values, step):
    return lax.ppermute(values, "grp", torus_shift(step, 0))


def keyval_grads_kernel(h0_ref, h1_ref, r0_ref, r1_ref, out_ref):
    total = dot_nn(h0_ref[...], r0_ref[...]) + dot_nn(h1_ref[...], r1_ref[...])
    out_ref[...] = total.astype(bf16).reshape(out_ref.shape)


def keyval_grads(h_turned, rights):
    left = pl.BlockSpec((1024, 2 * SPAN), lambda i: (i, 0))
    return kernel_call(
        keyval_grads_kernel,
        grid=(2,),
        in_specs=[left, left] + [whole_spec((2 * SPAN, 128))] * 2,
        out_specs=pl.BlockSpec((8, 128, 128), lambda i: (i, 0, 0)),
        out_shape=struct((GROUP, 128, 128), bf16),
        name="keyval_grads",
    )(*h_turned, *rights)


def project_back_kernel(q0_ref, q1_ref, r0_ref, r1_ref, wq_ref, wkv_ref, own_out, other_out):
    wq = wq_ref[...]
    wkv = wkv_ref[...].reshape(512, 128)
    for k, (q_ref, r_ref) in enumerate(((q0_ref, r0_ref), (q1_ref, r1_ref))):
        right = jnp.concatenate([q_ref[i] for i in range(4)], axis=1)
        d_h = (dot_nt(right, wq) + dot_nt(r_ref[...], wkv)).astype(bf16)
        spot = slice(k * SPAN, (k + 1) * SPAN)
        own_out[spot, :] = d_h[:SPAN]
        other_out[spot, :] = d_h[SPAN:]


def project_back(dqs, rights, wide_full, kv_full, after=()):
    args = (*dqs, *rights)
    out = pl.BlockSpec((2 * SPAN, 512), lambda i: (0, i))
    return kernel_call(
        project_back_kernel,
        grid=(4,),
        in_specs=[whole_spec(arg.shape) for arg in args]
        + [
            pl.BlockSpec((512, 512), lambda i: (i, 0)),
            pl.BlockSpec((4, 128, 128), lambda i: (i, 0, 0)),
        ],
        out_specs=[out, out],
        out_shape=[struct((2 * SPAN, D), bf16)] * 2,
        after=after,
        name="project_back",
    )(*args, wide_full, kv_full)


def as_rows(columns):
    return columns.T[:8, :]


def first_gain_kernel(wide_ref, kv_ref, own_ref, rep_ref, two_ref, two_rep, out_ref):
    grad = own_ref[...].astype(f32) + rep_ref[...].astype(f32)
    one = jnp.sum(wide_ref[...].astype(f32) * grad[:, :512], axis=1, keepdims=True)
    one = one + jnp.sum(kv_ref[...].astype(f32) * grad[:, 1024:], axis=1, keepdims=True)
    lane = lax.broadcasted_iota(jnp.int32, (128, 128), 1)
    rows = as_rows(jnp.where(lane == 0, one, 0.0))
    out_ref[...] = rows + (two_ref[...] + two_rep[...])


def gain_terms(wide_pack, kv_pack, sums, seconds):
    wide = pl.BlockSpec((128, 512), lambda i: (0, 0))
    args = (kv_pack, *sums, *seconds)
    return kernel_call(
        first_gain_kernel,
        grid=(1,),
        in_specs=[wide] + [whole_spec(arg.shape) for arg in args],
        out_specs=whole_spec((8, 128)),
        out_shape=struct((8, 128), f32),
        name="gain_terms",
    )(wide_pack, *args)


def second_gain_kernel(pack_ref, sum_ref, out_ref):
    total = jnp.zeros((pack_ref.shape[0], 1), f32)
    for column in range(0, WIDTH, 3 * TILE):
        span = slice(column, column + 2 * TILE)
        products = pack_ref[:, span].astype(f32) * sum_ref[:, span].astype(f32)
        total += jnp.sum(products, axis=1, keepdims=True)
    lane = lax.broadcasted_iota(jnp.int32, (128, 128), 1)
    out_ref[...] = as_rows(jnp.where(lane == 1, total, 0.0))


def second_gain_terms(mlp_pack, mlp_sum, after=()):
    return kernel_call(
        second_gain_kernel,
        grid=(1,),
        in_specs=[whole_spec(mlp_pack.shape), whole_spec(mlp_sum.shape)],
        out_specs=whole_spec((8, 128)),
        out_shape=struct((8, 128), f32),
        after=after,
        name="second_gain_terms",
    )(mlp_pack, mlp_sum)


def gain_adam_kernel(own, core, tp, both, w, m, s, w_o, m_o, s_o):
    total = (own[...] + core[...]) + (tp[...] + both[...])
    grad = total[:2, :] / w[...].astype(bf16).astype(f32)
    w_o[...], m_o[...], s_o[...] = adamw(w[...], m[...], s[...], grad, 1.0, 0.0)


def gain_adam(terms, states):
    args = (*terms, *[state.T for state in states])
    shape = args[-1].shape
    new = kernel_call(
        gain_adam_kernel,
        grid=(1,),
        in_specs=[whole_spec(arg.shape) for arg in args],
        out_specs=[whole_spec(shape)] * 3,
        out_shape=[struct(shape, f32)] * 3,
        name="gain_adam",
    )(*args)
    return [value.T for value in new]


def flat_view(values):
    rows, kinds, units = values.shape
    tiles = values.reshape(rows, kinds, units // SMALL, SMALL)
    tiles = with_layout_constraint(tiles, Layout(major_to_minor=(0, 2, 1, 3)))
    return tiles.transpose(0, 2, 1, 3).reshape(-1, SMALL)


def deep_view(values, shape):
    rows, kinds, units = shape
    tiles = values.reshape(rows, units // SMALL, kinds, SMALL).transpose(0, 2, 1, 3)
    tiles = with_layout_constraint(tiles, Layout(major_to_minor=(0, 2, 1, 3)))
    return tiles.reshape(shape)


def pack_kernel(quarter_ref, gu_ref, d_ref, out_ref):
    quarter = quarter_ref[0]
    start = window_start(quarter)
    stride = gu_ref.shape[0] // PACK_ROWS
    for tile in range(WINDOW_TILES):
        keep = jnp.where((quarter >= 2) & (tile == 0), 0.0, 1.0)
        for kind in range(3):
            if kind == 2:
                span = pl.ds(pl.multiple_of((start + tile) * SMALL, SMALL), SMALL)
                value = d_ref[:, span]
            else:
                value = gu_ref[pl.ds(2 * (start + tile) + kind, PACK_ROWS, stride), :]
            column = packed_column(tile, kind)
            out_ref[:, column : column + SMALL] = (value * keep).astype(bf16)


def pack_mlp(quarter, w_gateup, w_down, after=()):
    rows, units = w_down.shape
    per_row = 2 * units // SMALL
    return kernel_call(
        pack_kernel,
        prefetch=1,
        grid=(rows // PACK_ROWS,),
        in_specs=[
            pl.BlockSpec((PACK_ROWS * per_row, SMALL), lambda i, quarter: (i, 0)),
            pl.BlockSpec((PACK_ROWS, units), lambda i, quarter: (i, 0)),
        ],
        out_specs=pl.BlockSpec((PACK_ROWS, WIDTH), lambda i, quarter: (i, 0)),
        out_shape=struct((rows, WIDTH), bf16),
        after=after,
        name="pack_mlp",
    )(quarter, flat_view(w_gateup), w_down)


def mlp_adam_kernel(
    quarter_ref, own_ref, replica_ref, core_ref, both_ref, wg, mg, sg, wd, md, sd,
    wg_o, mg_o, sg_o, wd_o, md_o, sd_o, grads, *, rate_wide, rate_down,
):
    stride = wg.shape[0] // PACK_ROWS
    for part in range(4):
        same_core = quarter_ref[0] // 2 == part // 2
        same_replica = quarter_ref[0] % 2 == part % 2
        for tile in range(FIRST_OWN[part], FIRST_OWN[part + 1]):

            def grad(kind):
                column = packed_column(tile - WINDOW_STARTS[part], kind)
                spot = slice(column, column + SMALL)
                near = jnp.where(same_replica, own_ref[:, spot], replica_ref[:, spot])
                far = jnp.where(same_replica, core_ref[:, spot], both_ref[:, spot])
                return jnp.where(same_core, near, far).astype(f32)

            for kind in range(2):
                grads[pl.ds(2 * tile + kind, PACK_ROWS, stride), :] = grad(kind)
            span = slice(tile * SMALL, (tile + 1) * SMALL)
            wd_o[:, span], md_o[:, span], sd_o[:, span] = adamw(
                wd[:, span], md[:, span], sd[:, span], grad(2), rate_down, decay_rate
            )
    wg_o[...], mg_o[...], sg_o[...] = adamw(
        wg[...], mg[...], sg[...], grads[...], rate_wide, decay_rate
    )


def mlp_adam(quarter, sums, gateup, down, rate_wide, rate_down, after=()):
    rows, units = down[0].shape
    per_row = 2 * units // SMALL
    wide = pl.BlockSpec((PACK_ROWS * per_row, SMALL), lambda i, quarter: (i, 0))
    flat = pl.BlockSpec((PACK_ROWS, units), lambda i, quarter: (i, 0))
    grad = pl.BlockSpec((PACK_ROWS, WIDTH), lambda i, quarter: (i, 0))
    new = kernel_call(
        functools.partial(mlp_adam_kernel, rate_wide=rate_wide, rate_down=rate_down),
        prefetch=1,
        grid=(rows // PACK_ROWS,),
        in_specs=[grad] * 4 + [wide] * 3 + [flat] * 3,
        out_specs=[wide] * 3 + [flat] * 3,
        out_shape=[struct((rows * per_row, SMALL), f32)] * 3 + [struct(down[0].shape, f32)] * 3,
        scratch_shapes=[pltpu.VMEM((PACK_ROWS * per_row, SMALL), f32)],
        after=after,
        name="mlp_adam",
    )(quarter, *sums, *[flat_view(state) for state in gateup], *down)
    return [deep_view(value, gateup[0].shape) for value in new[:3]] + list(new[3:])


def attn_adam_kernel(
    core_ref, own_ref, rep_ref, other_ref, both_ref, wq, mq, sq, wo, mo, so, wkv, mkv, skv,
    wq_o, mq_o, sq_o, wo_o, mo_o, so_o, wkv_o, mkv_o, skv_o, *, rate_wide, rate_out,
):
    step = pl.program_id(0)
    mine = core_ref[0] == step

    def total(first, second, span):
        return first[:, span].astype(f32) + second[:, span].astype(f32)

    span = slice(0, 512)
    grad = jnp.where(mine, total(own_ref, rep_ref, span), total(other_ref, both_ref, span))
    wq_o[...], mq_o[...], sq_o[...] = adamw(wq[...], mq[...], sq[...], grad, rate_wide, decay_rate)
    span = slice(512, 1024)
    grad = jnp.where(mine, total(own_ref, rep_ref, span), total(other_ref, both_ref, span))
    wo_o[...], mo_o[...], so_o[...] = adamw(wo[...], mo[...], so[...], grad, rate_out, decay_rate)

    @pl.when(step == 0)
    def _():
        span = slice(1024, 1152)
        own = total(own_ref, rep_ref, span)
        other = total(other_ref, both_ref, span)
        first = jnp.where(mine, own, other)
        second = jnp.where(mine, other, own)
        low_half = lax.broadcasted_iota(jnp.int32, first.shape, 1) < HEAD_DIM
        grads = (
            jnp.where(low_half, first, pltpu.roll(second, HEAD_DIM, 1)),
            jnp.where(low_half, pltpu.roll(first, HEAD_DIM, 1), second),
        )
        for i, grad in enumerate(grads):
            wkv_o[:, i, :], mkv_o[:, i, :], skv_o[:, i, :] = adamw(
                wkv[:, i, :], mkv[:, i, :], skv[:, i, :], grad, rate_wide, decay_rate
            )


def attn_adam(core, sums, query, out, keyval, rate_wide, rate_out, after=()):
    rows, width = query[0].shape
    half = pl.BlockSpec((rows, width // 2), lambda i, core: (0, i))
    new = kernel_call(
        functools.partial(attn_adam_kernel, rate_wide=rate_wide, rate_out=rate_out),
        prefetch=1,
        grid=(2,),
        in_specs=[whole_spec(value.shape) for value in sums]
        + [half] * 6
        + [whole_spec(keyval[0].shape)] * 3,
        out_specs=[half] * 6 + [whole_spec(keyval[0].shape)] * 3,
        out_shape=[struct(state.shape, f32) for state in (*query, *out, *keyval)],
        after=after,
        name="attn_adam",
    )(core, *sums, *query, *out, *keyval)
    return new[:3], new[3:6], new[6:]


def swap_core(values):
    return lax.ppermute(values, "rep", CORE_SWAP)


def swap_replica(values):
    return lax.ppermute(values, "rep", REPLICA_SWAP)


def swap_tp(values):
    return lax.ppermute(values, "tp", TP_SWAP)


def swap_core_tp(values):
    return lax.ppermute(values, ("rep", "tp"), CORE_TP_SWAP)


def swap_both(values):
    return lax.ppermute(values, ("rep", "tp"), BOTH_SWAP)


def scatter_sums(parts, after=()):
    pairs = []
    for k in range(2):
        own, core, replica, both = parts[4 * k : 4 * k + 4]
        pairs += [(own, swap_core(core)), (replica, swap_core(both))]
    mine, replica, tp, both = add_quads(pairs, after=after)
    return mine, swap_replica(replica), swap_tp(tp), swap_both(both)


def spread(values):
    return lax.all_to_all(values, "grp", 0, 0, tiled=False)


def on_device(
    tokens,
    cotangent,
    offsets,
    w_query,
    moment_query,
    square_query,
    w_keyval,
    moment_keyval,
    square_keyval,
    w_out,
    moment_out,
    square_out,
    w_gateup,
    moment_gateup,
    square_gateup,
    w_down,
    moment_down,
    square_down,
    norm_gains,
    moment_gains,
    square_gains,
):
    sequences, own_len, width = tokens.shape
    core = lax.axis_index("rep") % 2
    core_list = core.reshape(1).astype(jnp.int32)
    place = jnp.stack([lax.axis_index("grp"), lax.axis_index("tp")]).astype(jnp.int32)

    wide_pack, kv_pack, kv_copies = pack_attn(
        core_list, w_query, w_out, w_keyval, norm_gains.T
    )
    wide_full = lax.all_gather(wide_pack, "grp", axis=0, tiled=True)
    kv_full = spread(kv_copies)
    quarter = (2 * core + lax.axis_index("rep") // 2).reshape(1).astype(jnp.int32)
    x_other = swap_core(tokens)
    dy_replica = swap_replica(cotangent)
    dy_parts = (cotangent, swap_core(cotangent), dy_replica, swap_core(dy_replica))
    offsets_other = swap_core(offsets)
    offsets_all = jnp.stack([offsets, offsets_other], axis=1).reshape(2 * sequences, GROUP)
    steps_in = jnp.arange(own_len, dtype=jnp.int32)
    starts = lax.dynamic_slice_in_dim(offsets_all, place[0], 1, 1)
    positions = (starts + steps_in[None, :]).reshape(2 * sequences * own_len)
    half_dim = HEAD_DIM // 2
    inverse = rope_base ** (-2.0 * jnp.arange(half_dim, dtype=f32) / HEAD_DIM)
    angles = positions.astype(f32)[:, None] * inverse[None, :]
    cos_part = jnp.cos(angles)
    sin_part = jnp.sin(angles)
    cos = jnp.concatenate([cos_part] * 4, axis=1)
    sin = jnp.concatenate([-sin_part, sin_part] * 2, axis=1)

    kv_one = project_kv(1, place, tokens, x_other, kv_full, cos, sin)
    dy_t = transposed(place, dy_parts)
    kv_zero = project_kv(0, place, tokens, x_other, kv_full, cos, sin, after=(kv_one[0],))
    mlp_pack = pack_mlp(quarter, w_gateup, w_down, after=(kv_zero[0],))
    mlp_full = lax.all_gather(mlp_pack, "grp", axis=0, tiled=True)
    h_turned = [kv_zero[1], kv_one[1]]
    kvs = {1: spread(kv_one[2])}
    kvs[0] = spread(kv_zero[2])
    q_one = project_q(1, place, kv_one[0], wide_full, cos, sin, after=(mlp_pack, kv_zero[0], dy_t))
    q_zero = project_q(0, place, kv_zero[0], wide_full, cos, sin, after=(q_one,))
    qs = [q_zero, q_one]
    one = attend(1, offsets_all, place, qs[1], kvs[1], wide_full, after=(q_zero,))
    one_share = add_low(one[2], swap_core(one[3]))
    received = swap_tp(one_share)
    zero = attend(0, offsets_all, place, qs[0], kvs[0], wide_full, after=(one_share,))
    os_ = [zero[0], one[0]]
    lses = [zero[1], one[1]]
    zero_part = add_low(zero[2], received)
    mid, h_two = middle(place, tokens, zero_part, swap_core(zero[3]), kv_full)
    h_parts = []
    for first, second in ((h_two, swap_replica(h_two)), (swap_tp(h_two), swap_both(h_two))):
        h_parts += [first, swap_core(first), second, swap_core(second)]
    side, mlp_sums = mlp(place, h_parts, dy_parts, dy_t, mlp_full)
    mlp_own = lax.psum_scatter(mlp_sums, "grp", scatter_dimension=0, tiled=True)

    sums = scatter_sums(mlp_back(side, mlp_full, 0, 2))
    out_parts = mlp_back(side, mlp_full, 2, 1, after=(sums[0],))
    out_shares = scatter_sums(out_parts)
    da = middle_back(place, sums, mid, cotangent, kv_full, after=(out_shares[0],))
    da_core = swap_core(da)
    da_parts = [da, da_core, swap_tp(da), swap_tp(da_core)]

    def back_of(k, after=()):
        return attend_back(
            k, offsets_all, place, da_parts[2 * k], da_parts[2 * k + 1], wide_full, qs[k], kvs[k],
            os_[k], lses[k], cos, sin, after=after,
        )

    first_back = back_of(0)
    out_sums = out_grads(da_parts, os_, after=(first_back[0],))
    out_own = lax.psum_scatter(out_sums, "grp", scatter_dimension=0, tiled=True)
    second_back = back_of(1, after=(out_sums,))
    dqs = [first_back[0], second_back[0]]
    mlp_replica = swap_replica(mlp_own)
    gain_two = second_gain_terms(mlp_pack, mlp_own, after=(second_back[0], mlp_replica))
    first_right = right_side(0, place, spread(first_back[1]), cos, sin, after=(gain_two,))
    q_sums = query_grads(place, h_turned, dqs, after=(first_right,))
    rate_wide = 2.0 * D ** (-0.5)
    rate_out = 2.0 * max(1, 2 * D // LENGTH) ** (-0.5)
    rate_down = 2.0 * FF ** (-0.5)
    new_mlp = mlp_adam(
        quarter,
        (mlp_own, mlp_replica, swap_core(mlp_own), swap_core(mlp_replica)),
        (w_gateup, moment_gateup, square_gateup),
        (w_down, moment_down, square_down),
        rate_wide,
        rate_down,
        after=(q_sums[0],),
    )
    x_terms = [q_sums[0]] + [along_x(q_sums[i], i) for i in range(1, 4)]
    q_lines = line_sums(place, x_terms, after=(new_mlp[-1],))
    second_right = right_side(1, place, spread(second_back[1]), cos, sin, after=(q_lines[0],))
    rights = [first_right, second_right]
    kv_sums = keyval_grads(h_turned, rights)
    own_part, other_part = project_back(dqs, rights, wide_full, kv_full, after=(kv_sums,))
    dh_share = add_low(own_part, swap_core(other_part))
    dh_received = swap_tp(dh_share)
    layer_mine = layer_part(mid, out_shares, after=(dh_share,))
    z_terms = [q_lines[0]] + [along_z(q_lines[i], i) for i in range(1, 4)]
    own = final_sums(z_terms, out_own, spread(kv_sums), after=(layer_mine,))

    replica = swap_replica(own)
    gain_own = gain_terms(
        wide_pack, kv_pack, (own, replica), (gain_two, swap_replica(gain_two))
    )
    layer_out = layer_out_of(place, layer_mine, swap_tp(layer_mine), after=(gain_own,))
    new_query, new_out, new_keyval = attn_adam(
        core_list,
        (own, replica, swap_core(own), swap_core(replica)),
        (w_query, moment_query, square_query),
        (w_out, moment_out, square_out),
        (w_keyval, moment_keyval, square_keyval),
        rate_wide,
        rate_out,
        after=(layer_out,),
    )
    input_grad = input_grad_of(
        place, (da, da_parts[2]), dh_share, dh_received, tokens, kv_full, after=(new_out[0],)
    )
    new_gains = gain_adam(
        (gain_own, swap_core(gain_own), swap_tp(gain_own), swap_core_tp(gain_own)),
        (norm_gains, moment_gains, square_gains),
    )
    return (
        layer_out,
        input_grad,
        *new_query,
        *new_keyval,
        *new_out,
        *new_mlp,
        *new_gains,
    )


def solution(mesh):
    rows = P("rep", "grp", None)
    flat = P("grp", "tp")
    deep = P("grp", None, "tp")
    states = (flat,) * 3 + (deep,) * 3 + (flat,) * 3 + (deep,) * 3 + (flat,) * 3
    states += (P("grp", None),) * 3
    return jax.shard_map(
        on_device,
        mesh=mesh,
        in_specs=(rows, rows, P("rep", None)) + states,
        out_specs=(rows, rows) + states,
        check_vma=False,
    )
```

```python
import functools

import jax
import jax.numpy as jnp
from jax import lax
from jax.experimental import pallas as pl
from jax.experimental.layout import Layout, with_layout_constraint
from jax.experimental.pallas import tpu as pltpu
from jax.sharding import PartitionSpec as P

D = 2048
HEAD_DIM = 64
FF = 5632
LENGTH = 2048
STEP = 10
GROUP = 16
SPAN = 128
TILE = 256

norm_epsilon = 1e-05
rope_base = 10000.0
neg_large = -1e30
beta_first = 0.9
beta_second = 0.95
adam_epsilon = 1e-08
decay_rate = 0.1

bf16 = jnp.bfloat16
f32 = jnp.float32

VMEM_LIMIT = 63 * 1024 * 1024

CORE_SWAP = [(0, 1), (1, 0), (2, 3), (3, 2)]
REPLICA_SWAP = [(0, 2), (1, 3), (2, 0), (3, 1)]
BOTH_CORES_SWAP = [(0, 3), (1, 2), (2, 1), (3, 0)]
TP_SWAP = [(0, 1), (1, 0)]
CORE_TP_SWAP = [(2 * r + t, 2 * (r ^ 1) + (1 - t)) for r in range(4) for t in range(2)]
BOTH_SWAP = [(2 * r + t, 2 * (r ^ 2) + (1 - t)) for r in range(4) for t in range(2)]


def struct(shape, dtype):
    return jax.ShapeDtypeStruct(shape, dtype)


def kernel_call(
    kernel, *, name, out_shape, grid=(), in_specs=None, out_specs=None, scratch_shapes=(), prefetch=0,
    after=(),
):
    first = prefetch + len(in_specs)

    def body(*refs):
        kernel(*refs[:first], *refs[first + len(after) :])

    grid_spec = pltpu.PrefetchScalarGridSpec(
        num_scalar_prefetch=prefetch,
        grid=grid,
        in_specs=list(in_specs) + [pl.BlockSpec(memory_space=pl.ANY)] * len(after),
        out_specs=out_specs,
        scratch_shapes=list(scratch_shapes),
    )
    call = pl.pallas_call(
        body,
        grid_spec=grid_spec,
        out_shape=out_shape,
        compiler_params=pltpu.CompilerParams(vmem_limit_bytes=VMEM_LIMIT),
        name=name,
    )
    return lambda *args: call(*args, *after)


def dot_nn(left, right):
    return lax.dot_general(left, right, (((1,), (0,)), ((), ())), preferred_element_type=f32)


def dot_nt(left, right):
    return lax.dot_general(left, right, (((1,), (1,)), ((), ())), preferred_element_type=f32)


def dot_tn(left, right):
    return lax.dot_general(left, right, (((0,), (0,)), ((), ())), preferred_element_type=f32)


def adamw(weight, moment, square, grad, rate, decay):
    moment = beta_first * moment + (1.0 - beta_first) * grad
    square = beta_second * square + (1.0 - beta_second) * grad * grad
    fix_first = 1.0 - beta_first**STEP
    fix_second = 1.0 - beta_second**STEP
    update = moment / fix_first / (jnp.sqrt(square / fix_second) + adam_epsilon)
    return (weight * (1.0 - rate * decay) - rate * update, moment, square)


def norm_back(upstream, gain, normed, scale):
    weighted = upstream * gain
    return scale * (weighted - normed * jnp.mean(weighted * normed, axis=-1, keepdims=True))


def partner(values):
    lane = lax.broadcasted_iota(jnp.int32, values.shape, 1)
    up = pltpu.roll(values, 96, 1)
    down = pltpu.roll(values, 32, 1)
    return jnp.where(lane % HEAD_DIM < HEAD_DIM // 2, up, down)


def row_of(block):
    return jnp.concatenate([block[i : i + 1, :] for i in range(GROUP)], axis=1)


def rms_scale(values):
    return lax.rsqrt(jnp.mean(values * values, axis=-1, keepdims=True) + norm_epsilon)


def gain_row(gain_ref, index):
    return row_of(gain_ref[:, index, :].astype(f32))


GAIN_SPEC = pl.BlockSpec((GROUP, 16, 128), lambda *_: (0, 8, 0))
WQ_SPEC = pl.BlockSpec((D, 512), lambda *_: (0, 0))
WO_SPEC = pl.BlockSpec((D, 512), lambda *_: (0, 1))
WKV_SPEC = pl.BlockSpec((GROUP, 128, 128), lambda *_: (0, 0, 0))
ROWS_SPEC = pl.BlockSpec((SPAN, D), lambda *_: (0, 0))


def half_of(place, k):
    return place[1] if k == 0 else 1 - place[1]


STRIP = 128
STRIP_SPEC = pl.BlockSpec((STRIP, D), lambda i, *_: (i, 0))
HALF_SPEC = pl.BlockSpec((SPAN // 2, D), lambda i, *_: (i, 0))


def seq_strip(k):
    return pl.BlockSpec((1, STRIP, D), lambda i, *refs: (half_of(refs[-1], k), i, 0))


def seq_spec(k):
    return pl.BlockSpec((1, SPAN, D), lambda *ids: (half_of(ids[-1], k), 0, 0))


def turn_spec(k):
    return pl.BlockSpec((SPAN, 128), lambda i, *refs: (2 * half_of(refs[-1], k) + i, 0))


def whole_spec(shape):
    return pl.BlockSpec(shape, lambda *_: (0,) * len(shape))


def pack_attn_kernel(core_ref, wq_ref, wo_ref, wkv_ref, gain_ref, wide_ref, kv_ref, copies_ref):
    lane = lax.broadcasted_iota(jnp.int32, (128, 128), 1)
    low_half = lane < HEAD_DIM
    first_core = core_ref[0] == 0
    key = jnp.where(first_core, wkv_ref[:, 0, :], pltpu.roll(wkv_ref[:, 0, :], HEAD_DIM, 1))
    value = jnp.where(first_core, pltpu.roll(wkv_ref[:, 1, :], HEAD_DIM, 1), wkv_ref[:, 1, :])
    kv = jnp.where(low_half, key, value).astype(bf16)
    wide_ref[:, :512] = wq_ref[...].astype(bf16)
    wide_ref[:, 512:] = wo_ref[...].astype(bf16)
    kv_ref[...] = kv
    gains = jnp.concatenate([gain_ref[...], jnp.zeros((14, 128), f32)], axis=0).astype(bf16)
    for g in range(GROUP):
        copies_ref[g, :128, :] = kv
        copies_ref[g, 128:, :] = gains


def pack_attn(core, w_query, w_out, w_keyval, gains):
    rows = w_query.shape[0]
    half = pl.BlockSpec((rows, 512), lambda i, core: (0, core[0]))
    shapes = [(rows, 1024), (rows, 128), (GROUP, rows + 16, 128)]
    return kernel_call(
        pack_attn_kernel,
        prefetch=1,
        grid=(1,),
        in_specs=[half, half, whole_spec(w_keyval.shape), whole_spec(gains.shape)],
        out_specs=[whole_spec(shape) for shape in shapes],
        out_shape=[struct(shape, bf16) for shape in shapes],
        name="pack_attn",
    )(core, w_query, w_out, w_keyval, gains)


def project_kv_kernel(
    place_ref, own_ref, other_ref, wkv_ref, gain_ref, cos_ref, sin_ref, h_ref, turned_ref, kv_ref
):
    mine = pl.program_id(0) == 0
    x = jnp.where(mine, own_ref[0].astype(f32), other_ref[0].astype(f32))
    h = (x * rms_scale(x) * gain_row(gain_ref, 0)).astype(bf16)
    h_ref[...] = h
    low_half = lax.broadcasted_iota(jnp.int32, (SPAN, 128), 1) < HEAD_DIM
    keyval = dot_nn(h, wkv_ref[...].reshape(D, 128))
    turned = keyval * cos_ref[...] + partner(keyval) * sin_ref[...]
    kv = jnp.where(low_half, turned, keyval).astype(bf16)
    kv_ref[...] = jnp.broadcast_to(kv[None], (GROUP, SPAN, 128))
    turned_ref[...] = h.T


def project_kv(k, place, x_own, x_other, kv_full, cos, sin, after=()):
    return kernel_call(
        project_kv_kernel,
        prefetch=1,
        grid=(2,),
        in_specs=[seq_spec(k), seq_spec(k), WKV_SPEC, GAIN_SPEC, turn_spec(k), turn_spec(k)],
        out_specs=[
            pl.BlockSpec((SPAN, D), lambda i, *_: (i, 0)),
            pl.BlockSpec((D, SPAN), lambda i, *_: (0, i)),
            pl.BlockSpec((GROUP, SPAN, 128), lambda i, *_: (0, i, 0)),
        ],
        out_shape=[
            struct((2 * SPAN, D), bf16),
            struct((D, 2 * SPAN), bf16),
            struct((GROUP, 2 * SPAN, 128), bf16),
        ],
        after=after,
        name="project_kv",
    )(place, x_own, x_other, kv_full, kv_full, cos, sin)


def project_q_kernel(place_ref, h_ref, wq_ref, cos_ref, sin_ref, q_ref):
    cos = cos_ref[...]
    sin = sin_ref[...]
    low_half = lax.broadcasted_iota(jnp.int32, (SPAN, 128), 1) < HEAD_DIM
    query = dot_nn(h_ref[...], wq_ref[...])
    for pair in range(4):
        block = query[:, pair * 128 : (pair + 1) * 128]
        turned = (block * cos + partner(block) * sin) * (HEAD_DIM**-0.5)
        q_ref[2 * pair] = jnp.where(low_half, turned, 0.0).astype(bf16)
        q_ref[2 * pair + 1] = jnp.where(
            low_half, pltpu.roll(turned, HEAD_DIM, 1), 0.0
        ).astype(bf16)


def project_q(k, place, h, wide_full, cos, sin, after=()):
    return kernel_call(
        project_q_kernel,
        prefetch=1,
        grid=(2,),
        in_specs=[pl.BlockSpec((SPAN, D), lambda i, *_: (i, 0)), WQ_SPEC, turn_spec(k), turn_spec(k)],
        out_specs=pl.BlockSpec((8, SPAN, 128), lambda i, *_: (0, i, 0)),
        out_shape=struct((8, 2 * SPAN, 128), bf16),
        after=after,
        name="project_q",
    )(place, h, wide_full, cos, sin)


CHUNK = 512
BACK_CHUNK = 1024


def causal_offsets():
    key = lax.broadcasted_iota(jnp.int32, (128, 256), 0)
    query = lax.broadcasted_iota(jnp.int32, (128, 256), 1) % SPAN
    return key - query


def masked(raw, differ, own, off_ref, seq, c):
    parts = []
    blocks = raw.shape[0] // 128
    for j in range(blocks):
        allowed = differ <= own - off_ref[seq, blocks * c + j]
        parts.append(jnp.where(allowed, raw[j * 128 : (j + 1) * 128], neg_large))
    return jnp.concatenate(parts, axis=0)


def attend_kernel(
    off_ref, place_ref, q_ref, kv_ref, wo_ref, o_ref, lse_ref, own_ref, other_ref, kvt, scores, *, k
):
    step = pl.program_id(0)
    seq = 2 * half_of(place_ref, k) + step
    kvt[...] = kv_ref[...].reshape(LENGTH, 128).T
    own = off_ref[seq, place_ref[0]]
    differ = causal_offsets()
    blocks = CHUNK // 128

    for pair in range(4):
        q = q_ref[2 * pair : 2 * pair + 2].reshape(256, 128)
        top = jnp.full((1, 256), neg_large, f32)
        for c in range(LENGTH // CHUNK):
            raw = dot_nt(kv_ref[blocks * c : blocks * (c + 1)].reshape(CHUNK, 128), q)
            score = masked(raw, differ, own, off_ref, seq, c)
            scores[pair % 2, c * CHUNK : (c + 1) * CHUNK, :] = score
            top = jnp.maximum(top, jnp.max(score, axis=0, keepdims=True))
        total = jnp.zeros((1, 256), f32)
        mixed = jnp.zeros((128, 256), f32)
        for c in range(LENGTH // CHUNK):
            weight = jnp.exp(scores[pair % 2, c * CHUNK : (c + 1) * CHUNK, :] - top)
            total = total + jnp.sum(weight, axis=0, keepdims=True)
            mixed = mixed + dot_nn(kvt[:, c * CHUNK : (c + 1) * CHUNK], weight.astype(bf16))
        out = (mixed[HEAD_DIM:, :] / total).T
        o_ref[pair] = jnp.concatenate([out[:SPAN], out[SPAN:]], axis=1).astype(bf16)
        lse_ref[0, pair : pair + 1, :] = top + jnp.log(total)

    heads = jnp.concatenate([o_ref[i] for i in range(4)], axis=1)
    part = dot_nt(heads, wo_ref[...]).astype(bf16)

    @pl.when(step == 0)
    def _():
        own_ref[...] = part

    @pl.when(step == 1)
    def _():
        other_ref[...] = part


def attend(k, offsets, place, q, kv_all, wo_full, after=()):
    grid_spec = dict(
        prefetch=2,
        grid=(2,),
        in_specs=[
            pl.BlockSpec((8, SPAN, 128), lambda i, *_: (0, i, 0)),
            pl.BlockSpec((GROUP, SPAN, 128), lambda i, *_: (0, i, 0)),
            WO_SPEC,
        ],
        out_specs=[
            pl.BlockSpec((4, SPAN, 128), lambda i, *_: (0, i, 0)),
            pl.BlockSpec((1, 4, 256), lambda i, *_: (i, 0, 0)),
            ROWS_SPEC,
            ROWS_SPEC,
        ],
        scratch_shapes=[pltpu.VMEM((128, LENGTH), bf16), pltpu.VMEM((2, LENGTH, 256), f32)],
    )
    return kernel_call(
        functools.partial(attend_kernel, k=k),
        **grid_spec,
        out_shape=[
            struct((4, 2 * SPAN, 128), bf16),
            struct((2, 4, 256), f32),
            struct((SPAN, D), bf16),
            struct((SPAN, D), bf16),
        ],
        after=after,
        name="attend",
    )(offsets, place, q, kv_all, wo_full)


def share_kernel(own_ref, other_ref, out_ref):
    out_ref[...] = (own_ref[...].astype(f32) + other_ref[...].astype(f32)).astype(bf16)


def add_low(first, second, after=()):
    rows, width = first.shape
    block = pl.BlockSpec((128, width), lambda i: (i, 0))
    return kernel_call(
        share_kernel,
        grid=(rows // 128,),
        in_specs=[block, block],
        out_specs=block,
        out_shape=struct(first.shape, bf16),
        after=after,
        name="add_low",
    )(first, second)


def middle_kernel(place_ref, x_ref, one_ref, two_ref, gain_ref, mid_ref, h_ref):
    total = one_ref[...].astype(f32) + two_ref[...].astype(f32)
    mid = x_ref[0].astype(f32) + total
    mid_ref[...] = mid
    h_ref[...] = (mid * rms_scale(mid) * gain_row(gain_ref, 1)).astype(bf16)


def middle(place, x_own, one, two, attn_full):
    return kernel_call(
        middle_kernel,
        prefetch=1,
        grid=(SPAN // STRIP,),
        in_specs=[seq_strip(0), STRIP_SPEC, STRIP_SPEC, GAIN_SPEC],
        out_specs=[STRIP_SPEC, STRIP_SPEC],
        out_shape=[struct((SPAN, D), f32), struct((SPAN, D), bf16)],
        name="middle",
    )(place, x_own, one, two, attn_full)


def sum_rows(refs):
    return sum(ref[...].astype(f32) for ref in refs)


def middle_back_kernel(place_ref, p0, p1, p2, p3, mid_ref, dy_ref, gain_ref, da_ref):
    upstream = sum_rows((p0, p1, p2, p3))
    mid = mid_ref[...]
    scale = rms_scale(mid)
    d_norm = norm_back(upstream, gain_row(gain_ref, 1), mid * scale, scale)
    da_ref[...] = (dy_ref[0].astype(f32) + d_norm).astype(bf16)


def middle_back(place, parts, mid, dy_own, attn_full, after=()):
    return kernel_call(
        middle_back_kernel,
        prefetch=1,
        grid=(SPAN // STRIP,),
        in_specs=[STRIP_SPEC] * 5 + [seq_strip(0), GAIN_SPEC],
        out_specs=STRIP_SPEC,
        out_shape=struct((SPAN, D), bf16),
        after=after,
        name="middle_back",
    )(place, *parts, mid, dy_own, attn_full)


def layer_part_kernel(mid_ref, p0, p1, p2, p3, out_ref):
    out_ref[...] = (mid_ref[...] + sum_rows((p0, p1, p2, p3))).astype(bf16)


def layer_part(mid, parts, after=()):
    return kernel_call(
        layer_part_kernel,
        grid=(SPAN // STRIP,),
        in_specs=[STRIP_SPEC] * 5,
        out_specs=STRIP_SPEC,
        out_shape=struct((SPAN, D), bf16),
        after=after,
        name="layer_part",
    )(mid, *parts)


def row_outputs_kernel(
    place_ref, mine_ref, other_ref, da0, da1, s0, s1, r0, r1, x_ref, gain_ref, out_ref, layer_ref
):
    layer_ref[half_of(place_ref, 0)] = mine_ref[...]
    layer_ref[half_of(place_ref, 1)] = other_ref[...]
    gain = gain_row(gain_ref, 0)
    for k, (da_ref, share, received) in enumerate(((da0, s0, r1), (da1, s1, r0))):
        upstream = share[...].astype(f32) + received[...].astype(f32)
        m = half_of(place_ref, k)
        x = x_ref[m].astype(f32)
        scale = rms_scale(x)
        out_ref[m] = da_ref[...].astype(f32) + norm_back(upstream, gain, x * scale, scale)


def row_outputs(place, mine, other, das, share, received, x_own, kv_full, after=()):
    steps = 2
    rows = SPAN // steps
    block = pl.BlockSpec((rows, D), lambda i, *_: (i, 0))
    second = pl.BlockSpec((rows, D), lambda i, *_: (steps + i, 0))
    seqs = pl.BlockSpec((2, rows, D), lambda i, *_: (0, i, 0))
    return kernel_call(
        row_outputs_kernel,
        prefetch=1,
        grid=(steps,),
        in_specs=[block] * 5 + [second, block, second, seqs, GAIN_SPEC],
        out_specs=[seqs, seqs],
        out_shape=[struct((2, SPAN, D), f32), struct((2, SPAN, D), bf16)],
        after=after,
        name="row_outputs",
    )(place, mine, other, *das, share, share, received, received, x_own, kv_full)


PACK_ROWS = 16
ALL_ROWS = 8 * SPAN
SMALL = 128
WINDOW_TILES = 6
WIDTH = 3 * WINDOW_TILES * SMALL
WINDOW_STARTS = (0, 6, 11, 16)
FIRST_OWN = (0, 6, 12, 17, 22)


def window_start(quarter):
    return jnp.where(quarter < 2, 6 * quarter, 5 * quarter + 1)


def packed_column(tile, kind):
    return 3 * TILE * (tile // 2) + TILE * kind + SMALL * (tile % 2)


def transpose_kernel(place_ref, *refs):
    parts, out_ref = refs[:-1], refs[-1]
    for k in range(2):
        for i, ref in enumerate(parts):
            start = (len(parts) * k + i) * SPAN
            out_ref[:, start : start + SPAN] = ref[half_of(place_ref, k)].T


def transposed(place, parts, after=()):
    seqs = pl.BlockSpec((2, SPAN, 512), lambda i, *_: (0, 0, i))
    return kernel_call(
        transpose_kernel,
        prefetch=1,
        grid=(D // 512,),
        in_specs=[seqs] * 4,
        out_specs=pl.BlockSpec((512, ALL_ROWS), lambda i, *_: (i, 0)),
        out_shape=struct((D, ALL_ROWS), bf16),
        after=after,
        name="transposed",
    )(place, *parts)


def mlp_kernel(place_ref, *refs):
    h_parts, dy_parts, dyt_ref, w_ref = refs[:8], refs[8:12], refs[12], refs[13]
    side_ref, sum_ref, h, ht, dy, dyt, sems = refs[14:]
    step = pl.program_id(0)

    def part_copies():
        copies = []
        for i, ref in enumerate(h_parts):
            spot = h.at[i * SPAN : (i + 1) * SPAN]
            copies.append(pltpu.make_async_copy(ref, spot, sems.at[i]))
        for k in range(2):
            for i, ref in enumerate(dy_parts):
                number = 4 * k + i
                spot = dy.at[number * SPAN : (number + 1) * SPAN]
                source = ref.at[half_of(place_ref, k)]
                copies.append(pltpu.make_async_copy(source, spot, sems.at[8 + number]))
        return copies

    turned_copy = pltpu.make_async_copy(dyt_ref, dyt, sems.at[16])

    @pl.when(step == 0)
    def _():
        copies = part_copies()
        for copy in copies:
            copy.start()
        turned_copy.start()
        for copy in copies:
            copy.wait()

    for start in range(0, ALL_ROWS, 256):
        rows = slice(start, start + 256)
        both = dot_nn(h[rows, :], w_ref[:, : 2 * TILE])
        upstream = dot_nn(dy[rows, :], w_ref[:, 2 * TILE :])
        gate = both[:, :TILE]
        up = both[:, TILE:]
        sigmoid = jax.nn.sigmoid(gate)
        active = gate * sigmoid
        side_ref[rows, :TILE] = (
            upstream * up * (sigmoid * (1.0 + gate * (1.0 - sigmoid)))
        ).astype(bf16)
        side_ref[rows, TILE : 2 * TILE] = (upstream * active).astype(bf16)
        side_ref[rows, 2 * TILE :] = (active * up).astype(bf16)

    @pl.when(step == 0)
    def _():
        ht[...] = h[...].T
        turned_copy.wait()

    sum_ref[:, : 2 * TILE] = dot_nn(ht[...], side_ref[:, : 2 * TILE]).astype(bf16)
    sum_ref[:, 2 * TILE :] = dot_nn(dyt[...], side_ref[:, 2 * TILE :]).astype(bf16)


def mlp(place, h_parts, dy_parts, dy_t, w_full, after=()):
    width = 3 * TILE
    return kernel_call(
        mlp_kernel,
        prefetch=1,
        grid=(WIDTH // width,),
        in_specs=[pl.BlockSpec(memory_space=pl.ANY)] * 13
        + [pl.BlockSpec((D, width), lambda i, *_: (0, i))],
        out_specs=[
            pl.BlockSpec((ALL_ROWS, width), lambda i, *_: (0, i)),
            pl.BlockSpec((D, width), lambda i, *_: (0, i)),
        ],
        out_shape=[struct((ALL_ROWS, WIDTH), bf16), struct((D, WIDTH), bf16)],
        scratch_shapes=[
            pltpu.VMEM((ALL_ROWS, D), bf16),
            pltpu.VMEM((D, ALL_ROWS), bf16),
            pltpu.VMEM((ALL_ROWS, D), bf16),
            pltpu.VMEM((D, ALL_ROWS), bf16),
            pltpu.SemaphoreType.DMA((17,)),
        ],
        after=after,
        name="mlp",
    )(place, *h_parts, *dy_parts, dy_t, w_full)


def mlp_back_kernel(side_ref, w_ref, *outs, first, count):
    total = jnp.zeros((ALL_ROWS, w_ref.shape[0]), f32)
    for column in range(0, WIDTH, 3 * TILE):
        span = slice(column + first * TILE, column + (first + count) * TILE)
        total = total + dot_nt(side_ref[:, span], w_ref[:, span])
    for out, i in zip(outs, range(8)):
        out[...] = total[i * SPAN : (i + 1) * SPAN].astype(bf16)


def mlp_back(side, w_full, first, count, after=()):
    return kernel_call(
        functools.partial(mlp_back_kernel, first=first, count=count),
        grid=(D // 512,),
        in_specs=[whole_spec((ALL_ROWS, WIDTH)), pl.BlockSpec((512, WIDTH), lambda i: (i, 0))],
        out_specs=[pl.BlockSpec((SPAN, 512), lambda i: (0, i))] * 8,
        out_shape=[struct((SPAN, D), bf16)] * 8,
        after=after,
        name="mlp_back",
    )(side, w_full)


def quad_kernel(*refs):
    for i in range(4):
        total = refs[2 * i][...].astype(f32) + refs[2 * i + 1][...].astype(f32)
        refs[8 + i][...] = total.astype(bf16)


def add_quads(pairs, after=()):
    return kernel_call(
        quad_kernel,
        grid=(2,),
        in_specs=[HALF_SPEC] * 8,
        out_specs=[HALF_SPEC] * 4,
        out_shape=[struct((SPAN, D), bf16)] * 4,
        after=after,
        name="add_quads",
    )(*[value for pair in pairs for value in pair])


def attend_back_kernel(
    off_ref, place_ref, own_ref, other_ref, wo_ref, q_ref, kv_ref, o_ref, lse_ref, cos_ref,
    sin_ref, dq_ref, dkv_ref, kvt, d_heads, dkv, *, k,
):
    step = pl.program_id(0)
    seq = 2 * half_of(place_ref, k) + step
    kvt[...] = kv_ref[...].reshape(LENGTH, 128).T
    dkv[...] = jnp.zeros_like(dkv)
    d_out_rows = jnp.where(step == 0, own_ref[...].astype(f32), other_ref[...].astype(f32))
    d_all = dot_nn(d_out_rows.astype(bf16), wo_ref[...])
    for pair in range(4):
        d_heads[pair] = d_all[:, pair * 128 : (pair + 1) * 128].astype(bf16).astype(f32)
    own = off_ref[seq, place_ref[0]]
    differ = causal_offsets()
    lane = lax.broadcasted_iota(jnp.int32, (SPAN, 128), 1)
    high_half = lane >= HEAD_DIM
    cos = cos_ref[...]
    sin = sin_ref[...]
    blocks = BACK_CHUNK // 128

    for pair in range(4):
        q = q_ref[2 * pair : 2 * pair + 2].reshape(256, 128)
        d_out = d_heads[pair]
        first = jnp.where(high_half, pltpu.roll(d_out, HEAD_DIM, 1), 0.0).astype(bf16)
        second = jnp.where(high_half, d_out, 0.0).astype(bf16)
        d_o = jnp.concatenate([first, second], axis=0)
        dots = (d_out * o_ref[pair].astype(f32)).T
        inner = jnp.concatenate(
            [
                jnp.sum(dots[:HEAD_DIM], axis=0, keepdims=True),
                jnp.sum(dots[HEAD_DIM:], axis=0, keepdims=True),
            ],
            axis=1,
        )
        lse = lse_ref[0, pair : pair + 1, :]
        d_query = jnp.zeros((128, 256), f32)
        for c in range(LENGTH // BACK_CHUNK):
            kv = kv_ref[blocks * c : blocks * (c + 1)].reshape(BACK_CHUNK, 128)
            score = masked(dot_nt(kv, q), differ, own, off_ref, seq, c)
            prob = jnp.exp(score - lse)
            d_prob = dot_nt(kv, d_o)
            d_score = (prob * (d_prob - inner)).astype(bf16)
            span = slice(c * BACK_CHUNK, (c + 1) * BACK_CHUNK)
            dkv[span, :] += dot_nn(d_score, q) + dot_nn(prob.astype(bf16), d_o)
            d_query = d_query + dot_nn(kvt[:, span], d_score)
        turned = d_query[:HEAD_DIM, :].T
        block = jnp.concatenate([turned[:SPAN], turned[SPAN:]], axis=1)
        block = (block * cos - partner(block) * sin) * (HEAD_DIM**-0.5)
        dq_ref[pair] = block.astype(bf16)

    dkv_ref[...] = dkv[...].astype(bf16).reshape(GROUP, SPAN, 128)


def attend_back(k, offsets, place, da_own, da_other, wo_full, q, kv_all, o, lse, cos, sin, after=()):
    turn = turn_spec(k)
    heads = pl.BlockSpec((4, SPAN, 128), lambda i, *_: (0, i, 0))
    group = pl.BlockSpec((GROUP, SPAN, 128), lambda i, *_: (0, i, 0))
    grid_spec = dict(
        prefetch=2,
        grid=(2,),
        in_specs=[
            ROWS_SPEC,
            ROWS_SPEC,
            WO_SPEC,
            pl.BlockSpec((8, SPAN, 128), lambda i, *_: (0, i, 0)),
            group,
            heads,
            pl.BlockSpec((1, 4, 256), lambda i, *_: (i, 0, 0)),
            turn,
            turn,
        ],
        out_specs=[heads, group],
        scratch_shapes=[
            pltpu.VMEM((128, LENGTH), bf16),
            pltpu.VMEM((4, SPAN, 128), f32),
            pltpu.VMEM((LENGTH, 128), f32),
        ],
    )
    return kernel_call(
        functools.partial(attend_back_kernel, k=k),
        **grid_spec,
        out_shape=[
            struct((4, 2 * SPAN, 128), bf16),
            struct((GROUP, 2 * SPAN, 128), bf16),
        ],
        after=after,
        name="attend_back",
    )(offsets, place, da_own, da_other, wo_full, q, kv_all, o, lse, cos, sin)


def out_grads_kernel(a0, a1, a2, a3, o0_ref, o1_ref, out_ref):
    heads = jnp.concatenate(
        [jnp.concatenate([ref[i] for i in range(4)], axis=1) for ref in (o0_ref, o1_ref)],
        axis=0,
    )
    rows = jnp.concatenate([ref[...] for ref in (a0, a1, a2, a3)], axis=0)
    out_ref[...] = dot_tn(rows, heads).astype(bf16)


def out_grads(da_parts, o_parts, after=()):
    return kernel_call(
        out_grads_kernel,
        grid=(4,),
        in_specs=[pl.BlockSpec((SPAN, 512), lambda i: (0, i))] * 4
        + [whole_spec((4, 2 * SPAN, 128))] * 2,
        out_specs=pl.BlockSpec((512, 512), lambda i: (i, 0)),
        out_shape=struct((D, 512), bf16),
        after=after,
        name="out_grads",
    )(*da_parts, *o_parts)


def right_kernel(place_ref, dkv_ref, cos_ref, sin_ref, out_ref):
    lane = lax.broadcasted_iota(jnp.int32, (SPAN, 128), 1)
    total = jnp.sum(dkv_ref[...].astype(f32), axis=0)
    turned = total * cos_ref[...] - partner(total) * sin_ref[...]
    out_ref[...] = jnp.where(lane < HEAD_DIM, turned, total).astype(bf16)


def right_side(k, place, dkv, cos, sin, after=()):
    return kernel_call(
        right_kernel,
        prefetch=1,
        grid=(2,),
        in_specs=[
            pl.BlockSpec((GROUP, SPAN, 128), lambda i, *_: (0, i, 0)),
            turn_spec(k),
            turn_spec(k),
        ],
        out_specs=pl.BlockSpec((SPAN, 128), lambda i, *_: (i, 0)),
        out_shape=struct((2 * SPAN, 128), bf16),
        after=after,
        name="right_side",
    )(place, dkv, cos, sin)


def query_grads_kernel(place_ref, h0_ref, h1_ref, q0_ref, q1_ref, *outs):
    rights = [jnp.concatenate([ref[i] for i in range(4)], axis=1) for ref in (q0_ref, q1_ref)]
    for step in range(4):
        for z in range(4):
            owner = z * 4 + (place_ref[0] + step) % 4
            rows = pl.ds(pl.multiple_of(owner * 128, 128), 128)
            total = dot_nn(h0_ref[rows, :], rights[0]) + dot_nn(h1_ref[rows, :], rights[1])
            outs[step][z] = total.astype(bf16)


def query_grads(place, h_turned, dqs, after=()):
    args = (*h_turned, *dqs)
    shape = (4, 128, 512)
    return kernel_call(
        query_grads_kernel,
        prefetch=1,
        grid=(1,),
        in_specs=[whole_spec(arg.shape) for arg in args],
        out_specs=[whole_spec(shape)] * 4,
        out_shape=[struct(shape, bf16)] * 4,
        after=after,
        name="query_grads",
    )(place, *args)


def line_sum_kernel(place_ref, e0, e1, e2, e3, *outs):
    for step in range(4):
        z = (place_ref[0] // 4 + step) % 4
        outs[step][...] = sum(ref[z].astype(f32) for ref in (e0, e1, e2, e3)).astype(bf16)


def line_sums(place, terms, after=()):
    shape = terms[0].shape[1:]
    return kernel_call(
        line_sum_kernel,
        prefetch=1,
        grid=(1,),
        in_specs=[whole_spec(term.shape) for term in terms],
        out_specs=[whole_spec(shape)] * 4,
        out_shape=[struct(shape, bf16)] * 4,
        after=after,
        name="line_sums",
    )(place, *terms)


def final_sums_kernel(e0, e1, e2, e3, out_ref, kv_ref, sum_ref):
    sum_ref[:, :512] = sum_rows((e0, e1, e2, e3)).astype(bf16)
    sum_ref[:, 512:1024] = out_ref[...]
    sum_ref[:, 1024:] = jnp.sum(kv_ref[...].astype(f32), axis=0).astype(bf16)


def final_sums(q_terms, out_own, kv_terms, after=()):
    args = (*q_terms, out_own, kv_terms)
    return kernel_call(
        final_sums_kernel,
        grid=(1,),
        in_specs=[whole_spec(arg.shape) for arg in args],
        out_specs=whole_spec((128, 1152)),
        out_shape=struct((128, 1152), bf16),
        after=after,
        name="final_sums",
    )(*args)


def torus_shift(dz, dx):
    return [
        (z * 4 + x, ((z + dz) % 4) * 4 + (x + dx) % 4) for z in range(4) for x in range(4)
    ]


def along_x(values, step):
    return lax.ppermute(values, "grp", torus_shift(0, step))


def along_z(values, step):
    return lax.ppermute(values, "grp", torus_shift(step, 0))


def keyval_grads_kernel(
    place_ref, h0_ref, h1_ref, r0_ref, dkv_ref, cos_ref, sin_ref, out_ref, right_ref
):
    lane = lax.broadcasted_iota(jnp.int32, (SPAN, 128), 1)
    for i in range(2):
        rows = slice(i * SPAN, (i + 1) * SPAN)
        total = jnp.sum(dkv_ref[:, rows, :].astype(f32), axis=0)
        turned = total * cos_ref[rows, :] - partner(total) * sin_ref[rows, :]
        right_ref[rows, :] = jnp.where(lane < HEAD_DIM, turned, total).astype(bf16)
    total = dot_nn(h0_ref[...], r0_ref[...]) + dot_nn(h1_ref[...], right_ref[...])
    out_ref[...] = total.reshape(out_ref.shape)


def keyval_grads(place, h_turned, first_right, dkv, cos, sin, after=()):
    turn = pl.BlockSpec((2 * SPAN, 128), lambda i, place: (half_of(place, 1), 0))
    args = (*h_turned, first_right, dkv)
    return kernel_call(
        keyval_grads_kernel,
        prefetch=1,
        grid=(1,),
        in_specs=[whole_spec(arg.shape) for arg in args] + [turn, turn],
        out_specs=[whole_spec((GROUP, 128, 128)), whole_spec((2 * SPAN, 128))],
        out_shape=[struct((GROUP, 128, 128), f32), struct((2 * SPAN, 128), bf16)],
        after=after,
        name="keyval_grads",
    )(place, *args, cos, sin)


def project_back_kernel(q0_ref, q1_ref, r0_ref, r1_ref, wq_ref, wkv_ref, own_out, other_out):
    wq = wq_ref[...]
    wkv = wkv_ref[...].reshape(512, 128)
    for k, (q_ref, r_ref) in enumerate(((q0_ref, r0_ref), (q1_ref, r1_ref))):
        right = jnp.concatenate([q_ref[i] for i in range(4)], axis=1)
        d_h = (dot_nt(right, wq) + dot_nt(r_ref[...], wkv)).astype(bf16)
        spot = slice(k * SPAN, (k + 1) * SPAN)
        own_out[spot, :] = d_h[:SPAN]
        other_out[spot, :] = d_h[SPAN:]


def project_back(dqs, rights, wide_full, kv_full, after=()):
    args = (*dqs, *rights)
    out = pl.BlockSpec((2 * SPAN, 512), lambda i: (0, i))
    return kernel_call(
        project_back_kernel,
        grid=(4,),
        in_specs=[whole_spec(arg.shape) for arg in args]
        + [
            pl.BlockSpec((512, 512), lambda i: (i, 0)),
            pl.BlockSpec((4, 128, 128), lambda i: (i, 0, 0)),
        ],
        out_specs=[out, out],
        out_shape=[struct((2 * SPAN, D), bf16)] * 2,
        after=after,
        name="project_back",
    )(*args, wide_full, kv_full)


def as_rows(columns):
    return columns.T[:8, :]


def first_gain_kernel(wide_ref, kv_ref, own_ref, rep_ref, two_ref, two_rep, out_ref):
    grad = own_ref[...].astype(f32) + rep_ref[...].astype(f32)
    one = jnp.sum(wide_ref[...].astype(f32) * grad[:, :512], axis=1, keepdims=True)
    one = one + jnp.sum(kv_ref[...].astype(f32) * grad[:, 1024:], axis=1, keepdims=True)
    lane = lax.broadcasted_iota(jnp.int32, (128, 128), 1)
    out_ref[...] = as_rows(jnp.where(lane == 0, one, two_ref[...] + two_rep[...]))


def gain_terms(wide_pack, kv_pack, sums, seconds):
    wide = pl.BlockSpec((128, 512), lambda i: (0, 0))
    args = (kv_pack, *sums, *seconds)
    return kernel_call(
        first_gain_kernel,
        grid=(1,),
        in_specs=[wide] + [whole_spec(arg.shape) for arg in args],
        out_specs=whole_spec((8, 128)),
        out_shape=struct((8, 128), f32),
        name="gain_terms",
    )(wide_pack, *args)


def second_gain_kernel(pack_ref, sum_ref, out_ref):
    total = jnp.zeros((pack_ref.shape[0], 1), f32)
    for column in range(0, WIDTH, 3 * TILE):
        span = slice(column, column + 2 * TILE)
        products = pack_ref[:, span].astype(f32) * sum_ref[:, span].astype(f32)
        total += jnp.sum(products, axis=1, keepdims=True)
    out_ref[...] = jnp.broadcast_to(total, out_ref.shape)


def second_gain_terms(mlp_pack, mlp_sum, after=()):
    return kernel_call(
        second_gain_kernel,
        grid=(1,),
        in_specs=[whole_spec(mlp_pack.shape), whole_spec(mlp_sum.shape)],
        out_specs=whole_spec((128, 128)),
        out_shape=struct((128, 128), f32),
        after=after,
        name="second_gain_terms",
    )(mlp_pack, mlp_sum)


def gain_adam_kernel(own, core, tp, both, w, m, s, w_o, m_o, s_o):
    total = (own[...] + core[...]) + (tp[...] + both[...])
    grad = total[:2, :] / w[...].astype(bf16).astype(f32)
    w_o[...], m_o[...], s_o[...] = adamw(w[...], m[...], s[...], grad, 1.0, 0.0)


def gain_adam(terms, states):
    args = (*terms, *[state.T for state in states])
    shape = args[-1].shape
    new = kernel_call(
        gain_adam_kernel,
        grid=(1,),
        in_specs=[whole_spec(arg.shape) for arg in args],
        out_specs=[whole_spec(shape)] * 3,
        out_shape=[struct(shape, f32)] * 3,
        name="gain_adam",
    )(*args)
    return [value.T for value in new]


def flat_view(values):
    rows, kinds, units = values.shape
    tiles = values.reshape(rows, kinds, units // SMALL, SMALL)
    tiles = with_layout_constraint(tiles, Layout(major_to_minor=(0, 2, 1, 3)))
    return tiles.transpose(0, 2, 1, 3).reshape(-1, SMALL)


def deep_view(values, shape):
    rows, kinds, units = shape
    tiles = values.reshape(rows, units // SMALL, kinds, SMALL).transpose(0, 2, 1, 3)
    tiles = with_layout_constraint(tiles, Layout(major_to_minor=(0, 2, 1, 3)))
    return tiles.reshape(shape)


def pack_kernel(quarter_ref, gu_ref, d_ref, out_ref):
    quarter = quarter_ref[0]
    start = window_start(quarter)
    stride = gu_ref.shape[0] // PACK_ROWS
    for tile in range(WINDOW_TILES):
        keep = jnp.where((quarter >= 2) & (tile == 0), 0.0, 1.0)
        for kind in range(3):
            if kind == 2:
                span = pl.ds(pl.multiple_of((start + tile) * SMALL, SMALL), SMALL)
                value = d_ref[:, span]
            else:
                value = gu_ref[pl.ds(2 * (start + tile) + kind, PACK_ROWS, stride), :]
            column = packed_column(tile, kind)
            out_ref[:, column : column + SMALL] = (value * keep).astype(bf16)


def pack_mlp(quarter, w_gateup, w_down, after=()):
    rows, units = w_down.shape
    per_row = 2 * units // SMALL
    return kernel_call(
        pack_kernel,
        prefetch=1,
        grid=(rows // PACK_ROWS,),
        in_specs=[
            pl.BlockSpec((PACK_ROWS * per_row, SMALL), lambda i, quarter: (i, 0)),
            pl.BlockSpec((PACK_ROWS, units), lambda i, quarter: (i, 0)),
        ],
        out_specs=pl.BlockSpec((PACK_ROWS, WIDTH), lambda i, quarter: (i, 0)),
        out_shape=struct((rows, WIDTH), bf16),
        after=after,
        name="pack_mlp",
    )(quarter, flat_view(w_gateup), w_down)


def mlp_adam_kernel(
    quarter_ref, own_ref, replica_ref, core_ref, both_ref, wg, mg, sg, wd, md, sd,
    wg_o, mg_o, sg_o, wd_o, md_o, sd_o, grads, *, rate_wide, rate_down,
):
    stride = wg.shape[0] // PACK_ROWS
    for part in range(4):
        same_core = quarter_ref[0] // 2 == part // 2
        same_replica = quarter_ref[0] % 2 == part % 2
        for tile in range(FIRST_OWN[part], FIRST_OWN[part + 1]):

            def grad(kind):
                column = packed_column(tile - WINDOW_STARTS[part], kind)
                spot = slice(column, column + SMALL)
                near = jnp.where(same_replica, own_ref[:, spot], replica_ref[:, spot])
                far = jnp.where(same_replica, core_ref[:, spot], both_ref[:, spot])
                return jnp.where(same_core, near, far).astype(f32)

            for kind in range(2):
                grads[pl.ds(2 * tile + kind, PACK_ROWS, stride), :] = grad(kind)
            span = slice(tile * SMALL, (tile + 1) * SMALL)
            wd_o[:, span], md_o[:, span], sd_o[:, span] = adamw(
                wd[:, span], md[:, span], sd[:, span], grad(2), rate_down, decay_rate
            )
    wg_o[...], mg_o[...], sg_o[...] = adamw(
        wg[...], mg[...], sg[...], grads[...], rate_wide, decay_rate
    )


def mlp_adam(quarter, sums, gateup, down, rate_wide, rate_down, after=()):
    rows, units = down[0].shape
    per_row = 2 * units // SMALL
    wide = pl.BlockSpec((PACK_ROWS * per_row, SMALL), lambda i, quarter: (i, 0))
    flat = pl.BlockSpec((PACK_ROWS, units), lambda i, quarter: (i, 0))
    grad = pl.BlockSpec((PACK_ROWS, WIDTH), lambda i, quarter: (i, 0))
    new = kernel_call(
        functools.partial(mlp_adam_kernel, rate_wide=rate_wide, rate_down=rate_down),
        prefetch=1,
        grid=(rows // PACK_ROWS,),
        in_specs=[grad] * 4 + [wide] * 3 + [flat] * 3,
        out_specs=[wide] * 3 + [flat] * 3,
        out_shape=[struct((rows * per_row, SMALL), f32)] * 3
        + [struct(down[0].shape, f32)] * 3,
        scratch_shapes=[pltpu.VMEM((PACK_ROWS * per_row, SMALL), f32)],
        after=after,
        name="mlp_adam",
    )(quarter, *sums, *[flat_view(state) for state in gateup], *down)
    return [deep_view(value, gateup[0].shape) for value in new[:3]] + list(new[3:])


def attn_adam_kernel(
    core_ref, own_ref, rep_ref, other_ref, both_ref, wq, mq, sq, wo, mo, so, wkv, mkv, skv,
    wq_o, mq_o, sq_o, wo_o, mo_o, so_o, wkv_o, mkv_o, skv_o, *, rate_wide, rate_out,
):
    mine = core_ref[0] == 0

    def halves(span):
        own = own_ref[:, span].astype(f32) + rep_ref[:, span].astype(f32)
        other = other_ref[:, span].astype(f32) + both_ref[:, span].astype(f32)
        return jnp.where(mine, own, other), jnp.where(mine, other, own)

    for i, grad in enumerate(halves(slice(0, 512))):
        span = slice(512 * i, 512 * (i + 1))
        wq_o[:, span], mq_o[:, span], sq_o[:, span] = adamw(
            wq[:, span], mq[:, span], sq[:, span], grad, rate_wide, decay_rate
        )
    for i, grad in enumerate(halves(slice(512, 1024))):
        span = slice(512 * i, 512 * (i + 1))
        wo_o[:, span], mo_o[:, span], so_o[:, span] = adamw(
            wo[:, span], mo[:, span], so[:, span], grad, rate_out, decay_rate
        )
    first, second = halves(slice(1024, 1152))
    low_half = lax.broadcasted_iota(jnp.int32, first.shape, 1) < HEAD_DIM
    grads = (
        jnp.where(low_half, first, pltpu.roll(second, HEAD_DIM, 1)),
        jnp.where(low_half, pltpu.roll(first, HEAD_DIM, 1), second),
    )
    for i, grad in enumerate(grads):
        wkv_o[:, i, :], mkv_o[:, i, :], skv_o[:, i, :] = adamw(
            wkv[:, i, :], mkv[:, i, :], skv[:, i, :], grad, rate_wide, decay_rate
        )


def attn_adam(core, sums, query, out, keyval, rate_wide, rate_out, after=()):
    rows = 32
    grad = pl.BlockSpec((rows, sums[0].shape[1]), lambda i, core: (i, 0))
    flat = pl.BlockSpec((rows, query[0].shape[1]), lambda i, core: (i, 0))
    deep = pl.BlockSpec((rows, *keyval[0].shape[1:]), lambda i, core: (i, 0, 0))
    new = kernel_call(
        functools.partial(attn_adam_kernel, rate_wide=rate_wide, rate_out=rate_out),
        prefetch=1,
        grid=(query[0].shape[0] // rows,),
        in_specs=[grad] * 4 + [flat] * 6 + [deep] * 3,
        out_specs=[flat] * 6 + [deep] * 3,
        out_shape=[struct(state.shape, f32) for state in (*query, *out, *keyval)],
        after=after,
        name="attn_adam",
    )(core, *sums, *query, *out, *keyval)
    return new[:3], new[3:6], new[6:]


def swap_core(values):
    return lax.ppermute(values, "rep", CORE_SWAP)


def swap_replica(values):
    return lax.ppermute(values, "rep", REPLICA_SWAP)


def swap_replica_core(values):
    return lax.ppermute(values, "rep", BOTH_CORES_SWAP)


def swap_tp(values):
    return lax.ppermute(values, "tp", TP_SWAP)


def swap_core_tp(values):
    return lax.ppermute(values, ("rep", "tp"), CORE_TP_SWAP)


def swap_both(values):
    return lax.ppermute(values, ("rep", "tp"), BOTH_SWAP)


def scatter_sums(parts, after=()):
    pairs = []
    for k in range(2):
        own, core, replica, both = parts[4 * k : 4 * k + 4]
        pairs += [(own, swap_core(core)), (replica, swap_core(both))]
    mine, replica, tp, both = add_quads(pairs, after=after)
    return mine, swap_replica(replica), swap_tp(tp), swap_both(both)


def spread(values):
    return lax.all_to_all(values, "grp", 0, 0, tiled=False)


def on_device(
    tokens,
    cotangent,
    offsets,
    w_query,
    moment_query,
    square_query,
    w_keyval,
    moment_keyval,
    square_keyval,
    w_out,
    moment_out,
    square_out,
    w_gateup,
    moment_gateup,
    square_gateup,
    w_down,
    moment_down,
    square_down,
    norm_gains,
    moment_gains,
    square_gains,
):
    sequences, own_len, width = tokens.shape
    core = lax.axis_index("rep") % 2
    core_list = core.reshape(1).astype(jnp.int32)
    place = jnp.stack([lax.axis_index("grp"), lax.axis_index("tp")]).astype(jnp.int32)

    wide_pack, kv_pack, kv_copies = pack_attn(
        core_list, w_query, w_out, w_keyval, norm_gains.T
    )
    wide_full = lax.all_gather(wide_pack, "grp", axis=0, tiled=True)
    kv_full = spread(kv_copies)
    quarter = (2 * core + lax.axis_index("rep") // 2).reshape(1).astype(jnp.int32)
    x_other = swap_core(tokens)
    dy_replica = swap_replica(cotangent)
    dy_parts = (cotangent, swap_core(cotangent), dy_replica, swap_replica_core(cotangent))
    offsets_other = swap_core(offsets)
    offsets_all = jnp.stack([offsets, offsets_other], axis=1).reshape(2 * sequences, GROUP)
    steps_in = jnp.arange(own_len, dtype=jnp.int32)
    starts = lax.dynamic_slice_in_dim(offsets_all, place[0], 1, 1)
    positions = (starts + steps_in[None, :]).reshape(2 * sequences * own_len)
    half_dim = HEAD_DIM // 2
    inverse = rope_base ** (-2.0 * jnp.arange(half_dim, dtype=f32) / HEAD_DIM)
    angles = positions.astype(f32)[:, None] * inverse[None, :]
    cos_part = jnp.cos(angles)
    sin_part = jnp.sin(angles)
    cos = jnp.concatenate([cos_part] * 4, axis=1)
    sin = jnp.concatenate([-sin_part, sin_part] * 2, axis=1)

    kv_one = project_kv(1, place, tokens, x_other, kv_full, cos, sin)
    kv_zero = project_kv(
        0, place, tokens, x_other, kv_full, cos, sin, after=(kv_one[0], dy_replica)
    )
    h_turned = [kv_zero[1], kv_one[1]]
    kvs = {1: spread(kv_one[2])}
    kvs[0] = spread(kv_zero[2])
    dy_t = transposed(place, dy_parts, after=(kv_zero[0],))
    mlp_pack = pack_mlp(quarter, w_gateup, w_down, after=(kvs[1], dy_t))
    mlp_full = lax.all_gather(mlp_pack, "grp", axis=0, tiled=True)
    q_one = project_q(1, place, kv_one[0], wide_full, cos, sin, after=(mlp_pack,))
    one = attend(1, offsets_all, place, q_one, kvs[1], wide_full)
    one_share = add_low(one[2], swap_core(one[3]))
    q_zero = project_q(0, place, kv_zero[0], wide_full, cos, sin, after=(one[0],))
    qs = [q_zero, q_one]
    received = swap_tp(one_share)
    zero = attend(0, offsets_all, place, qs[0], kvs[0], wide_full, after=(one_share,))
    os_ = [zero[0], one[0]]
    lses = [zero[1], one[1]]
    zero_part = add_low(zero[2], received)
    mid, h_two = middle(place, tokens, zero_part, swap_core(zero[3]), kv_full)
    h_parts = []
    for first, second in ((h_two, swap_replica(h_two)), (swap_tp(h_two), swap_both(h_two))):
        h_parts += [first, swap_core(first), second, swap_core(second)]
    side, mlp_sums = mlp(place, h_parts, dy_parts, dy_t, mlp_full)
    mlp_own = lax.psum_scatter(mlp_sums, "grp", scatter_dimension=0, tiled=True)

    sums = scatter_sums(mlp_back(side, mlp_full, 0, 2))
    out_parts = mlp_back(side, mlp_full, 2, 1, after=(sums[0],))
    da = middle_back(place, sums, mid, cotangent, kv_full, after=(out_parts[0],))
    da_core = swap_core(da)
    da_parts = [da, da_core, swap_tp(da), swap_tp(da_core)]

    def back_of(k, after=()):
        return attend_back(
            k, offsets_all, place, da_parts[2 * k], da_parts[2 * k + 1], wide_full, qs[k], kvs[k],
            os_[k], lses[k], cos, sin, after=after,
        )

    first_back = back_of(0)
    out_shares = scatter_sums(out_parts, after=(first_back[0],))
    out_sums = out_grads(da_parts, os_, after=(out_shares[0],))
    out_own = lax.psum_scatter(out_sums, "grp", scatter_dimension=0, tiled=True)
    second_back = back_of(1, after=(out_sums,))
    dqs = [first_back[0], second_back[0]]
    mlp_replica = swap_replica(mlp_own)
    first_right = right_side(0, place, spread(first_back[1]), cos, sin, after=(second_back[0],))
    q_sums = query_grads(place, h_turned, dqs, after=(first_right,))
    rate_wide = 2.0 * D ** (-0.5)
    rate_out = 2.0 * max(1, 2 * D // LENGTH) ** (-0.5)
    rate_down = 2.0 * FF ** (-0.5)
    new_mlp = mlp_adam(
        quarter,
        (mlp_own, mlp_replica, swap_core(mlp_own), swap_replica_core(mlp_own)),
        (w_gateup, moment_gateup, square_gateup),
        (w_down, moment_down, square_down),
        rate_wide,
        rate_down,
        after=(q_sums[0],),
    )
    layer_mine = layer_part(mid, out_shares, after=(new_mlp[-1],))
    x_terms = [q_sums[0]] + [along_x(q_sums[i], i) for i in range(1, 4)]
    kv_sums, second_right = keyval_grads(
        place, h_turned, first_right, spread(second_back[1]), cos, sin, after=(layer_mine,)
    )
    q_lines = line_sums(place, x_terms, after=(kv_sums,))
    rights = [first_right, second_right]
    own_part, other_part = project_back(
        dqs, rights, wide_full, kv_full, after=(q_lines[0],)
    )
    dh_share = add_low(own_part, swap_core(other_part))
    dh_received = swap_tp(dh_share)
    gain_two = second_gain_terms(mlp_pack, mlp_own, after=(dh_share,))
    z_terms = [q_lines[0]] + [along_z(q_lines[i], i) for i in range(1, 4)]
    own = final_sums(z_terms, out_own, spread(kv_sums), after=(gain_two,))

    replica = swap_replica(own)
    gain_own = gain_terms(
        wide_pack, kv_pack, (own, replica), (gain_two, swap_replica(gain_two))
    )
    new_query, new_out, new_keyval = attn_adam(
        core_list,
        (own, replica, swap_core(own), swap_replica_core(own)),
        (w_query, moment_query, square_query),
        (w_out, moment_out, square_out),
        (w_keyval, moment_keyval, square_keyval),
        rate_wide,
        rate_out,
        after=(gain_own,),
    )
    input_grad, layer_out = row_outputs(
        place, layer_mine, swap_tp(layer_mine), (da, da_parts[2]), dh_share, dh_received, tokens, kv_full, after=(new_out[0],)
    )
    new_gains = gain_adam(
        (gain_own, swap_core(gain_own), swap_tp(gain_own), swap_core_tp(gain_own)),
        (norm_gains, moment_gains, square_gains),
    )
    return (
        layer_out,
        input_grad,
        *new_query,
        *new_keyval,
        *new_out,
        *new_mlp,
        *new_gains,
    )


def solution(mesh):
    rows = P("rep", "grp", None)
    flat = P("grp", "tp")
    deep = P("grp", None, "tp")
    states = (flat,) * 3 + (deep,) * 3 + (flat,) * 3 + (deep,) * 3 + (flat,) * 3
    states += (P("grp", None),) * 3
    return jax.shard_map(
        on_device,
        mesh=mesh,
        in_specs=(rows, rows, P("rep", None)) + states,
        out_specs=(rows, rows) + states,
        check_vma=False,
    )
```

```python
import functools

import jax
import jax.numpy as jnp
from jax import lax
from jax.experimental import pallas as pl
from jax.experimental.layout import Layout, with_layout_constraint
from jax.experimental.pallas import tpu as pltpu
from jax.sharding import PartitionSpec as P

D = 2048
HEAD_DIM = 64
FF = 5632
LENGTH = 2048
STEP = 10
GROUP = 16
SPAN = 128
TILE = 256

norm_epsilon = 1e-05
rope_base = 10000.0
neg_large = -1e30
beta_first = 0.9
beta_second = 0.95
adam_epsilon = 1e-08
decay_rate = 0.1

bf16 = jnp.bfloat16
f32 = jnp.float32

VMEM_LIMIT = 63 * 1024 * 1024

CORE_SWAP = [(0, 1), (1, 0), (2, 3), (3, 2)]
REPLICA_SWAP = [(0, 2), (1, 3), (2, 0), (3, 1)]
BOTH_CORES_SWAP = [(0, 3), (1, 2), (2, 1), (3, 0)]
TP_SWAP = [(0, 1), (1, 0)]
CORE_TP_SWAP = [(2 * r + t, 2 * (r ^ 1) + (1 - t)) for r in range(4) for t in range(2)]
BOTH_SWAP = [(2 * r + t, 2 * (r ^ 2) + (1 - t)) for r in range(4) for t in range(2)]


def struct(shape, dtype):
    return jax.ShapeDtypeStruct(shape, dtype)


def kernel_call(
    kernel, *, name, out_shape, grid=(), in_specs=None, out_specs=None, scratch_shapes=(), prefetch=0,
    after=(),
):
    first = prefetch + len(in_specs)

    def body(*refs):
        kernel(*refs[:first], *refs[first + len(after) :])

    grid_spec = pltpu.PrefetchScalarGridSpec(
        num_scalar_prefetch=prefetch,
        grid=grid,
        in_specs=list(in_specs) + [pl.BlockSpec(memory_space=pl.ANY)] * len(after),
        out_specs=out_specs,
        scratch_shapes=list(scratch_shapes),
    )
    call = pl.pallas_call(
        body,
        grid_spec=grid_spec,
        out_shape=out_shape,
        compiler_params=pltpu.CompilerParams(vmem_limit_bytes=VMEM_LIMIT),
        name=name,
    )
    return lambda *args: call(*args, *after)


def dot_nn(left, right):
    return lax.dot_general(left, right, (((1,), (0,)), ((), ())), preferred_element_type=f32)


def dot_nt(left, right):
    return lax.dot_general(left, right, (((1,), (1,)), ((), ())), preferred_element_type=f32)


def dot_tn(left, right):
    return lax.dot_general(left, right, (((0,), (0,)), ((), ())), preferred_element_type=f32)


def adamw(weight, moment, square, grad, rate, decay):
    moment = beta_first * moment + (1.0 - beta_first) * grad
    square = beta_second * square + (1.0 - beta_second) * grad * grad
    fix_first = 1.0 - beta_first**STEP
    fix_second = 1.0 - beta_second**STEP
    update = moment / fix_first / (jnp.sqrt(square / fix_second) + adam_epsilon)
    return (weight * (1.0 - rate * decay) - rate * update, moment, square)


def norm_back(upstream, gain, normed, scale):
    weighted = upstream * gain
    return scale * (weighted - normed * jnp.mean(weighted * normed, axis=-1, keepdims=True))


def partner(values):
    lane = lax.broadcasted_iota(jnp.int32, values.shape, 1)
    up = pltpu.roll(values, 96, 1)
    down = pltpu.roll(values, 32, 1)
    return jnp.where(lane % HEAD_DIM < HEAD_DIM // 2, up, down)


def row_of(block):
    return jnp.concatenate([block[i : i + 1, :] for i in range(GROUP)], axis=1)


def rms_scale(values):
    return lax.rsqrt(jnp.mean(values * values, axis=-1, keepdims=True) + norm_epsilon)


def gain_row(gain_ref, index):
    return row_of(gain_ref[:, index, :].astype(f32))


GAIN_SPEC = pl.BlockSpec((GROUP, 16, 128), lambda *_: (0, 8, 0))
WQ_SPEC = pl.BlockSpec((D, 512), lambda *_: (0, 0))
WO_SPEC = pl.BlockSpec((D, 512), lambda *_: (0, 1))
WKV_SPEC = pl.BlockSpec((GROUP, 128, 128), lambda *_: (0, 0, 0))
ROWS_SPEC = pl.BlockSpec((SPAN, D), lambda *_: (0, 0))


def half_of(place, k):
    return place[1] if k == 0 else 1 - place[1]


STRIP = 128
STRIP_SPEC = pl.BlockSpec((STRIP, D), lambda i, *_: (i, 0))
HALF_SPEC = pl.BlockSpec((SPAN // 2, D), lambda i, *_: (i, 0))


def seq_strip(k):
    return pl.BlockSpec((1, STRIP, D), lambda i, *refs: (half_of(refs[-1], k), i, 0))


def seq_spec(k):
    return pl.BlockSpec((1, SPAN, D), lambda *ids: (half_of(ids[-1], k), 0, 0))


def turn_spec(k):
    return pl.BlockSpec((SPAN, 128), lambda i, *refs: (2 * half_of(refs[-1], k) + i, 0))


def whole_spec(shape):
    return pl.BlockSpec(shape, lambda *_: (0,) * len(shape))


def pack_attn_kernel(core_ref, wq_ref, wo_ref, wkv_ref, gain_ref, wide_ref, kv_ref, copies_ref):
    lane = lax.broadcasted_iota(jnp.int32, (128, 128), 1)
    low_half = lane < HEAD_DIM
    first_core = core_ref[0] == 0
    key = jnp.where(first_core, wkv_ref[:, 0, :], pltpu.roll(wkv_ref[:, 0, :], HEAD_DIM, 1))
    value = jnp.where(first_core, pltpu.roll(wkv_ref[:, 1, :], HEAD_DIM, 1), wkv_ref[:, 1, :])
    kv = jnp.where(low_half, key, value).astype(bf16)
    wide_ref[:, :512] = wq_ref[...].astype(bf16)
    wide_ref[:, 512:] = wo_ref[...].astype(bf16)
    kv_ref[...] = kv
    gains = jnp.concatenate([gain_ref[...], jnp.zeros((14, 128), f32)], axis=0).astype(bf16)
    for g in range(GROUP):
        copies_ref[g, :128, :] = kv
        copies_ref[g, 128:, :] = gains


def pack_attn(core, w_query, w_out, w_keyval, gains):
    rows = w_query.shape[0]
    half = pl.BlockSpec((rows, 512), lambda i, core: (0, core[0]))
    shapes = [(rows, 1024), (rows, 128), (GROUP, rows + 16, 128)]
    return kernel_call(
        pack_attn_kernel,
        prefetch=1,
        grid=(1,),
        in_specs=[half, half, whole_spec(w_keyval.shape), whole_spec(gains.shape)],
        out_specs=[whole_spec(shape) for shape in shapes],
        out_shape=[struct(shape, bf16) for shape in shapes],
        name="pack_attn",
    )(core, w_query, w_out, w_keyval, gains)


def project_kv_kernel(
    place_ref, own_ref, other_ref, wkv_ref, gain_ref, cos_ref, sin_ref, h_ref, turned_ref, kv_ref
):
    mine = pl.program_id(0) == 0
    x = jnp.where(mine, own_ref[0].astype(f32), other_ref[0].astype(f32))
    h = (x * rms_scale(x) * gain_row(gain_ref, 0)).astype(bf16)
    h_ref[...] = h
    low_half = lax.broadcasted_iota(jnp.int32, (SPAN, 128), 1) < HEAD_DIM
    keyval = dot_nn(h, wkv_ref[...].reshape(D, 128))
    turned = keyval * cos_ref[...] + partner(keyval) * sin_ref[...]
    kv = jnp.where(low_half, turned, keyval).astype(bf16)
    kv_ref[...] = jnp.broadcast_to(kv[None], (GROUP, SPAN, 128))
    turned_ref[...] = h.T


def project_kv(k, place, x_own, x_other, kv_full, cos, sin, after=()):
    return kernel_call(
        project_kv_kernel,
        prefetch=1,
        grid=(2,),
        in_specs=[seq_spec(k), seq_spec(k), WKV_SPEC, GAIN_SPEC, turn_spec(k), turn_spec(k)],
        out_specs=[
            pl.BlockSpec((SPAN, D), lambda i, *_: (i, 0)),
            pl.BlockSpec((D, SPAN), lambda i, *_: (0, i)),
            pl.BlockSpec((GROUP, SPAN, 128), lambda i, *_: (0, i, 0)),
        ],
        out_shape=[
            struct((2 * SPAN, D), bf16),
            struct((D, 2 * SPAN), bf16),
            struct((GROUP, 2 * SPAN, 128), bf16),
        ],
        after=after,
        name="project_kv",
    )(place, x_own, x_other, kv_full, kv_full, cos, sin)


def project_q_kernel(place_ref, h_ref, wq_ref, cos_ref, sin_ref, q_ref):
    cos = cos_ref[...]
    sin = sin_ref[...]
    low_half = lax.broadcasted_iota(jnp.int32, cos.shape, 1) < HEAD_DIM
    query = dot_nn(h_ref[...], wq_ref[...])
    for pair in range(4):
        block = query[:, pair * 128 : (pair + 1) * 128]
        turned = (block * cos + partner(block) * sin) * (HEAD_DIM**-0.5)
        q_ref[2 * pair] = jnp.where(low_half, turned, 0.0).astype(bf16)
        q_ref[2 * pair + 1] = jnp.where(
            low_half, pltpu.roll(turned, HEAD_DIM, 1), 0.0
        ).astype(bf16)


def project_q(k, place, h, wide_full, cos, sin, after=()):
    turn = pl.BlockSpec((2 * SPAN, 128), lambda i, place: (half_of(place, k), 0))
    return kernel_call(
        project_q_kernel,
        prefetch=1,
        grid=(1,),
        in_specs=[whole_spec((2 * SPAN, D)), WQ_SPEC, turn, turn],
        out_specs=whole_spec((8, 2 * SPAN, 128)),
        out_shape=struct((8, 2 * SPAN, 128), bf16),
        after=after,
        name="project_q",
    )(place, h, wide_full, cos, sin)


CHUNK = 512
BACK_CHUNK = 1024


def causal_offsets():
    key = lax.broadcasted_iota(jnp.int32, (128, 256), 0)
    query = lax.broadcasted_iota(jnp.int32, (128, 256), 1) % SPAN
    return key - query


def masked(raw, differ, own, off_ref, seq, c):
    parts = []
    blocks = raw.shape[0] // 128
    for j in range(blocks):
        allowed = differ <= own - off_ref[seq, blocks * c + j]
        parts.append(jnp.where(allowed, raw[j * 128 : (j + 1) * 128], neg_large))
    return jnp.concatenate(parts, axis=0)


def attend_kernel(
    off_ref, place_ref, q_ref, kv_ref, wo_ref, o_ref, lse_ref, own_ref, other_ref, kvt, scores, *, k
):
    step = pl.program_id(0)
    seq = 2 * half_of(place_ref, k) + step
    kvt[...] = kv_ref[...].reshape(LENGTH, 128).T
    own = off_ref[seq, place_ref[0]]
    differ = causal_offsets()
    blocks = CHUNK // 128

    for pair in range(4):
        q = q_ref[2 * pair : 2 * pair + 2].reshape(256, 128)
        top = jnp.full((1, 256), neg_large, f32)
        for c in range(LENGTH // CHUNK):
            raw = dot_nt(kv_ref[blocks * c : blocks * (c + 1)].reshape(CHUNK, 128), q)
            score = masked(raw, differ, own, off_ref, seq, c)
            scores[pair % 2, c * CHUNK : (c + 1) * CHUNK, :] = score
            top = jnp.maximum(top, jnp.max(score, axis=0, keepdims=True))
        total = jnp.zeros((1, 256), f32)
        mixed = jnp.zeros((128, 256), f32)
        for c in range(LENGTH // CHUNK):
            weight = jnp.exp(scores[pair % 2, c * CHUNK : (c + 1) * CHUNK, :] - top)
            total = total + jnp.sum(weight, axis=0, keepdims=True)
            mixed = mixed + dot_nn(kvt[:, c * CHUNK : (c + 1) * CHUNK], weight.astype(bf16))
        out = (mixed[HEAD_DIM:, :] / total).T
        o_ref[pair] = jnp.concatenate([out[:SPAN], out[SPAN:]], axis=1).astype(bf16)
        lse_ref[0, pair : pair + 1, :] = top + jnp.log(total)

    heads = jnp.concatenate([o_ref[i] for i in range(4)], axis=1)
    part = dot_nt(heads, wo_ref[...]).astype(bf16)

    @pl.when(step == 0)
    def _():
        own_ref[...] = part

    @pl.when(step == 1)
    def _():
        other_ref[...] = part


def attend(k, offsets, place, q, kv_all, wo_full, after=()):
    grid_spec = dict(
        prefetch=2,
        grid=(2,),
        in_specs=[
            pl.BlockSpec((8, SPAN, 128), lambda i, *_: (0, i, 0)),
            pl.BlockSpec((GROUP, SPAN, 128), lambda i, *_: (0, i, 0)),
            WO_SPEC,
        ],
        out_specs=[
            pl.BlockSpec((4, SPAN, 128), lambda i, *_: (0, i, 0)),
            pl.BlockSpec((1, 4, 256), lambda i, *_: (i, 0, 0)),
            ROWS_SPEC,
            ROWS_SPEC,
        ],
        scratch_shapes=[pltpu.VMEM((128, LENGTH), bf16), pltpu.VMEM((2, LENGTH, 256), f32)],
    )
    return kernel_call(
        functools.partial(attend_kernel, k=k),
        **grid_spec,
        out_shape=[
            struct((4, 2 * SPAN, 128), bf16),
            struct((2, 4, 256), f32),
            struct((SPAN, D), bf16),
            struct((SPAN, D), bf16),
        ],
        after=after,
        name="attend",
    )(offsets, place, q, kv_all, wo_full)


def share_kernel(own_ref, other_ref, out_ref):
    out_ref[...] = (own_ref[...].astype(f32) + other_ref[...].astype(f32)).astype(bf16)


def add_low(first, second, after=()):
    rows, width = first.shape
    block = pl.BlockSpec((128, width), lambda i: (i, 0))
    return kernel_call(
        share_kernel,
        grid=(rows // 128,),
        in_specs=[block, block],
        out_specs=block,
        out_shape=struct(first.shape, bf16),
        after=after,
        name="add_low",
    )(first, second)


def middle_kernel(place_ref, x_ref, one_ref, two_ref, gain_ref, mid_ref, h_ref):
    total = one_ref[...].astype(f32) + two_ref[...].astype(f32)
    mid = x_ref[0].astype(f32) + total
    mid_ref[...] = mid
    h_ref[...] = (mid * rms_scale(mid) * gain_row(gain_ref, 1)).astype(bf16)


def middle(place, x_own, one, two, attn_full):
    return kernel_call(
        middle_kernel,
        prefetch=1,
        grid=(SPAN // STRIP,),
        in_specs=[seq_strip(0), STRIP_SPEC, STRIP_SPEC, GAIN_SPEC],
        out_specs=[STRIP_SPEC, STRIP_SPEC],
        out_shape=[struct((SPAN, D), f32), struct((SPAN, D), bf16)],
        name="middle",
    )(place, x_own, one, two, attn_full)


def sum_rows(refs):
    return sum(ref[...].astype(f32) for ref in refs)


def middle_back_kernel(place_ref, p0, p1, p2, p3, mid_ref, dy_ref, gain_ref, da_ref):
    upstream = sum_rows((p0, p1, p2, p3))
    mid = mid_ref[...]
    scale = rms_scale(mid)
    d_norm = norm_back(upstream, gain_row(gain_ref, 1), mid * scale, scale)
    da_ref[...] = (dy_ref[0].astype(f32) + d_norm).astype(bf16)


def middle_back(place, parts, mid, dy_own, attn_full, after=()):
    return kernel_call(
        middle_back_kernel,
        prefetch=1,
        grid=(SPAN // STRIP,),
        in_specs=[STRIP_SPEC] * 5 + [seq_strip(0), GAIN_SPEC],
        out_specs=STRIP_SPEC,
        out_shape=struct((SPAN, D), bf16),
        after=after,
        name="middle_back",
    )(place, *parts, mid, dy_own, attn_full)


def layer_part_kernel(mid_ref, p0, p1, p2, p3, out_ref):
    out_ref[...] = (mid_ref[...] + sum_rows((p0, p1, p2, p3))).astype(bf16)


def layer_part(mid, parts, after=()):
    return kernel_call(
        layer_part_kernel,
        grid=(SPAN // STRIP,),
        in_specs=[STRIP_SPEC] * 5,
        out_specs=STRIP_SPEC,
        out_shape=struct((SPAN, D), bf16),
        after=after,
        name="layer_part",
    )(mid, *parts)


def row_outputs_kernel(
    place_ref, mine_ref, other_ref, da0, da1, s0, s1, r0, r1, x_ref, gain_ref, out_ref, layer_ref
):
    layer_ref[half_of(place_ref, 0)] = mine_ref[...]
    layer_ref[half_of(place_ref, 1)] = other_ref[...]
    gain = gain_row(gain_ref, 0)
    for k, (da_ref, share, received) in enumerate(((da0, s0, r1), (da1, s1, r0))):
        upstream = share[...].astype(f32) + received[...].astype(f32)
        m = half_of(place_ref, k)
        x = x_ref[m].astype(f32)
        scale = rms_scale(x)
        out_ref[m] = da_ref[...].astype(f32) + norm_back(upstream, gain, x * scale, scale)


def row_outputs(place, mine, other, das, share, received, x_own, kv_full, after=()):
    steps = 2
    rows = SPAN // steps
    block = pl.BlockSpec((rows, D), lambda i, *_: (i, 0))
    second = pl.BlockSpec((rows, D), lambda i, *_: (steps + i, 0))
    seqs = pl.BlockSpec((2, rows, D), lambda i, *_: (0, i, 0))
    return kernel_call(
        row_outputs_kernel,
        prefetch=1,
        grid=(steps,),
        in_specs=[block] * 5 + [second, block, second, seqs, GAIN_SPEC],
        out_specs=[seqs, seqs],
        out_shape=[struct((2, SPAN, D), f32), struct((2, SPAN, D), bf16)],
        after=after,
        name="row_outputs",
    )(place, mine, other, *das, share, share, received, received, x_own, kv_full)


PACK_ROWS = 16
ALL_ROWS = 8 * SPAN
SMALL = 128
WINDOW_TILES = 6
WIDTH = 3 * WINDOW_TILES * SMALL
WINDOW_STARTS = (0, 6, 11, 16)
FIRST_OWN = (0, 6, 12, 17, 22)


def window_start(quarter):
    return jnp.where(quarter < 2, 6 * quarter, 5 * quarter + 1)


def packed_column(tile, kind):
    return 3 * TILE * (tile // 2) + TILE * kind + SMALL * (tile % 2)


def transpose_kernel(place_ref, *refs):
    parts, out_ref = refs[:-1], refs[-1]
    for k in range(2):
        for i, ref in enumerate(parts):
            start = (len(parts) * k + i) * SPAN
            out_ref[:, start : start + SPAN] = ref[half_of(place_ref, k)].T


def transposed(place, parts, after=()):
    seqs = pl.BlockSpec((2, SPAN, 512), lambda i, *_: (0, 0, i))
    return kernel_call(
        transpose_kernel,
        prefetch=1,
        grid=(D // 512,),
        in_specs=[seqs] * 4,
        out_specs=pl.BlockSpec((512, ALL_ROWS), lambda i, *_: (i, 0)),
        out_shape=struct((D, ALL_ROWS), bf16),
        after=after,
        name="transposed",
    )(place, *parts)


def mlp_kernel(place_ref, *refs):
    h_parts, dy_parts, dyt_ref, w_ref = refs[:8], refs[8:12], refs[12], refs[13]
    side_ref, sum_ref, h, ht, dy, dyt, sems = refs[14:]
    step = pl.program_id(0)

    def part_copies():
        copies = []
        for i, ref in enumerate(h_parts):
            spot = h.at[i * SPAN : (i + 1) * SPAN]
            copies.append(pltpu.make_async_copy(ref, spot, sems.at[i]))
        for k in range(2):
            for i, ref in enumerate(dy_parts):
                number = 4 * k + i
                spot = dy.at[number * SPAN : (number + 1) * SPAN]
                source = ref.at[half_of(place_ref, k)]
                copies.append(pltpu.make_async_copy(source, spot, sems.at[8 + number]))
        return copies

    turned_copy = pltpu.make_async_copy(dyt_ref, dyt, sems.at[16])

    def work(start):
        rows = slice(start, start + 256)
        both = dot_nn(h[rows, :], w_ref[:, : 2 * TILE])
        upstream = dot_nn(dy[rows, :], w_ref[:, 2 * TILE :])
        gate = both[:, :TILE]
        up = both[:, TILE:]
        sigmoid = jax.nn.sigmoid(gate)
        active = gate * sigmoid
        side_ref[rows, :TILE] = (
            upstream * up * (sigmoid * (1.0 + gate * (1.0 - sigmoid)))
        ).astype(bf16)
        side_ref[rows, TILE : 2 * TILE] = (upstream * active).astype(bf16)
        side_ref[rows, 2 * TILE :] = (active * up).astype(bf16)

    @pl.when(step == 0)
    def _():
        copies = part_copies()
        for i in range(8):
            copies[i].start()
            copies[8 + i].start()
        turned_copy.start()
        for start in range(0, ALL_ROWS, 256):
            for i in range(start // SPAN, start // SPAN + 2):
                copies[i].wait()
                copies[8 + i].wait()
            work(start)
        ht[...] = h[...].T
        turned_copy.wait()

    @pl.when(step > 0)
    def _():
        for start in range(0, ALL_ROWS, 256):
            work(start)

    sum_ref[:, : 2 * TILE] = dot_nn(ht[...], side_ref[:, : 2 * TILE]).astype(bf16)
    sum_ref[:, 2 * TILE :] = dot_nn(dyt[...], side_ref[:, 2 * TILE :]).astype(bf16)


def mlp(place, h_parts, dy_parts, dy_t, w_full, after=()):
    width = 3 * TILE
    return kernel_call(
        mlp_kernel,
        prefetch=1,
        grid=(WIDTH // width,),
        in_specs=[pl.BlockSpec(memory_space=pl.ANY)] * 13
        + [pl.BlockSpec((D, width), lambda i, *_: (0, i))],
        out_specs=[
            pl.BlockSpec((ALL_ROWS, width), lambda i, *_: (0, i)),
            pl.BlockSpec((D, width), lambda i, *_: (0, i)),
        ],
        out_shape=[struct((ALL_ROWS, WIDTH), bf16), struct((D, WIDTH), bf16)],
        scratch_shapes=[
            pltpu.VMEM((ALL_ROWS, D), bf16),
            pltpu.VMEM((D, ALL_ROWS), bf16),
            pltpu.VMEM((ALL_ROWS, D), bf16),
            pltpu.VMEM((D, ALL_ROWS), bf16),
            pltpu.SemaphoreType.DMA((17,)),
        ],
        after=after,
        name="mlp",
    )(place, *h_parts, *dy_parts, dy_t, w_full)


def mlp_back_kernel(side_ref, w_ref, *outs, first, count):
    total = jnp.zeros((ALL_ROWS, w_ref.shape[0]), f32)
    for column in range(0, WIDTH, 3 * TILE):
        span = slice(column + first * TILE, column + (first + count) * TILE)
        total = total + dot_nt(side_ref[:, span], w_ref[:, span])
    for out, i in zip(outs, range(8)):
        out[...] = total[i * SPAN : (i + 1) * SPAN].astype(bf16)


def mlp_back(side, w_full, first, count, after=()):
    return kernel_call(
        functools.partial(mlp_back_kernel, first=first, count=count),
        grid=(D // 512,),
        in_specs=[whole_spec((ALL_ROWS, WIDTH)), pl.BlockSpec((512, WIDTH), lambda i: (i, 0))],
        out_specs=[pl.BlockSpec((SPAN, 512), lambda i: (0, i))] * 8,
        out_shape=[struct((SPAN, D), bf16)] * 8,
        after=after,
        name="mlp_back",
    )(side, w_full)


def quad_kernel(*refs):
    count = (len(refs) + 4) // 2
    inputs, outs = refs[:count], refs[count:]
    for i in range(4):
        total = inputs[2 * i][...].astype(f32) + inputs[2 * i + 1][...].astype(f32)
        outs[i][...] = total.astype(bf16)
    for source, target in zip(inputs[8:], outs[4:]):
        target[...] = source[...]


def add_quads(pairs, held=(), after=()):
    count = len(held)
    return kernel_call(
        quad_kernel,
        grid=(2,),
        in_specs=[HALF_SPEC] * (8 + count),
        out_specs=[HALF_SPEC] * (4 + count),
        out_shape=[struct((SPAN, D), bf16)] * (4 + count),
        after=after,
        name="add_quads",
    )(*[value for pair in pairs for value in pair], *held)


def attend_back_kernel(
    off_ref, place_ref, own_ref, other_ref, wo_ref, q_ref, kv_ref, o_ref, lse_ref, cos_ref,
    sin_ref, dq_ref, dkv_ref, kvt, d_heads, dkv, *, k,
):
    step = pl.program_id(0)
    seq = 2 * half_of(place_ref, k) + step
    kvt[...] = kv_ref[...].reshape(LENGTH, 128).T
    dkv[...] = jnp.zeros_like(dkv)
    d_out_rows = jnp.where(step == 0, own_ref[...].astype(f32), other_ref[...].astype(f32))
    d_all = dot_nn(d_out_rows.astype(bf16), wo_ref[...])
    for pair in range(4):
        d_heads[pair] = d_all[:, pair * 128 : (pair + 1) * 128].astype(bf16).astype(f32)
    own = off_ref[seq, place_ref[0]]
    differ = causal_offsets()
    lane = lax.broadcasted_iota(jnp.int32, (SPAN, 128), 1)
    high_half = lane >= HEAD_DIM
    cos = cos_ref[...]
    sin = sin_ref[...]
    blocks = BACK_CHUNK // 128

    for pair in range(4):
        q = q_ref[2 * pair : 2 * pair + 2].reshape(256, 128)
        d_out = d_heads[pair]
        first = jnp.where(high_half, pltpu.roll(d_out, HEAD_DIM, 1), 0.0).astype(bf16)
        second = jnp.where(high_half, d_out, 0.0).astype(bf16)
        d_o = jnp.concatenate([first, second], axis=0)
        dots = (d_out * o_ref[pair].astype(f32)).T
        inner = jnp.concatenate(
            [
                jnp.sum(dots[:HEAD_DIM], axis=0, keepdims=True),
                jnp.sum(dots[HEAD_DIM:], axis=0, keepdims=True),
            ],
            axis=1,
        )
        lse = lse_ref[0, pair : pair + 1, :]
        d_query = jnp.zeros((128, 256), f32)
        for c in range(LENGTH // BACK_CHUNK):
            kv = kv_ref[blocks * c : blocks * (c + 1)].reshape(BACK_CHUNK, 128)
            score = masked(dot_nt(kv, q), differ, own, off_ref, seq, c)
            prob = jnp.exp(score - lse)
            d_prob = dot_nt(kv, d_o)
            d_score = (prob * (d_prob - inner)).astype(bf16)
            span = slice(c * BACK_CHUNK, (c + 1) * BACK_CHUNK)
            dkv[span, :] += dot_nn(d_score, q) + dot_nn(prob.astype(bf16), d_o)
            d_query = d_query + dot_nn(kvt[:, span], d_score)
        turned = d_query[:HEAD_DIM, :].T
        block = jnp.concatenate([turned[:SPAN], turned[SPAN:]], axis=1)
        block = (block * cos - partner(block) * sin) * (HEAD_DIM**-0.5)
        dq_ref[pair] = block.astype(bf16)

    dkv_ref[...] = dkv[...].astype(bf16).reshape(GROUP, SPAN, 128)


def attend_back(k, offsets, place, da_own, da_other, wo_full, q, kv_all, o, lse, cos, sin, after=()):
    turn = turn_spec(k)
    heads = pl.BlockSpec((4, SPAN, 128), lambda i, *_: (0, i, 0))
    group = pl.BlockSpec((GROUP, SPAN, 128), lambda i, *_: (0, i, 0))
    grid_spec = dict(
        prefetch=2,
        grid=(2,),
        in_specs=[
            ROWS_SPEC,
            ROWS_SPEC,
            WO_SPEC,
            pl.BlockSpec((8, SPAN, 128), lambda i, *_: (0, i, 0)),
            group,
            heads,
            pl.BlockSpec((1, 4, 256), lambda i, *_: (i, 0, 0)),
            turn,
            turn,
        ],
        out_specs=[heads, group],
        scratch_shapes=[
            pltpu.VMEM((128, LENGTH), bf16),
            pltpu.VMEM((4, SPAN, 128), f32),
            pltpu.VMEM((LENGTH, 128), f32),
        ],
    )
    return kernel_call(
        functools.partial(attend_back_kernel, k=k),
        **grid_spec,
        out_shape=[
            struct((4, 2 * SPAN, 128), bf16),
            struct((GROUP, 2 * SPAN, 128), bf16),
        ],
        after=after,
        name="attend_back",
    )(offsets, place, da_own, da_other, wo_full, q, kv_all, o, lse, cos, sin)


def out_grads_kernel(a0, a1, a2, a3, o0_ref, o1_ref, out_ref):
    heads = jnp.concatenate(
        [jnp.concatenate([ref[i] for i in range(4)], axis=1) for ref in (o0_ref, o1_ref)],
        axis=0,
    )
    rows = jnp.concatenate([ref[...] for ref in (a0, a1, a2, a3)], axis=0)
    out_ref[...] = dot_tn(rows, heads).astype(bf16)


def out_grads(da_parts, o_parts, after=()):
    return kernel_call(
        out_grads_kernel,
        grid=(4,),
        in_specs=[pl.BlockSpec((SPAN, 512), lambda i: (0, i))] * 4
        + [whole_spec((4, 2 * SPAN, 128))] * 2,
        out_specs=pl.BlockSpec((512, 512), lambda i: (i, 0)),
        out_shape=struct((D, 512), bf16),
        after=after,
        name="out_grads",
    )(*da_parts, *o_parts)


def right_kernel(place_ref, dkv_ref, cos_ref, sin_ref, out_ref):
    lane = lax.broadcasted_iota(jnp.int32, (SPAN, 128), 1)
    total = jnp.sum(dkv_ref[...].astype(f32), axis=0)
    turned = total * cos_ref[...] - partner(total) * sin_ref[...]
    out_ref[...] = jnp.where(lane < HEAD_DIM, turned, total).astype(bf16)


def right_side(k, place, dkv, cos, sin, after=()):
    return kernel_call(
        right_kernel,
        prefetch=1,
        grid=(2,),
        in_specs=[
            pl.BlockSpec((GROUP, SPAN, 128), lambda i, *_: (0, i, 0)),
            turn_spec(k),
            turn_spec(k),
        ],
        out_specs=pl.BlockSpec((SPAN, 128), lambda i, *_: (i, 0)),
        out_shape=struct((2 * SPAN, 128), bf16),
        after=after,
        name="right_side",
    )(place, dkv, cos, sin)


def query_grads_kernel(place_ref, h0_ref, h1_ref, q0_ref, q1_ref, *outs):
    rights = [jnp.concatenate([ref[i] for i in range(4)], axis=1) for ref in (q0_ref, q1_ref)]
    for step in range(4):
        for z in range(4):
            owner = z * 4 + (place_ref[0] + step) % 4
            rows = pl.ds(pl.multiple_of(owner * 128, 128), 128)
            total = dot_nn(h0_ref[rows, :], rights[0]) + dot_nn(h1_ref[rows, :], rights[1])
            outs[step][z] = total.astype(bf16)


def query_grads(place, h_turned, dqs, after=()):
    args = (*h_turned, *dqs)
    shape = (4, 128, 512)
    return kernel_call(
        query_grads_kernel,
        prefetch=1,
        grid=(1,),
        in_specs=[whole_spec(arg.shape) for arg in args],
        out_specs=[whole_spec(shape)] * 4,
        out_shape=[struct(shape, bf16)] * 4,
        after=after,
        name="query_grads",
    )(place, *args)


def line_sum_kernel(place_ref, e0, e1, e2, e3, *outs):
    for step in range(4):
        z = (place_ref[0] // 4 + step) % 4
        outs[step][...] = sum(ref[z].astype(f32) for ref in (e0, e1, e2, e3)).astype(bf16)


def line_sums(place, terms, after=()):
    shape = terms[0].shape[1:]
    return kernel_call(
        line_sum_kernel,
        prefetch=1,
        grid=(1,),
        in_specs=[whole_spec(term.shape) for term in terms],
        out_specs=[whole_spec(shape)] * 4,
        out_shape=[struct(shape, bf16)] * 4,
        after=after,
        name="line_sums",
    )(place, *terms)


def final_sums_kernel(e0, e1, e2, e3, out_ref, kv_ref, sum_ref):
    sum_ref[:, :512] = sum_rows((e0, e1, e2, e3)).astype(bf16)
    sum_ref[:, 512:1024] = out_ref[...]
    sum_ref[:, 1024:] = jnp.sum(kv_ref[...].astype(f32), axis=0).astype(bf16)


def final_sums(q_terms, out_own, kv_terms, after=()):
    args = (*q_terms, out_own, kv_terms)
    return kernel_call(
        final_sums_kernel,
        grid=(1,),
        in_specs=[whole_spec(arg.shape) for arg in args],
        out_specs=whole_spec((128, 1152)),
        out_shape=struct((128, 1152), bf16),
        after=after,
        name="final_sums",
    )(*args)


def torus_shift(dz, dx):
    return [
        (z * 4 + x, ((z + dz) % 4) * 4 + (x + dx) % 4) for z in range(4) for x in range(4)
    ]


def along_x(values, step):
    return lax.ppermute(values, "grp", torus_shift(0, step))


def along_z(values, step):
    return lax.ppermute(values, "grp", torus_shift(step, 0))


def keyval_grads_kernel(
    place_ref, h0_ref, h1_ref, r0_ref, dkv_ref, cos_ref, sin_ref, out_ref, right_ref
):
    lane = lax.broadcasted_iota(jnp.int32, (SPAN, 128), 1)
    for i in range(2):
        rows = slice(i * SPAN, (i + 1) * SPAN)
        total = jnp.sum(dkv_ref[:, rows, :].astype(f32), axis=0)
        turned = total * cos_ref[rows, :] - partner(total) * sin_ref[rows, :]
        right_ref[rows, :] = jnp.where(lane < HEAD_DIM, turned, total).astype(bf16)
    total = dot_nn(h0_ref[...], r0_ref[...]) + dot_nn(h1_ref[...], right_ref[...])
    out_ref[...] = total.reshape(out_ref.shape)


def keyval_grads(place, h_turned, first_right, dkv, cos, sin, after=()):
    turn = pl.BlockSpec((2 * SPAN, 128), lambda i, place: (half_of(place, 1), 0))
    args = (*h_turned, first_right, dkv)
    return kernel_call(
        keyval_grads_kernel,
        prefetch=1,
        grid=(1,),
        in_specs=[whole_spec(arg.shape) for arg in args] + [turn, turn],
        out_specs=[whole_spec((GROUP, 128, 128)), whole_spec((2 * SPAN, 128))],
        out_shape=[struct((GROUP, 128, 128), f32), struct((2 * SPAN, 128), bf16)],
        after=after,
        name="keyval_grads",
    )(place, *args, cos, sin)


def project_back_kernel(q0_ref, q1_ref, r0_ref, r1_ref, wq_ref, wkv_ref, own_out, other_out):
    wq = wq_ref[...]
    wkv = wkv_ref[...].reshape(512, 128)
    for k, (q_ref, r_ref) in enumerate(((q0_ref, r0_ref), (q1_ref, r1_ref))):
        right = jnp.concatenate([q_ref[i] for i in range(4)], axis=1)
        d_h = (dot_nt(right, wq) + dot_nt(r_ref[...], wkv)).astype(bf16)
        spot = slice(k * SPAN, (k + 1) * SPAN)
        own_out[spot, :] = d_h[:SPAN]
        other_out[spot, :] = d_h[SPAN:]


def project_back(dqs, rights, wide_full, kv_full, after=()):
    args = (*dqs, *rights)
    out = pl.BlockSpec((2 * SPAN, 512), lambda i: (0, i))
    return kernel_call(
        project_back_kernel,
        grid=(4,),
        in_specs=[whole_spec(arg.shape) for arg in args]
        + [
            pl.BlockSpec((512, 512), lambda i: (i, 0)),
            pl.BlockSpec((4, 128, 128), lambda i: (i, 0, 0)),
        ],
        out_specs=[out, out],
        out_shape=[struct((2 * SPAN, D), bf16)] * 2,
        after=after,
        name="project_back",
    )(*args, wide_full, kv_full)


def as_rows(columns):
    return columns.T[:8, :]


def first_gain_kernel(wide_ref, kv_ref, own_ref, rep_ref, two_ref, two_rep, out_ref):
    grad = own_ref[...].astype(f32) + rep_ref[...].astype(f32)
    one = jnp.sum(wide_ref[...].astype(f32) * grad[:, :512], axis=1, keepdims=True)
    one = one + jnp.sum(kv_ref[...].astype(f32) * grad[:, 1024:], axis=1, keepdims=True)
    lane = lax.broadcasted_iota(jnp.int32, (128, 128), 1)
    out_ref[...] = as_rows(jnp.where(lane == 0, one, two_ref[...] + two_rep[...]))


def gain_terms(wide_pack, kv_pack, sums, seconds):
    wide = pl.BlockSpec((128, 512), lambda i: (0, 0))
    args = (kv_pack, *sums, *seconds)
    return kernel_call(
        first_gain_kernel,
        grid=(1,),
        in_specs=[wide] + [whole_spec(arg.shape) for arg in args],
        out_specs=whole_spec((8, 128)),
        out_shape=struct((8, 128), f32),
        name="gain_terms",
    )(wide_pack, *args)


def second_gain_kernel(pack_ref, sum_ref, held_ref, out_ref, copy_ref):
    total = jnp.zeros((pack_ref.shape[0], 1), f32)
    for column in range(0, WIDTH, 3 * TILE):
        span = slice(column, column + 2 * TILE)
        products = pack_ref[:, span].astype(f32) * sum_ref[:, span].astype(f32)
        total += jnp.sum(products, axis=1, keepdims=True)
    out_ref[...] = jnp.broadcast_to(total, out_ref.shape)
    copy_ref[...] = held_ref[...]


def second_gain_terms(mlp_pack, mlp_sum, held, after=()):
    args = (mlp_pack, mlp_sum, held)
    return kernel_call(
        second_gain_kernel,
        grid=(1,),
        in_specs=[whole_spec(arg.shape) for arg in args],
        out_specs=[whole_spec((128, 128)), whole_spec(held.shape)],
        out_shape=[struct((128, 128), f32), struct(held.shape, held.dtype)],
        after=after,
        name="second_gain_terms",
    )(*args)


def gain_adam_kernel(own, core, tp, both, w, m, s, w_o, m_o, s_o):
    total = (own[...] + core[...]) + (tp[...] + both[...])
    grad = total[:2, :] / w[...].astype(bf16).astype(f32)
    w_o[...], m_o[...], s_o[...] = adamw(w[...], m[...], s[...], grad, 1.0, 0.0)


def gain_adam(terms, states):
    args = (*terms, *[state.T for state in states])
    shape = args[-1].shape
    new = kernel_call(
        gain_adam_kernel,
        grid=(1,),
        in_specs=[whole_spec(arg.shape) for arg in args],
        out_specs=[whole_spec(shape)] * 3,
        out_shape=[struct(shape, f32)] * 3,
        name="gain_adam",
    )(*args)
    return [value.T for value in new]


def flat_view(values):
    rows, kinds, units = values.shape
    tiles = values.reshape(rows, kinds, units // SMALL, SMALL)
    tiles = with_layout_constraint(tiles, Layout(major_to_minor=(0, 2, 1, 3)))
    return tiles.transpose(0, 2, 1, 3).reshape(-1, SMALL)


def deep_view(values, shape):
    rows, kinds, units = shape
    tiles = values.reshape(rows, units // SMALL, kinds, SMALL).transpose(0, 2, 1, 3)
    tiles = with_layout_constraint(tiles, Layout(major_to_minor=(0, 2, 1, 3)))
    return tiles.reshape(shape)


def pack_kernel(quarter_ref, gu_ref, d_ref, out_ref):
    quarter = quarter_ref[0]
    start = window_start(quarter)
    stride = gu_ref.shape[0] // PACK_ROWS
    for tile in range(WINDOW_TILES):
        keep = jnp.where((quarter >= 2) & (tile == 0), 0.0, 1.0)
        for kind in range(3):
            if kind == 2:
                span = pl.ds(pl.multiple_of((start + tile) * SMALL, SMALL), SMALL)
                value = d_ref[:, span]
            else:
                value = gu_ref[pl.ds(2 * (start + tile) + kind, PACK_ROWS, stride), :]
            column = packed_column(tile, kind)
            out_ref[:, column : column + SMALL] = (value * keep).astype(bf16)


def pack_mlp(quarter, w_gateup, w_down, after=()):
    rows, units = w_down.shape
    per_row = 2 * units // SMALL
    return kernel_call(
        pack_kernel,
        prefetch=1,
        grid=(rows // PACK_ROWS,),
        in_specs=[
            pl.BlockSpec((PACK_ROWS * per_row, SMALL), lambda i, quarter: (i, 0)),
            pl.BlockSpec((PACK_ROWS, units), lambda i, quarter: (i, 0)),
        ],
        out_specs=pl.BlockSpec((PACK_ROWS, WIDTH), lambda i, quarter: (i, 0)),
        out_shape=struct((rows, WIDTH), bf16),
        after=after,
        name="pack_mlp",
    )(quarter, flat_view(w_gateup), w_down)


def mlp_adam_kernel(
    quarter_ref, own_ref, replica_ref, core_ref, both_ref, wg, mg, sg, wd, md, sd,
    wg_o, mg_o, sg_o, wd_o, md_o, sd_o, grads, *, rate_wide, rate_down,
):
    stride = wg.shape[0] // PACK_ROWS
    for part in range(4):
        same_core = quarter_ref[0] // 2 == part // 2
        same_replica = quarter_ref[0] % 2 == part % 2
        for tile in range(FIRST_OWN[part], FIRST_OWN[part + 1]):

            def grad(kind):
                column = packed_column(tile - WINDOW_STARTS[part], kind)
                spot = slice(column, column + SMALL)
                near = jnp.where(same_replica, own_ref[:, spot], replica_ref[:, spot])
                far = jnp.where(same_replica, core_ref[:, spot], both_ref[:, spot])
                return jnp.where(same_core, near, far).astype(f32)

            for kind in range(2):
                grads[pl.ds(2 * tile + kind, PACK_ROWS, stride), :] = grad(kind)
            span = slice(tile * SMALL, (tile + 1) * SMALL)
            wd_o[:, span], md_o[:, span], sd_o[:, span] = adamw(
                wd[:, span], md[:, span], sd[:, span], grad(2), rate_down, decay_rate
            )
    wg_o[...], mg_o[...], sg_o[...] = adamw(
        wg[...], mg[...], sg[...], grads[...], rate_wide, decay_rate
    )


def mlp_adam(quarter, sums, gateup, down, rate_wide, rate_down, after=()):
    rows, units = down[0].shape
    per_row = 2 * units // SMALL
    wide = pl.BlockSpec((PACK_ROWS * per_row, SMALL), lambda i, quarter: (i, 0))
    flat = pl.BlockSpec((PACK_ROWS, units), lambda i, quarter: (i, 0))
    grad = pl.BlockSpec((PACK_ROWS, WIDTH), lambda i, quarter: (i, 0))
    new = kernel_call(
        functools.partial(mlp_adam_kernel, rate_wide=rate_wide, rate_down=rate_down),
        prefetch=1,
        grid=(rows // PACK_ROWS,),
        in_specs=[grad] * 4 + [wide] * 3 + [flat] * 3,
        out_specs=[wide] * 3 + [flat] * 3,
        out_shape=[struct((rows * per_row, SMALL), f32)] * 3
        + [struct(down[0].shape, f32)] * 3,
        scratch_shapes=[pltpu.VMEM((PACK_ROWS * per_row, SMALL), f32)],
        after=after,
        name="mlp_adam",
    )(quarter, *sums, *[flat_view(state) for state in gateup], *down)
    return [deep_view(value, gateup[0].shape) for value in new[:3]] + list(new[3:])


def attn_adam_kernel(
    core_ref, own_ref, rep_ref, other_ref, both_ref, wq, mq, sq, wo, mo, so, wkv, mkv, skv,
    wq_o, mq_o, sq_o, wo_o, mo_o, so_o, wkv_o, mkv_o, skv_o, *, rate_wide, rate_out,
):
    mine = core_ref[0] == 0

    def halves(span):
        own = own_ref[:, span].astype(f32) + rep_ref[:, span].astype(f32)
        other = other_ref[:, span].astype(f32) + both_ref[:, span].astype(f32)
        return jnp.where(mine, own, other), jnp.where(mine, other, own)

    for i, grad in enumerate(halves(slice(0, 512))):
        span = slice(512 * i, 512 * (i + 1))
        wq_o[:, span], mq_o[:, span], sq_o[:, span] = adamw(
            wq[:, span], mq[:, span], sq[:, span], grad, rate_wide, decay_rate
        )
    for i, grad in enumerate(halves(slice(512, 1024))):
        span = slice(512 * i, 512 * (i + 1))
        wo_o[:, span], mo_o[:, span], so_o[:, span] = adamw(
            wo[:, span], mo[:, span], so[:, span], grad, rate_out, decay_rate
        )
    first, second = halves(slice(1024, 1152))
    low_half = lax.broadcasted_iota(jnp.int32, first.shape, 1) < HEAD_DIM
    grads = (
        jnp.where(low_half, first, pltpu.roll(second, HEAD_DIM, 1)),
        jnp.where(low_half, pltpu.roll(first, HEAD_DIM, 1), second),
    )
    for i, grad in enumerate(grads):
        wkv_o[:, i, :], mkv_o[:, i, :], skv_o[:, i, :] = adamw(
            wkv[:, i, :], mkv[:, i, :], skv[:, i, :], grad, rate_wide, decay_rate
        )


def attn_adam(core, sums, query, out, keyval, rate_wide, rate_out, after=()):
    rows = 32
    grad = pl.BlockSpec((rows, sums[0].shape[1]), lambda i, core: (i, 0))
    flat = pl.BlockSpec((rows, query[0].shape[1]), lambda i, core: (i, 0))
    deep = pl.BlockSpec((rows, *keyval[0].shape[1:]), lambda i, core: (i, 0, 0))
    new = kernel_call(
        functools.partial(attn_adam_kernel, rate_wide=rate_wide, rate_out=rate_out),
        prefetch=1,
        grid=(query[0].shape[0] // rows,),
        in_specs=[grad] * 4 + [flat] * 6 + [deep] * 3,
        out_specs=[flat] * 6 + [deep] * 3,
        out_shape=[struct(state.shape, f32) for state in (*query, *out, *keyval)],
        after=after,
        name="attn_adam",
    )(core, *sums, *query, *out, *keyval)
    return new[:3], new[3:6], new[6:]


def swap_core(values):
    return lax.ppermute(values, "rep", CORE_SWAP)


def swap_replica(values):
    return lax.ppermute(values, "rep", REPLICA_SWAP)


def swap_replica_core(values):
    return lax.ppermute(values, "rep", BOTH_CORES_SWAP)


def swap_tp(values):
    return lax.ppermute(values, "tp", TP_SWAP)


def swap_core_tp(values):
    return lax.ppermute(values, ("rep", "tp"), CORE_TP_SWAP)


def swap_both(values):
    return lax.ppermute(values, ("rep", "tp"), BOTH_SWAP)


def scatter_sums(parts, held=(), after=()):
    pairs = []
    for k in range(2):
        own, core, replica, both = parts[4 * k : 4 * k + 4]
        pairs += [(own, swap_core(core)), (replica, swap_core(both))]
    mine, replica, tp, both, *copies = add_quads(pairs, held=held, after=after)
    return mine, swap_replica(replica), swap_tp(tp), swap_both(both), *copies


def spread(values):
    return lax.all_to_all(values, "grp", 0, 0, tiled=False)


def on_device(
    tokens,
    cotangent,
    offsets,
    w_query,
    moment_query,
    square_query,
    w_keyval,
    moment_keyval,
    square_keyval,
    w_out,
    moment_out,
    square_out,
    w_gateup,
    moment_gateup,
    square_gateup,
    w_down,
    moment_down,
    square_down,
    norm_gains,
    moment_gains,
    square_gains,
):
    sequences, own_len, width = tokens.shape
    core = lax.axis_index("rep") % 2
    core_list = core.reshape(1).astype(jnp.int32)
    place = jnp.stack([lax.axis_index("grp"), lax.axis_index("tp")]).astype(jnp.int32)

    wide_pack, kv_pack, kv_copies = pack_attn(
        core_list, w_query, w_out, w_keyval, norm_gains.T
    )
    wide_full = lax.all_gather(wide_pack, "grp", axis=0, tiled=True)
    kv_full = spread(kv_copies)
    quarter = (2 * core + lax.axis_index("rep") // 2).reshape(1).astype(jnp.int32)
    x_other = swap_core(tokens)
    dy_replica = swap_replica(cotangent)
    dy_parts = (cotangent, swap_core(cotangent), dy_replica, swap_replica_core(cotangent))
    offsets_other = swap_core(offsets)
    offsets_all = jnp.stack([offsets, offsets_other], axis=1).reshape(2 * sequences, GROUP)
    steps_in = jnp.arange(own_len, dtype=jnp.int32)
    starts = lax.dynamic_slice_in_dim(offsets_all, place[0], 1, 1)
    positions = (starts + steps_in[None, :]).reshape(2 * sequences * own_len)
    half_dim = HEAD_DIM // 2
    inverse = rope_base ** (-2.0 * jnp.arange(half_dim, dtype=f32) / HEAD_DIM)
    angles = positions.astype(f32)[:, None] * inverse[None, :]
    cos_part = jnp.cos(angles)
    sin_part = jnp.sin(angles)
    cos = jnp.concatenate([cos_part] * 4, axis=1)
    sin = jnp.concatenate([-sin_part, sin_part] * 2, axis=1)

    kv_one = project_kv(1, place, tokens, x_other, kv_full, cos, sin)
    kv_zero = project_kv(
        0, place, tokens, x_other, kv_full, cos, sin, after=(kv_one[0], dy_replica)
    )
    h_turned = [kv_zero[1], kv_one[1]]
    kvs = {1: spread(kv_one[2])}
    kvs[0] = spread(kv_zero[2])
    dy_t = transposed(place, dy_parts, after=(kv_zero[0],))
    mlp_pack = pack_mlp(quarter, w_gateup, w_down, after=(kvs[1], dy_t))
    mlp_full = lax.all_gather(mlp_pack, "grp", axis=0, tiled=True)
    q_one = project_q(1, place, kv_one[0], wide_full, cos, sin, after=(mlp_pack,))
    one = attend(1, offsets_all, place, q_one, kvs[1], wide_full)
    one_share = add_low(one[2], swap_core(one[3]))
    q_zero = project_q(0, place, kv_zero[0], wide_full, cos, sin, after=(one[0],))
    qs = [q_zero, q_one]
    received = swap_tp(one_share)
    zero = attend(0, offsets_all, place, qs[0], kvs[0], wide_full, after=(one_share,))
    os_ = [zero[0], one[0]]
    lses = [zero[1], one[1]]
    zero_part = add_low(zero[2], received)
    mid, h_two = middle(place, tokens, zero_part, swap_core(zero[3]), kv_full)
    h_parts = []
    for first, second in ((h_two, swap_replica(h_two)), (swap_tp(h_two), swap_both(h_two))):
        h_parts += [first, swap_core(first), second, swap_core(second)]
    side, mlp_sums = mlp(place, h_parts, dy_parts, dy_t, mlp_full)
    mlp_own = lax.psum_scatter(mlp_sums, "grp", scatter_dimension=0, tiled=True)

    sums = scatter_sums(mlp_back(side, mlp_full, 0, 2))
    out_parts = mlp_back(side, mlp_full, 2, 1, after=(sums[0],))
    da = middle_back(place, sums, mid, cotangent, kv_full, after=(out_parts[0],))
    da_tp = swap_tp(da)
    da_parts = [da, swap_core(da)]

    def back_of(k, after=()):
        return attend_back(
            k, offsets_all, place, da_parts[2 * k], da_parts[2 * k + 1], wide_full, qs[k], kvs[k],
            os_[k], lses[k], cos, sin, after=after,
        )

    first_back = back_of(0)
    *out_shares, da_tp = scatter_sums(out_parts, held=(da_tp,), after=(first_back[0],))
    da_parts += [da_tp, swap_core(da_tp)]
    out_sums = out_grads(da_parts, os_, after=(out_shares[0],))
    out_own = lax.psum_scatter(out_sums, "grp", scatter_dimension=0, tiled=True)
    second_back = back_of(1, after=(out_sums,))
    dqs = [first_back[0], second_back[0]]
    gain_two, mlp_replica = second_gain_terms(
        mlp_pack, mlp_own, swap_replica(mlp_own), after=(second_back[0],)
    )
    first_right = right_side(0, place, spread(first_back[1]), cos, sin, after=(gain_two,))
    q_sums = query_grads(place, h_turned, dqs, after=(first_right,))
    rate_wide = 2.0 * D ** (-0.5)
    rate_out = 2.0 * max(1, 2 * D // LENGTH) ** (-0.5)
    rate_down = 2.0 * FF ** (-0.5)
    new_mlp = mlp_adam(
        quarter,
        (mlp_own, mlp_replica, swap_core(mlp_own), swap_core(mlp_replica)),
        (w_gateup, moment_gateup, square_gateup),
        (w_down, moment_down, square_down),
        rate_wide,
        rate_down,
        after=(q_sums[0],),
    )
    layer_mine = layer_part(mid, out_shares, after=(new_mlp[-1],))
    x_terms = [q_sums[0]] + [along_x(q_sums[i], i) for i in range(1, 4)]
    kv_sums, second_right = keyval_grads(
        place, h_turned, first_right, spread(second_back[1]), cos, sin, after=(layer_mine,)
    )
    layer_other = swap_tp(layer_mine)
    q_lines = line_sums(place, x_terms, after=(kv_sums, layer_other))
    rights = [first_right, second_right]
    own_part, other_part = project_back(
        dqs, rights, wide_full, kv_full, after=(q_lines[0],)
    )
    dh_share = add_low(own_part, swap_core(other_part))
    dh_received = swap_tp(dh_share)
    z_terms = [q_lines[0]] + [along_z(q_lines[i], i) for i in range(1, 4)]
    own = final_sums(z_terms, out_own, spread(kv_sums), after=(dh_share,))

    replica = swap_replica(own)
    gain_own = gain_terms(
        wide_pack, kv_pack, (own, replica), (gain_two, swap_replica(gain_two))
    )
    new_query, new_out, new_keyval = attn_adam(
        core_list,
        (own, replica, swap_core(own), swap_core(replica)),
        (w_query, moment_query, square_query),
        (w_out, moment_out, square_out),
        (w_keyval, moment_keyval, square_keyval),
        rate_wide,
        rate_out,
        after=(gain_own,),
    )
    input_grad, layer_out = row_outputs(
        place, layer_mine, layer_other, (da, da_parts[2]), dh_share, dh_received, tokens, kv_full, after=(new_out[0],)
    )
    new_gains = gain_adam(
        (gain_own, swap_core(gain_own), swap_tp(gain_own), swap_core_tp(gain_own)),
        (norm_gains, moment_gains, square_gains),
    )
    return (
        layer_out,
        input_grad,
        *new_query,
        *new_keyval,
        *new_out,
        *new_mlp,
        *new_gains,
    )


def solution(mesh):
    rows = P("rep", "grp", None)
    flat = P("grp", "tp")
    deep = P("grp", None, "tp")
    states = (flat,) * 3 + (deep,) * 3 + (flat,) * 3 + (deep,) * 3 + (flat,) * 3
    states += (P("grp", None),) * 3
    return jax.shard_map(
        on_device,
        mesh=mesh,
        in_specs=(rows, rows, P("rep", None)) + states,
        out_specs=(rows, rows) + states,
        check_vma=False,
    )
```

```python
import functools

import jax
import jax.numpy as jnp
from jax import lax
from jax.experimental import pallas as pl
from jax.experimental.layout import Layout, with_layout_constraint
from jax.experimental.pallas import tpu as pltpu
from jax.sharding import PartitionSpec as P

D = 2048
HEAD_DIM = 64
FF = 5632
LENGTH = 2048
STEP = 10
GROUP = 16
SPAN = 128
TILE = 256

norm_epsilon = 1e-05
rope_base = 10000.0
neg_large = -1e30
beta_first = 0.9
beta_second = 0.95
adam_epsilon = 1e-08
decay_rate = 0.1

bf16 = jnp.bfloat16
f32 = jnp.float32

VMEM_LIMIT = 63 * 1024 * 1024

CORE_SWAP = [(0, 1), (1, 0), (2, 3), (3, 2)]
REPLICA_SWAP = [(0, 2), (1, 3), (2, 0), (3, 1)]
BOTH_CORES_SWAP = [(0, 3), (1, 2), (2, 1), (3, 0)]
TP_SWAP = [(0, 1), (1, 0)]
CORE_TP_SWAP = [(2 * r + t, 2 * (r ^ 1) + (1 - t)) for r in range(4) for t in range(2)]
BOTH_SWAP = [(2 * r + t, 2 * (r ^ 2) + (1 - t)) for r in range(4) for t in range(2)]


def struct(shape, dtype):
    return jax.ShapeDtypeStruct(shape, dtype)


def kernel_call(
    kernel, *, name, out_shape, grid=(), in_specs=None, out_specs=None, scratch_shapes=(), prefetch=0,
    after=(),
):
    first = prefetch + len(in_specs)

    def body(*refs):
        kernel(*refs[:first], *refs[first + len(after) :])

    grid_spec = pltpu.PrefetchScalarGridSpec(
        num_scalar_prefetch=prefetch,
        grid=grid,
        in_specs=list(in_specs) + [pl.BlockSpec(memory_space=pl.ANY)] * len(after),
        out_specs=out_specs,
        scratch_shapes=list(scratch_shapes),
    )
    call = pl.pallas_call(
        body,
        grid_spec=grid_spec,
        out_shape=out_shape,
        compiler_params=pltpu.CompilerParams(vmem_limit_bytes=VMEM_LIMIT),
        name=name,
    )
    return lambda *args: call(*args, *after)


def dot_nn(left, right):
    return lax.dot_general(left, right, (((1,), (0,)), ((), ())), preferred_element_type=f32)


def dot_nt(left, right):
    return lax.dot_general(left, right, (((1,), (1,)), ((), ())), preferred_element_type=f32)


def dot_tn(left, right):
    return lax.dot_general(left, right, (((0,), (0,)), ((), ())), preferred_element_type=f32)


def adamw(weight, moment, square, grad, rate, decay):
    moment = beta_first * moment + (1.0 - beta_first) * grad
    square = beta_second * square + (1.0 - beta_second) * grad * grad
    fix_first = 1.0 - beta_first**STEP
    fix_second = 1.0 - beta_second**STEP
    update = moment / fix_first / (jnp.sqrt(square / fix_second) + adam_epsilon)
    return (weight * (1.0 - rate * decay) - rate * update, moment, square)


def norm_back(upstream, gain, normed, scale):
    weighted = upstream * gain
    return scale * (weighted - normed * jnp.mean(weighted * normed, axis=-1, keepdims=True))


def partner(values):
    lane = lax.broadcasted_iota(jnp.int32, values.shape, 1)
    up = pltpu.roll(values, 96, 1)
    down = pltpu.roll(values, 32, 1)
    return jnp.where(lane % HEAD_DIM < HEAD_DIM // 2, up, down)


def row_of(block):
    return jnp.concatenate([block[i : i + 1, :] for i in range(GROUP)], axis=1)


def rms_scale(values):
    return lax.rsqrt(jnp.mean(values * values, axis=-1, keepdims=True) + norm_epsilon)


def gain_row(gain_ref, index):
    return row_of(gain_ref[:, index, :].astype(f32))


GAIN_SPEC = pl.BlockSpec((GROUP, 16, 128), lambda *_: (0, 8, 0))
WQ_SPEC = pl.BlockSpec((D, 512), lambda *_: (0, 0))
WO_SPEC = pl.BlockSpec((D, 512), lambda *_: (0, 1))
WKV_SPEC = pl.BlockSpec((GROUP, 128, 128), lambda *_: (0, 0, 0))
ROWS_SPEC = pl.BlockSpec((SPAN, D), lambda *_: (0, 0))


def half_of(place, k):
    return place[1] if k == 0 else 1 - place[1]


STRIP = 128
STRIP_SPEC = pl.BlockSpec((STRIP, D), lambda i, *_: (i, 0))
HALF_SPEC = pl.BlockSpec((SPAN // 2, D), lambda i, *_: (i, 0))


def seq_strip(k):
    return pl.BlockSpec((1, STRIP, D), lambda i, *refs: (half_of(refs[-1], k), i, 0))


def seq_spec(k):
    return pl.BlockSpec((1, SPAN, D), lambda *ids: (half_of(ids[-1], k), 0, 0))


def turn_spec(k):
    return pl.BlockSpec((SPAN, 128), lambda i, *refs: (2 * half_of(refs[-1], k) + i, 0))


def whole_spec(shape):
    return pl.BlockSpec(shape, lambda *_: (0,) * len(shape))


def pack_attn_kernel(core_ref, wq_ref, wo_ref, wkv_ref, gain_ref, wide_ref, kv_ref, copies_ref):
    lane = lax.broadcasted_iota(jnp.int32, (128, 128), 1)
    low_half = lane < HEAD_DIM
    first_core = core_ref[0] == 0
    key = jnp.where(first_core, wkv_ref[:, 0, :], pltpu.roll(wkv_ref[:, 0, :], HEAD_DIM, 1))
    value = jnp.where(first_core, pltpu.roll(wkv_ref[:, 1, :], HEAD_DIM, 1), wkv_ref[:, 1, :])
    kv = jnp.where(low_half, key, value).astype(bf16)
    wide_ref[:, :512] = wq_ref[...].astype(bf16)
    wide_ref[:, 512:] = wo_ref[...].astype(bf16)
    kv_ref[...] = kv
    gains = jnp.concatenate([gain_ref[...], jnp.zeros((14, 128), f32)], axis=0).astype(bf16)
    for g in range(GROUP):
        copies_ref[g, :128, :] = kv
        copies_ref[g, 128:, :] = gains


def pack_attn(core, w_query, w_out, w_keyval, gains):
    rows = w_query.shape[0]
    half = pl.BlockSpec((rows, 512), lambda i, core: (0, core[0]))
    shapes = [(rows, 1024), (rows, 128), (GROUP, rows + 16, 128)]
    return kernel_call(
        pack_attn_kernel,
        prefetch=1,
        grid=(1,),
        in_specs=[half, half, whole_spec(w_keyval.shape), whole_spec(gains.shape)],
        out_specs=[whole_spec(shape) for shape in shapes],
        out_shape=[struct(shape, bf16) for shape in shapes],
        name="pack_attn",
    )(core, w_query, w_out, w_keyval, gains)


def project_kv_kernel(
    place_ref, own_ref, other_ref, wkv_ref, gain_ref, cos_ref, sin_ref, h_ref, turned_ref, kv_ref
):
    mine = pl.program_id(0) == 0
    x = jnp.where(mine, own_ref[0].astype(f32), other_ref[0].astype(f32))
    h = (x * rms_scale(x) * gain_row(gain_ref, 0)).astype(bf16)
    h_ref[...] = h
    low_half = lax.broadcasted_iota(jnp.int32, (SPAN, 128), 1) < HEAD_DIM
    keyval = dot_nn(h, wkv_ref[...].reshape(D, 128))
    turned = keyval * cos_ref[...] + partner(keyval) * sin_ref[...]
    kv = jnp.where(low_half, turned, keyval).astype(bf16)
    kv_ref[...] = jnp.broadcast_to(kv[None], (GROUP, SPAN, 128))
    turned_ref[...] = h.T


def project_kv(k, place, x_own, x_other, kv_full, cos, sin, after=()):
    return kernel_call(
        project_kv_kernel,
        prefetch=1,
        grid=(2,),
        in_specs=[seq_spec(k), seq_spec(k), WKV_SPEC, GAIN_SPEC, turn_spec(k), turn_spec(k)],
        out_specs=[
            pl.BlockSpec((SPAN, D), lambda i, *_: (i, 0)),
            pl.BlockSpec((D, SPAN), lambda i, *_: (0, i)),
            pl.BlockSpec((GROUP, SPAN, 128), lambda i, *_: (0, i, 0)),
        ],
        out_shape=[
            struct((2 * SPAN, D), bf16),
            struct((D, 2 * SPAN), bf16),
            struct((GROUP, 2 * SPAN, 128), bf16),
        ],
        after=after,
        name="project_kv",
    )(place, x_own, x_other, kv_full, kv_full, cos, sin)


def project_q_kernel(place_ref, h_ref, wq_ref, cos_ref, sin_ref, q_ref):
    cos = cos_ref[...]
    sin = sin_ref[...]
    low_half = lax.broadcasted_iota(jnp.int32, cos.shape, 1) < HEAD_DIM
    query = dot_nn(h_ref[...], wq_ref[...])
    for pair in range(4):
        block = query[:, pair * 128 : (pair + 1) * 128]
        turned = (block * cos + partner(block) * sin) * (HEAD_DIM**-0.5)
        q_ref[2 * pair] = jnp.where(low_half, turned, 0.0).astype(bf16)
        q_ref[2 * pair + 1] = jnp.where(
            low_half, pltpu.roll(turned, HEAD_DIM, 1), 0.0
        ).astype(bf16)


def project_q(k, place, h, wide_full, cos, sin, after=()):
    turn = pl.BlockSpec((2 * SPAN, 128), lambda i, place: (half_of(place, k), 0))
    return kernel_call(
        project_q_kernel,
        prefetch=1,
        grid=(1,),
        in_specs=[whole_spec((2 * SPAN, D)), WQ_SPEC, turn, turn],
        out_specs=whole_spec((8, 2 * SPAN, 128)),
        out_shape=struct((8, 2 * SPAN, 128), bf16),
        after=after,
        name="project_q",
    )(place, h, wide_full, cos, sin)


CHUNK = 512
BACK_CHUNK = 1024


def causal_offsets():
    key = lax.broadcasted_iota(jnp.int32, (128, 256), 0)
    query = lax.broadcasted_iota(jnp.int32, (128, 256), 1) % SPAN
    return key - query


def masked(raw, differ, own, off_ref, seq, c):
    parts = []
    blocks = raw.shape[0] // 128
    for j in range(blocks):
        allowed = differ <= own - off_ref[seq, blocks * c + j]
        parts.append(jnp.where(allowed, raw[j * 128 : (j + 1) * 128], neg_large))
    return jnp.concatenate(parts, axis=0)


def attend_kernel(
    off_ref, place_ref, q_ref, kv_ref, wo_ref, o_ref, lse_ref, own_ref, other_ref, kvt, scores, *, k
):
    step = pl.program_id(0)
    seq = 2 * half_of(place_ref, k) + step
    kvt[...] = kv_ref[...].reshape(LENGTH, 128).T
    own = off_ref[seq, place_ref[0]]
    differ = causal_offsets()
    blocks = CHUNK // 128

    for pair in range(4):
        q = q_ref[2 * pair : 2 * pair + 2].reshape(256, 128)
        top = jnp.full((1, 256), neg_large, f32)
        for c in range(LENGTH // CHUNK):
            raw = dot_nt(kv_ref[blocks * c : blocks * (c + 1)].reshape(CHUNK, 128), q)
            score = masked(raw, differ, own, off_ref, seq, c)
            scores[pair % 2, c * CHUNK : (c + 1) * CHUNK, :] = score
            top = jnp.maximum(top, jnp.max(score, axis=0, keepdims=True))
        total = jnp.zeros((1, 256), f32)
        mixed = jnp.zeros((128, 256), f32)
        for c in range(LENGTH // CHUNK):
            weight = jnp.exp(scores[pair % 2, c * CHUNK : (c + 1) * CHUNK, :] - top)
            total = total + jnp.sum(weight, axis=0, keepdims=True)
            mixed = mixed + dot_nn(kvt[:, c * CHUNK : (c + 1) * CHUNK], weight.astype(bf16))
        out = (mixed[HEAD_DIM:, :] / total).T
        o_ref[pair] = jnp.concatenate([out[:SPAN], out[SPAN:]], axis=1).astype(bf16)
        lse_ref[0, pair : pair + 1, :] = top + jnp.log(total)

    heads = jnp.concatenate([o_ref[i] for i in range(4)], axis=1)
    part = dot_nt(heads, wo_ref[...]).astype(bf16)

    @pl.when(step == 0)
    def _():
        own_ref[...] = part

    @pl.when(step == 1)
    def _():
        other_ref[...] = part


def attend(k, offsets, place, q, kv_all, wo_full, after=()):
    grid_spec = dict(
        prefetch=2,
        grid=(2,),
        in_specs=[
            pl.BlockSpec((8, SPAN, 128), lambda i, *_: (0, i, 0)),
            pl.BlockSpec((GROUP, SPAN, 128), lambda i, *_: (0, i, 0)),
            WO_SPEC,
        ],
        out_specs=[
            pl.BlockSpec((4, SPAN, 128), lambda i, *_: (0, i, 0)),
            pl.BlockSpec((1, 4, 256), lambda i, *_: (i, 0, 0)),
            ROWS_SPEC,
            ROWS_SPEC,
        ],
        scratch_shapes=[pltpu.VMEM((128, LENGTH), bf16), pltpu.VMEM((2, LENGTH, 256), f32)],
    )
    return kernel_call(
        functools.partial(attend_kernel, k=k),
        **grid_spec,
        out_shape=[
            struct((4, 2 * SPAN, 128), bf16),
            struct((2, 4, 256), f32),
            struct((SPAN, D), bf16),
            struct((SPAN, D), bf16),
        ],
        after=after,
        name="attend",
    )(offsets, place, q, kv_all, wo_full)


def share_kernel(own_ref, other_ref, out_ref):
    out_ref[...] = (own_ref[...].astype(f32) + other_ref[...].astype(f32)).astype(bf16)


def add_low(first, second, after=()):
    rows, width = first.shape
    block = pl.BlockSpec((128, width), lambda i: (i, 0))
    return kernel_call(
        share_kernel,
        grid=(rows // 128,),
        in_specs=[block, block],
        out_specs=block,
        out_shape=struct(first.shape, bf16),
        after=after,
        name="add_low",
    )(first, second)


def middle_kernel(place_ref, x_ref, one_ref, two_ref, gain_ref, mid_ref, h_ref):
    total = one_ref[...].astype(f32) + two_ref[...].astype(f32)
    mid = x_ref[0].astype(f32) + total
    mid_ref[...] = mid
    h_ref[...] = (mid * rms_scale(mid) * gain_row(gain_ref, 1)).astype(bf16)


def middle(place, x_own, one, two, attn_full):
    return kernel_call(
        middle_kernel,
        prefetch=1,
        grid=(SPAN // STRIP,),
        in_specs=[seq_strip(0), STRIP_SPEC, STRIP_SPEC, GAIN_SPEC],
        out_specs=[STRIP_SPEC, STRIP_SPEC],
        out_shape=[struct((SPAN, D), f32), struct((SPAN, D), bf16)],
        name="middle",
    )(place, x_own, one, two, attn_full)


def sum_rows(refs):
    return sum(ref[...].astype(f32) for ref in refs)


def middle_back_kernel(place_ref, p0, p1, p2, p3, mid_ref, dy_ref, gain_ref, da_ref):
    upstream = sum_rows((p0, p1, p2, p3))
    mid = mid_ref[...]
    scale = rms_scale(mid)
    d_norm = norm_back(upstream, gain_row(gain_ref, 1), mid * scale, scale)
    da_ref[...] = (dy_ref[0].astype(f32) + d_norm).astype(bf16)


def middle_back(place, parts, mid, dy_own, attn_full, after=()):
    return kernel_call(
        middle_back_kernel,
        prefetch=1,
        grid=(SPAN // STRIP,),
        in_specs=[STRIP_SPEC] * 5 + [seq_strip(0), GAIN_SPEC],
        out_specs=STRIP_SPEC,
        out_shape=struct((SPAN, D), bf16),
        after=after,
        name="middle_back",
    )(place, *parts, mid, dy_own, attn_full)


def layer_part_kernel(mid_ref, p0, p1, p2, p3, out_ref):
    out_ref[...] = (mid_ref[...] + sum_rows((p0, p1, p2, p3))).astype(bf16)


def layer_part(mid, parts, after=()):
    return kernel_call(
        layer_part_kernel,
        grid=(SPAN // STRIP,),
        in_specs=[STRIP_SPEC] * 5,
        out_specs=STRIP_SPEC,
        out_shape=struct((SPAN, D), bf16),
        after=after,
        name="layer_part",
    )(mid, *parts)


def row_outputs_kernel(
    place_ref, mine_ref, other_ref, da0, da1, s0, s1, r0, r1, x_ref, gain_ref, out_ref, layer_ref
):
    layer_ref[half_of(place_ref, 0)] = mine_ref[...]
    layer_ref[half_of(place_ref, 1)] = other_ref[...]
    gain = gain_row(gain_ref, 0)
    for k, (da_ref, share, received) in enumerate(((da0, s0, r1), (da1, s1, r0))):
        upstream = share[...].astype(f32) + received[...].astype(f32)
        m = half_of(place_ref, k)
        x = x_ref[m].astype(f32)
        scale = rms_scale(x)
        out_ref[m] = da_ref[...].astype(f32) + norm_back(upstream, gain, x * scale, scale)


def row_outputs(place, mine, other, das, share, received, x_own, kv_full, after=()):
    steps = 2
    rows = SPAN // steps
    block = pl.BlockSpec((rows, D), lambda i, *_: (i, 0))
    second = pl.BlockSpec((rows, D), lambda i, *_: (steps + i, 0))
    seqs = pl.BlockSpec((2, rows, D), lambda i, *_: (0, i, 0))
    return kernel_call(
        row_outputs_kernel,
        prefetch=1,
        grid=(steps,),
        in_specs=[block] * 5 + [second, block, second, seqs, GAIN_SPEC],
        out_specs=[seqs, seqs],
        out_shape=[struct((2, SPAN, D), f32), struct((2, SPAN, D), bf16)],
        after=after,
        name="row_outputs",
    )(place, mine, other, *das, share, share, received, received, x_own, kv_full)


PACK_ROWS = 16
ALL_ROWS = 8 * SPAN
SMALL = 128
WINDOW_TILES = 6
WIDTH = 3 * WINDOW_TILES * SMALL
WINDOW_STARTS = (0, 6, 11, 16)
FIRST_OWN = (0, 6, 12, 17, 22)


def window_start(quarter):
    return jnp.where(quarter < 2, 6 * quarter, 5 * quarter + 1)


def packed_column(tile, kind):
    return 3 * TILE * (tile // 2) + TILE * kind + SMALL * (tile % 2)


def transpose_kernel(place_ref, *refs):
    parts, out_ref = refs[:-1], refs[-1]
    for k in range(2):
        for i, ref in enumerate(parts):
            start = (len(parts) * k + i) * SPAN
            out_ref[:, start : start + SPAN] = ref[half_of(place_ref, k)].T


def transposed(place, parts, after=()):
    seqs = pl.BlockSpec((2, SPAN, 512), lambda i, *_: (0, 0, i))
    return kernel_call(
        transpose_kernel,
        prefetch=1,
        grid=(D // 512,),
        in_specs=[seqs] * 4,
        out_specs=pl.BlockSpec((512, ALL_ROWS), lambda i, *_: (i, 0)),
        out_shape=struct((D, ALL_ROWS), bf16),
        after=after,
        name="transposed",
    )(place, *parts)


def mlp_kernel(place_ref, *refs):
    h_parts, dy_parts, dyt_ref, w_ref = refs[:8], refs[8:12], refs[12], refs[13]
    side_ref, sum_ref, h, ht, dy, dyt, sems = refs[14:]
    step = pl.program_id(0)

    def part_copies():
        copies = []
        for i, ref in enumerate(h_parts):
            spot = h.at[i * SPAN : (i + 1) * SPAN]
            copies.append(pltpu.make_async_copy(ref, spot, sems.at[i]))
        for k in range(2):
            for i, ref in enumerate(dy_parts):
                number = 4 * k + i
                spot = dy.at[number * SPAN : (number + 1) * SPAN]
                source = ref.at[half_of(place_ref, k)]
                copies.append(pltpu.make_async_copy(source, spot, sems.at[8 + number]))
        return copies

    turned_copy = pltpu.make_async_copy(dyt_ref, dyt, sems.at[16])

    def work(start):
        rows = slice(start, start + 256)
        both = dot_nn(h[rows, :], w_ref[:, : 2 * TILE])
        upstream = dot_nn(dy[rows, :], w_ref[:, 2 * TILE :])
        gate = both[:, :TILE]
        up = both[:, TILE:]
        sigmoid = jax.nn.sigmoid(gate)
        active = gate * sigmoid
        side_ref[rows, :TILE] = (
            upstream * up * (sigmoid * (1.0 + gate * (1.0 - sigmoid)))
        ).astype(bf16)
        side_ref[rows, TILE : 2 * TILE] = (upstream * active).astype(bf16)
        side_ref[rows, 2 * TILE :] = (active * up).astype(bf16)

    @pl.when(step == 0)
    def _():
        copies = part_copies()
        for i in range(8):
            copies[i].start()
            copies[8 + i].start()
        turned_copy.start()
        for start in range(0, ALL_ROWS, 256):
            for i in range(start // SPAN, start // SPAN + 2):
                copies[i].wait()
                copies[8 + i].wait()
            work(start)
        ht[...] = h[...].T
        turned_copy.wait()

    @pl.when(step > 0)
    def _():
        for start in range(0, ALL_ROWS, 256):
            work(start)

    sum_ref[:, : 2 * TILE] = dot_nn(ht[...], side_ref[:, : 2 * TILE]).astype(bf16)
    sum_ref[:, 2 * TILE :] = dot_nn(dyt[...], side_ref[:, 2 * TILE :]).astype(bf16)


def mlp(place, h_parts, dy_parts, dy_t, w_full, after=()):
    width = 3 * TILE
    return kernel_call(
        mlp_kernel,
        prefetch=1,
        grid=(WIDTH // width,),
        in_specs=[pl.BlockSpec(memory_space=pl.ANY)] * 13
        + [pl.BlockSpec((D, width), lambda i, *_: (0, i))],
        out_specs=[
            pl.BlockSpec((ALL_ROWS, width), lambda i, *_: (0, i)),
            pl.BlockSpec((D, width), lambda i, *_: (0, i)),
        ],
        out_shape=[struct((ALL_ROWS, WIDTH), bf16), struct((D, WIDTH), bf16)],
        scratch_shapes=[
            pltpu.VMEM((ALL_ROWS, D), bf16),
            pltpu.VMEM((D, ALL_ROWS), bf16),
            pltpu.VMEM((ALL_ROWS, D), bf16),
            pltpu.VMEM((D, ALL_ROWS), bf16),
            pltpu.SemaphoreType.DMA((17,)),
        ],
        after=after,
        name="mlp",
    )(place, *h_parts, *dy_parts, dy_t, w_full)


def mlp_back_kernel(side_ref, w_ref, *outs, first, count):
    total = jnp.zeros((ALL_ROWS, w_ref.shape[0]), f32)
    for column in range(0, WIDTH, 3 * TILE):
        span = slice(column + first * TILE, column + (first + count) * TILE)
        total = total + dot_nt(side_ref[:, span], w_ref[:, span])
    for out, i in zip(outs, range(8)):
        out[...] = total[i * SPAN : (i + 1) * SPAN].astype(bf16)


def mlp_back(side, w_full, first, count, after=()):
    return kernel_call(
        functools.partial(mlp_back_kernel, first=first, count=count),
        grid=(D // 512,),
        in_specs=[whole_spec((ALL_ROWS, WIDTH)), pl.BlockSpec((512, WIDTH), lambda i: (i, 0))],
        out_specs=[pl.BlockSpec((SPAN, 512), lambda i: (0, i))] * 8,
        out_shape=[struct((SPAN, D), bf16)] * 8,
        after=after,
        name="mlp_back",
    )(side, w_full)


def quad_kernel(*refs):
    count = (len(refs) + 4) // 2
    inputs, outs = refs[:count], refs[count:]
    for i in range(4):
        total = inputs[2 * i][...].astype(f32) + inputs[2 * i + 1][...].astype(f32)
        outs[i][...] = total.astype(bf16)
    for source, target in zip(inputs[8:], outs[4:]):
        target[...] = source[...]


def add_quads(pairs, held=(), after=()):
    count = len(held)
    return kernel_call(
        quad_kernel,
        grid=(2,),
        in_specs=[HALF_SPEC] * (8 + count),
        out_specs=[HALF_SPEC] * (4 + count),
        out_shape=[struct((SPAN, D), bf16)] * (4 + count),
        after=after,
        name="add_quads",
    )(*[value for pair in pairs for value in pair], *held)


def attend_back_kernel(
    off_ref, place_ref, own_ref, other_ref, wo_ref, q_ref, kv_ref, o_ref, lse_ref, cos_ref,
    sin_ref, dq_ref, dkv_ref, kvt, d_heads, dkv, *, k,
):
    step = pl.program_id(0)
    seq = 2 * half_of(place_ref, k) + step
    kvt[...] = kv_ref[...].reshape(LENGTH, 128).T
    dkv[...] = jnp.zeros_like(dkv)
    d_out_rows = jnp.where(step == 0, own_ref[...].astype(f32), other_ref[...].astype(f32))
    d_all = dot_nn(d_out_rows.astype(bf16), wo_ref[...])
    for pair in range(4):
        d_heads[pair] = d_all[:, pair * 128 : (pair + 1) * 128].astype(bf16).astype(f32)
    own = off_ref[seq, place_ref[0]]
    differ = causal_offsets()
    lane = lax.broadcasted_iota(jnp.int32, (SPAN, 128), 1)
    high_half = lane >= HEAD_DIM
    cos = cos_ref[...]
    sin = sin_ref[...]
    blocks = BACK_CHUNK // 128

    for pair in range(4):
        q = q_ref[2 * pair : 2 * pair + 2].reshape(256, 128)
        d_out = d_heads[pair]
        first = jnp.where(high_half, pltpu.roll(d_out, HEAD_DIM, 1), 0.0).astype(bf16)
        second = jnp.where(high_half, d_out, 0.0).astype(bf16)
        d_o = jnp.concatenate([first, second], axis=0)
        dots = (d_out * o_ref[pair].astype(f32)).T
        inner = jnp.concatenate(
            [
                jnp.sum(dots[:HEAD_DIM], axis=0, keepdims=True),
                jnp.sum(dots[HEAD_DIM:], axis=0, keepdims=True),
            ],
            axis=1,
        )
        lse = lse_ref[0, pair : pair + 1, :]
        d_query = jnp.zeros((128, 256), f32)
        for c in range(LENGTH // BACK_CHUNK):
            kv = kv_ref[blocks * c : blocks * (c + 1)].reshape(BACK_CHUNK, 128)
            score = masked(dot_nt(kv, q), differ, own, off_ref, seq, c)
            prob = jnp.exp(score - lse)
            d_prob = dot_nt(kv, d_o)
            d_score = (prob * (d_prob - inner)).astype(bf16)
            span = slice(c * BACK_CHUNK, (c + 1) * BACK_CHUNK)
            dkv[span, :] += dot_nn(d_score, q) + dot_nn(prob.astype(bf16), d_o)
            d_query = d_query + dot_nn(kvt[:, span], d_score)
        turned = d_query[:HEAD_DIM, :].T
        block = jnp.concatenate([turned[:SPAN], turned[SPAN:]], axis=1)
        block = (block * cos - partner(block) * sin) * (HEAD_DIM**-0.5)
        dq_ref[pair] = block.astype(bf16)

    dkv_ref[...] = dkv[...].astype(bf16).reshape(GROUP, SPAN, 128)


def attend_back(k, offsets, place, da_own, da_other, wo_full, q, kv_all, o, lse, cos, sin, after=()):
    turn = turn_spec(k)
    heads = pl.BlockSpec((4, SPAN, 128), lambda i, *_: (0, i, 0))
    group = pl.BlockSpec((GROUP, SPAN, 128), lambda i, *_: (0, i, 0))
    grid_spec = dict(
        prefetch=2,
        grid=(2,),
        in_specs=[
            ROWS_SPEC,
            ROWS_SPEC,
            WO_SPEC,
            pl.BlockSpec((8, SPAN, 128), lambda i, *_: (0, i, 0)),
            group,
            heads,
            pl.BlockSpec((1, 4, 256), lambda i, *_: (i, 0, 0)),
            turn,
            turn,
        ],
        out_specs=[heads, group],
        scratch_shapes=[
            pltpu.VMEM((128, LENGTH), bf16),
            pltpu.VMEM((4, SPAN, 128), f32),
            pltpu.VMEM((LENGTH, 128), f32),
        ],
    )
    return kernel_call(
        functools.partial(attend_back_kernel, k=k),
        **grid_spec,
        out_shape=[
            struct((4, 2 * SPAN, 128), bf16),
            struct((GROUP, 2 * SPAN, 128), bf16),
        ],
        after=after,
        name="attend_back",
    )(offsets, place, da_own, da_other, wo_full, q, kv_all, o, lse, cos, sin)


def out_grads_kernel(a0, a1, a2, a3, o0_ref, o1_ref, out_ref):
    heads = jnp.concatenate(
        [jnp.concatenate([ref[i] for i in range(4)], axis=1) for ref in (o0_ref, o1_ref)],
        axis=0,
    )
    rows = jnp.concatenate([ref[...] for ref in (a0, a1, a2, a3)], axis=0)
    out_ref[...] = dot_tn(rows, heads).astype(bf16)


def out_grads(da_parts, o_parts, after=()):
    return kernel_call(
        out_grads_kernel,
        grid=(4,),
        in_specs=[pl.BlockSpec((SPAN, 512), lambda i: (0, i))] * 4
        + [whole_spec((4, 2 * SPAN, 128))] * 2,
        out_specs=pl.BlockSpec((512, 512), lambda i: (i, 0)),
        out_shape=struct((D, 512), bf16),
        after=after,
        name="out_grads",
    )(*da_parts, *o_parts)


def right_kernel(place_ref, dkv_ref, cos_ref, sin_ref, out_ref):
    lane = lax.broadcasted_iota(jnp.int32, (SPAN, 128), 1)
    total = jnp.sum(dkv_ref[...].astype(f32), axis=0)
    turned = total * cos_ref[...] - partner(total) * sin_ref[...]
    out_ref[...] = jnp.where(lane < HEAD_DIM, turned, total).astype(bf16)


def right_side(k, place, dkv, cos, sin, after=()):
    return kernel_call(
        right_kernel,
        prefetch=1,
        grid=(2,),
        in_specs=[
            pl.BlockSpec((GROUP, SPAN, 128), lambda i, *_: (0, i, 0)),
            turn_spec(k),
            turn_spec(k),
        ],
        out_specs=pl.BlockSpec((SPAN, 128), lambda i, *_: (i, 0)),
        out_shape=struct((2 * SPAN, 128), bf16),
        after=after,
        name="right_side",
    )(place, dkv, cos, sin)


def query_grads_kernel(place_ref, h0_ref, h1_ref, q0_ref, q1_ref, *outs):
    rights = [jnp.concatenate([ref[i] for i in range(4)], axis=1) for ref in (q0_ref, q1_ref)]
    for step in range(4):
        for z in range(4):
            owner = z * 4 + (place_ref[0] + step) % 4
            rows = pl.ds(pl.multiple_of(owner * 128, 128), 128)
            total = dot_nn(h0_ref[rows, :], rights[0]) + dot_nn(h1_ref[rows, :], rights[1])
            outs[step][z] = total.astype(bf16)


def query_grads(place, h_turned, dqs, after=()):
    args = (*h_turned, *dqs)
    shape = (4, 128, 512)
    return kernel_call(
        query_grads_kernel,
        prefetch=1,
        grid=(1,),
        in_specs=[whole_spec(arg.shape) for arg in args],
        out_specs=[whole_spec(shape)] * 4,
        out_shape=[struct(shape, bf16)] * 4,
        after=after,
        name="query_grads",
    )(place, *args)


def line_sum_kernel(place_ref, e0, e1, e2, e3, *outs):
    for step in range(4):
        z = (place_ref[0] // 4 + step) % 4
        outs[step][...] = sum(ref[z].astype(f32) for ref in (e0, e1, e2, e3)).astype(bf16)


def line_sums(place, terms, after=()):
    shape = terms[0].shape[1:]
    return kernel_call(
        line_sum_kernel,
        prefetch=1,
        grid=(1,),
        in_specs=[whole_spec(term.shape) for term in terms],
        out_specs=[whole_spec(shape)] * 4,
        out_shape=[struct(shape, bf16)] * 4,
        after=after,
        name="line_sums",
    )(place, *terms)


def final_sums_kernel(e0, e1, e2, e3, out_ref, kv_ref, sum_ref):
    sum_ref[:, :512] = sum_rows((e0, e1, e2, e3)).astype(bf16)
    sum_ref[:, 512:1024] = out_ref[...]
    sum_ref[:, 1024:] = jnp.sum(kv_ref[...].astype(f32), axis=0).astype(bf16)


def final_sums(q_terms, out_own, kv_terms, after=()):
    args = (*q_terms, out_own, kv_terms)
    return kernel_call(
        final_sums_kernel,
        grid=(1,),
        in_specs=[whole_spec(arg.shape) for arg in args],
        out_specs=whole_spec((128, 1152)),
        out_shape=struct((128, 1152), bf16),
        after=after,
        name="final_sums",
    )(*args)


def torus_shift(dz, dx):
    return [
        (z * 4 + x, ((z + dz) % 4) * 4 + (x + dx) % 4) for z in range(4) for x in range(4)
    ]


def along_x(values, step):
    return lax.ppermute(values, "grp", torus_shift(0, step))


def along_z(values, step):
    return lax.ppermute(values, "grp", torus_shift(step, 0))


def keyval_grads_kernel(
    place_ref, h0_ref, h1_ref, r0_ref, dkv_ref, cos_ref, sin_ref, out_ref, right_ref
):
    lane = lax.broadcasted_iota(jnp.int32, (SPAN, 128), 1)
    for i in range(2):
        rows = slice(i * SPAN, (i + 1) * SPAN)
        total = jnp.sum(dkv_ref[:, rows, :].astype(f32), axis=0)
        turned = total * cos_ref[rows, :] - partner(total) * sin_ref[rows, :]
        right_ref[rows, :] = jnp.where(lane < HEAD_DIM, turned, total).astype(bf16)
    total = dot_nn(h0_ref[...], r0_ref[...]) + dot_nn(h1_ref[...], right_ref[...])
    out_ref[...] = total.reshape(out_ref.shape)


def keyval_grads(place, h_turned, first_right, dkv, cos, sin, after=()):
    turn = pl.BlockSpec((2 * SPAN, 128), lambda i, place: (half_of(place, 1), 0))
    args = (*h_turned, first_right, dkv)
    return kernel_call(
        keyval_grads_kernel,
        prefetch=1,
        grid=(1,),
        in_specs=[whole_spec(arg.shape) for arg in args] + [turn, turn],
        out_specs=[whole_spec((GROUP, 128, 128)), whole_spec((2 * SPAN, 128))],
        out_shape=[struct((GROUP, 128, 128), f32), struct((2 * SPAN, 128), bf16)],
        after=after,
        name="keyval_grads",
    )(place, *args, cos, sin)


def project_back_kernel(q0_ref, q1_ref, r0_ref, r1_ref, wq_ref, wkv_ref, own_out, other_out):
    wq = wq_ref[...]
    wkv = wkv_ref[...].reshape(512, 128)
    for k, (q_ref, r_ref) in enumerate(((q0_ref, r0_ref), (q1_ref, r1_ref))):
        right = jnp.concatenate([q_ref[i] for i in range(4)], axis=1)
        d_h = (dot_nt(right, wq) + dot_nt(r_ref[...], wkv)).astype(bf16)
        spot = slice(k * SPAN, (k + 1) * SPAN)
        own_out[spot, :] = d_h[:SPAN]
        other_out[spot, :] = d_h[SPAN:]


def project_back(dqs, rights, wide_full, kv_full, after=()):
    args = (*dqs, *rights)
    out = pl.BlockSpec((2 * SPAN, 512), lambda i: (0, i))
    return kernel_call(
        project_back_kernel,
        grid=(4,),
        in_specs=[whole_spec(arg.shape) for arg in args]
        + [
            pl.BlockSpec((512, 512), lambda i: (i, 0)),
            pl.BlockSpec((4, 128, 128), lambda i: (i, 0, 0)),
        ],
        out_specs=[out, out],
        out_shape=[struct((2 * SPAN, D), bf16)] * 2,
        after=after,
        name="project_back",
    )(*args, wide_full, kv_full)


def as_rows(columns):
    return columns.T[:8, :]


def first_gain_kernel(wide_ref, kv_ref, own_ref, rep_ref, two_ref, two_rep, out_ref):
    grad = own_ref[...].astype(f32) + rep_ref[...].astype(f32)
    one = jnp.sum(wide_ref[...].astype(f32) * grad[:, :512], axis=1, keepdims=True)
    one = one + jnp.sum(kv_ref[...].astype(f32) * grad[:, 1024:], axis=1, keepdims=True)
    lane = lax.broadcasted_iota(jnp.int32, (128, 128), 1)
    out_ref[...] = as_rows(jnp.where(lane == 0, one, two_ref[...] + two_rep[...]))


def gain_terms(wide_pack, kv_pack, sums, seconds, after=()):
    wide = pl.BlockSpec((128, 512), lambda i: (0, 0))
    args = (kv_pack, *sums, *seconds)
    return kernel_call(
        first_gain_kernel,
        grid=(1,),
        in_specs=[wide] + [whole_spec(arg.shape) for arg in args],
        out_specs=whole_spec((8, 128)),
        out_shape=struct((8, 128), f32),
        after=after,
        name="gain_terms",
    )(wide_pack, *args)


def second_gain_kernel(pack_ref, sum_ref, held_ref, out_ref, copy_ref):
    total = jnp.zeros((pack_ref.shape[0], 1), f32)
    for column in range(0, WIDTH, 3 * TILE):
        span = slice(column, column + 2 * TILE)
        products = pack_ref[:, span].astype(f32) * sum_ref[:, span].astype(f32)
        total += jnp.sum(products, axis=1, keepdims=True)
    out_ref[...] = jnp.broadcast_to(total, out_ref.shape)
    copy_ref[...] = held_ref[...]


def second_gain_terms(mlp_pack, mlp_sum, held, after=()):
    args = (mlp_pack, mlp_sum, held)
    return kernel_call(
        second_gain_kernel,
        grid=(1,),
        in_specs=[whole_spec(arg.shape) for arg in args],
        out_specs=[whole_spec((128, 128)), whole_spec(held.shape)],
        out_shape=[struct((128, 128), f32), struct(held.shape, held.dtype)],
        after=after,
        name="second_gain_terms",
    )(*args)


def gain_adam_kernel(own, core, tp, both, w, m, s, w_o, m_o, s_o):
    total = (own[...] + core[...]) + (tp[...] + both[...])
    grad = total[:2, :] / w[...].astype(bf16).astype(f32)
    w_o[...], m_o[...], s_o[...] = adamw(w[...], m[...], s[...], grad, 1.0, 0.0)


def gain_adam(terms, states):
    args = (*terms, *[state.T for state in states])
    shape = args[-1].shape
    new = kernel_call(
        gain_adam_kernel,
        grid=(1,),
        in_specs=[whole_spec(arg.shape) for arg in args],
        out_specs=[whole_spec(shape)] * 3,
        out_shape=[struct(shape, f32)] * 3,
        name="gain_adam",
    )(*args)
    return [value.T for value in new]


def flat_view(values):
    rows, kinds, units = values.shape
    tiles = values.reshape(rows, kinds, units // SMALL, SMALL)
    tiles = with_layout_constraint(tiles, Layout(major_to_minor=(0, 2, 1, 3)))
    return tiles.transpose(0, 2, 1, 3).reshape(-1, SMALL)


def deep_view(values, shape):
    rows, kinds, units = shape
    tiles = values.reshape(rows, units // SMALL, kinds, SMALL).transpose(0, 2, 1, 3)
    tiles = with_layout_constraint(tiles, Layout(major_to_minor=(0, 2, 1, 3)))
    return tiles.reshape(shape)


def pack_kernel(quarter_ref, gu_ref, d_ref, out_ref):
    quarter = quarter_ref[0]
    start = window_start(quarter)
    stride = gu_ref.shape[0] // PACK_ROWS
    for tile in range(WINDOW_TILES):
        keep = jnp.where((quarter >= 2) & (tile == 0), 0.0, 1.0)
        for kind in range(3):
            if kind == 2:
                span = pl.ds(pl.multiple_of((start + tile) * SMALL, SMALL), SMALL)
                value = d_ref[:, span]
            else:
                value = gu_ref[pl.ds(2 * (start + tile) + kind, PACK_ROWS, stride), :]
            column = packed_column(tile, kind)
            out_ref[:, column : column + SMALL] = (value * keep).astype(bf16)


def pack_mlp(quarter, w_gateup, w_down, after=()):
    rows, units = w_down.shape
    per_row = 2 * units // SMALL
    return kernel_call(
        pack_kernel,
        prefetch=1,
        grid=(rows // PACK_ROWS,),
        in_specs=[
            pl.BlockSpec((PACK_ROWS * per_row, SMALL), lambda i, quarter: (i, 0)),
            pl.BlockSpec((PACK_ROWS, units), lambda i, quarter: (i, 0)),
        ],
        out_specs=pl.BlockSpec((PACK_ROWS, WIDTH), lambda i, quarter: (i, 0)),
        out_shape=struct((rows, WIDTH), bf16),
        after=after,
        name="pack_mlp",
    )(quarter, flat_view(w_gateup), w_down)


def mlp_adam_kernel(
    quarter_ref, own_ref, replica_ref, core_ref, both_ref, wg, mg, sg, wd, md, sd,
    wg_o, mg_o, sg_o, wd_o, md_o, sd_o, grads, *, rate_wide, rate_down,
):
    stride = wg.shape[0] // PACK_ROWS
    for part in range(4):
        same_core = quarter_ref[0] // 2 == part // 2
        same_replica = quarter_ref[0] % 2 == part % 2
        for tile in range(FIRST_OWN[part], FIRST_OWN[part + 1]):

            def grad(kind):
                column = packed_column(tile - WINDOW_STARTS[part], kind)
                spot = slice(column, column + SMALL)
                near = jnp.where(same_replica, own_ref[:, spot], replica_ref[:, spot])
                far = jnp.where(same_replica, core_ref[:, spot], both_ref[:, spot])
                return jnp.where(same_core, near, far).astype(f32)

            for kind in range(2):
                grads[pl.ds(2 * tile + kind, PACK_ROWS, stride), :] = grad(kind)
            span = slice(tile * SMALL, (tile + 1) * SMALL)
            wd_o[:, span], md_o[:, span], sd_o[:, span] = adamw(
                wd[:, span], md[:, span], sd[:, span], grad(2), rate_down, decay_rate
            )
    wg_o[...], mg_o[...], sg_o[...] = adamw(
        wg[...], mg[...], sg[...], grads[...], rate_wide, decay_rate
    )


def mlp_adam(quarter, sums, gateup, down, rate_wide, rate_down, after=()):
    rows, units = down[0].shape
    per_row = 2 * units // SMALL
    wide = pl.BlockSpec((PACK_ROWS * per_row, SMALL), lambda i, quarter: (i, 0))
    flat = pl.BlockSpec((PACK_ROWS, units), lambda i, quarter: (i, 0))
    grad = pl.BlockSpec((PACK_ROWS, WIDTH), lambda i, quarter: (i, 0))
    new = kernel_call(
        functools.partial(mlp_adam_kernel, rate_wide=rate_wide, rate_down=rate_down),
        prefetch=1,
        grid=(rows // PACK_ROWS,),
        in_specs=[grad] * 4 + [wide] * 3 + [flat] * 3,
        out_specs=[wide] * 3 + [flat] * 3,
        out_shape=[struct((rows * per_row, SMALL), f32)] * 3
        + [struct(down[0].shape, f32)] * 3,
        scratch_shapes=[pltpu.VMEM((PACK_ROWS * per_row, SMALL), f32)],
        after=after,
        name="mlp_adam",
    )(quarter, *sums, *[flat_view(state) for state in gateup], *down)
    return [deep_view(value, gateup[0].shape) for value in new[:3]] + list(new[3:])


def attn_adam_kernel(
    core_ref, own_ref, rep_ref, other_ref, both_ref, wq, mq, sq, wo, mo, so, wkv, mkv, skv,
    wq_o, mq_o, sq_o, wo_o, mo_o, so_o, wkv_o, mkv_o, skv_o, *, rate_wide, rate_out,
):
    mine = core_ref[0] == 0

    def halves(span):
        own = own_ref[:, span].astype(f32) + rep_ref[:, span].astype(f32)
        other = other_ref[:, span].astype(f32) + both_ref[:, span].astype(f32)
        return jnp.where(mine, own, other), jnp.where(mine, other, own)

    for i, grad in enumerate(halves(slice(0, 512))):
        span = slice(512 * i, 512 * (i + 1))
        wq_o[:, span], mq_o[:, span], sq_o[:, span] = adamw(
            wq[:, span], mq[:, span], sq[:, span], grad, rate_wide, decay_rate
        )
    for i, grad in enumerate(halves(slice(512, 1024))):
        span = slice(512 * i, 512 * (i + 1))
        wo_o[:, span], mo_o[:, span], so_o[:, span] = adamw(
            wo[:, span], mo[:, span], so[:, span], grad, rate_out, decay_rate
        )
    first, second = halves(slice(1024, 1152))
    low_half = lax.broadcasted_iota(jnp.int32, first.shape, 1) < HEAD_DIM
    grads = (
        jnp.where(low_half, first, pltpu.roll(second, HEAD_DIM, 1)),
        jnp.where(low_half, pltpu.roll(first, HEAD_DIM, 1), second),
    )
    for i, grad in enumerate(grads):
        wkv_o[:, i, :], mkv_o[:, i, :], skv_o[:, i, :] = adamw(
            wkv[:, i, :], mkv[:, i, :], skv[:, i, :], grad, rate_wide, decay_rate
        )


def attn_adam(core, sums, query, out, keyval, rate_wide, rate_out, after=()):
    rows = 32
    grad = pl.BlockSpec((rows, sums[0].shape[1]), lambda i, core: (i, 0))
    flat = pl.BlockSpec((rows, query[0].shape[1]), lambda i, core: (i, 0))
    deep = pl.BlockSpec((rows, *keyval[0].shape[1:]), lambda i, core: (i, 0, 0))
    new = kernel_call(
        functools.partial(attn_adam_kernel, rate_wide=rate_wide, rate_out=rate_out),
        prefetch=1,
        grid=(query[0].shape[0] // rows,),
        in_specs=[grad] * 4 + [flat] * 6 + [deep] * 3,
        out_specs=[flat] * 6 + [deep] * 3,
        out_shape=[struct(state.shape, f32) for state in (*query, *out, *keyval)],
        after=after,
        name="attn_adam",
    )(core, *sums, *query, *out, *keyval)
    return new[:3], new[3:6], new[6:]


def swap_core(values):
    return lax.ppermute(values, "rep", CORE_SWAP)


def swap_replica(values):
    return lax.ppermute(values, "rep", REPLICA_SWAP)


def swap_replica_core(values):
    return lax.ppermute(values, "rep", BOTH_CORES_SWAP)


def swap_tp(values):
    return lax.ppermute(values, "tp", TP_SWAP)


def swap_core_tp(values):
    return lax.ppermute(values, ("rep", "tp"), CORE_TP_SWAP)


def swap_both(values):
    return lax.ppermute(values, ("rep", "tp"), BOTH_SWAP)


def scatter_sums(parts, held=(), after=()):
    pairs = []
    for k in range(2):
        own, core, replica, both = parts[4 * k : 4 * k + 4]
        pairs += [(own, swap_core(core)), (replica, swap_core(both))]
    mine, replica, tp, both, *copies = add_quads(pairs, held=held, after=after)
    return mine, swap_replica(replica), swap_tp(tp), swap_both(both), *copies


def spread(values):
    return lax.all_to_all(values, "grp", 0, 0, tiled=False)


def on_device(
    tokens,
    cotangent,
    offsets,
    w_query,
    moment_query,
    square_query,
    w_keyval,
    moment_keyval,
    square_keyval,
    w_out,
    moment_out,
    square_out,
    w_gateup,
    moment_gateup,
    square_gateup,
    w_down,
    moment_down,
    square_down,
    norm_gains,
    moment_gains,
    square_gains,
):
    sequences, own_len, width = tokens.shape
    core = lax.axis_index("rep") % 2
    core_list = core.reshape(1).astype(jnp.int32)
    place = jnp.stack([lax.axis_index("grp"), lax.axis_index("tp")]).astype(jnp.int32)

    wide_pack, kv_pack, kv_copies = pack_attn(
        core_list, w_query, w_out, w_keyval, norm_gains.T
    )
    wide_full = lax.all_gather(wide_pack, "grp", axis=0, tiled=True)
    kv_full = spread(kv_copies)
    quarter = (2 * core + lax.axis_index("rep") // 2).reshape(1).astype(jnp.int32)
    x_other = swap_core(tokens)
    dy_replica = swap_replica(cotangent)
    dy_parts = (cotangent, swap_core(cotangent), dy_replica, swap_replica_core(cotangent))
    offsets_other = swap_core(offsets)
    offsets_all = jnp.stack([offsets, offsets_other], axis=1).reshape(2 * sequences, GROUP)
    steps_in = jnp.arange(own_len, dtype=jnp.int32)
    starts = lax.dynamic_slice_in_dim(offsets_all, place[0], 1, 1)
    positions = (starts + steps_in[None, :]).reshape(2 * sequences * own_len)
    half_dim = HEAD_DIM // 2
    inverse = rope_base ** (-2.0 * jnp.arange(half_dim, dtype=f32) / HEAD_DIM)
    angles = positions.astype(f32)[:, None] * inverse[None, :]
    cos_part = jnp.cos(angles)
    sin_part = jnp.sin(angles)
    cos = jnp.concatenate([cos_part] * 4, axis=1)
    sin = jnp.concatenate([-sin_part, sin_part] * 2, axis=1)

    kv_one = project_kv(1, place, tokens, x_other, kv_full, cos, sin)
    kv_zero = project_kv(
        0, place, tokens, x_other, kv_full, cos, sin, after=(kv_one[0], dy_replica)
    )
    h_turned = [kv_zero[1], kv_one[1]]
    kvs = {1: spread(kv_one[2])}
    kvs[0] = spread(kv_zero[2])
    dy_t = transposed(place, dy_parts, after=(kv_zero[0],))
    mlp_pack = pack_mlp(quarter, w_gateup, w_down, after=(kvs[1], dy_t))
    mlp_full = lax.all_gather(mlp_pack, "grp", axis=0, tiled=True)
    q_one = project_q(1, place, kv_one[0], wide_full, cos, sin, after=(mlp_pack,))
    one = attend(1, offsets_all, place, q_one, kvs[1], wide_full)
    one_share = add_low(one[2], swap_core(one[3]))
    q_zero = project_q(0, place, kv_zero[0], wide_full, cos, sin, after=(one[0],))
    qs = [q_zero, q_one]
    received = swap_tp(one_share)
    zero = attend(0, offsets_all, place, qs[0], kvs[0], wide_full, after=(one_share,))
    os_ = [zero[0], one[0]]
    lses = [zero[1], one[1]]
    zero_part = add_low(zero[2], received)
    mid, h_two = middle(place, tokens, zero_part, swap_core(zero[3]), kv_full)
    h_parts = []
    for first, second in ((h_two, swap_replica(h_two)), (swap_tp(h_two), swap_both(h_two))):
        h_parts += [first, swap_core(first), second, swap_core(second)]
    side, mlp_sums = mlp(place, h_parts, dy_parts, dy_t, mlp_full)
    mlp_own = lax.psum_scatter(mlp_sums, "grp", scatter_dimension=0, tiled=True)

    sums = scatter_sums(mlp_back(side, mlp_full, 0, 2))
    out_parts = mlp_back(side, mlp_full, 2, 1, after=(sums[0],))
    da = middle_back(place, sums, mid, cotangent, kv_full, after=(out_parts[0],))
    da_tp = swap_tp(da)
    da_parts = [da, swap_core(da)]

    def back_of(k, after=()):
        return attend_back(
            k, offsets_all, place, da_parts[2 * k], da_parts[2 * k + 1], wide_full, qs[k], kvs[k],
            os_[k], lses[k], cos, sin, after=after,
        )

    first_back = back_of(0)
    *out_shares, da_tp = scatter_sums(out_parts, held=(da_tp,), after=(first_back[0],))
    da_parts += [da_tp, swap_core(da_tp)]
    out_sums = out_grads(da_parts, os_, after=(out_shares[0],))
    out_own = lax.psum_scatter(out_sums, "grp", scatter_dimension=0, tiled=True)
    second_back = back_of(1, after=(out_sums,))
    dqs = [first_back[0], second_back[0]]
    gain_two, mlp_replica = second_gain_terms(
        mlp_pack, mlp_own, swap_replica(mlp_own), after=(second_back[0],)
    )
    first_right = right_side(0, place, spread(first_back[1]), cos, sin, after=(gain_two,))
    q_sums = query_grads(place, h_turned, dqs, after=(first_right,))
    rate_wide = 2.0 * D ** (-0.5)
    rate_out = 2.0 * max(1, 2 * D // LENGTH) ** (-0.5)
    rate_down = 2.0 * FF ** (-0.5)
    new_mlp = mlp_adam(
        quarter,
        (mlp_own, mlp_replica, swap_core(mlp_own), swap_core(mlp_replica)),
        (w_gateup, moment_gateup, square_gateup),
        (w_down, moment_down, square_down),
        rate_wide,
        rate_down,
        after=(q_sums[0],),
    )
    layer_mine = layer_part(mid, out_shares, after=(new_mlp[-1],))
    x_terms = [q_sums[0]] + [along_x(q_sums[i], i) for i in range(1, 4)]
    kv_sums, second_right = keyval_grads(
        place, h_turned, first_right, spread(second_back[1]), cos, sin, after=(layer_mine,)
    )
    layer_other = swap_tp(layer_mine)
    q_lines = line_sums(place, x_terms, after=(kv_sums, layer_other))
    rights = [first_right, second_right]
    gain_replica = swap_replica(gain_two)
    own_part, other_part = project_back(
        dqs, rights, wide_full, kv_full, after=(q_lines[0], gain_replica)
    )
    dh_share = add_low(own_part, swap_core(other_part))
    dh_received = swap_tp(dh_share)
    z_terms = [q_lines[0]] + [along_z(q_lines[i], i) for i in range(1, 4)]
    own = final_sums(z_terms, out_own, spread(kv_sums), after=(dh_share,))

    replica = swap_replica(own)
    input_grad, layer_out = row_outputs(
        place, layer_mine, layer_other, (da, da_parts[2]), dh_share, dh_received, tokens, kv_full,
        after=(own,),
    )
    gain_own = gain_terms(
        wide_pack, kv_pack, (own, replica), (gain_two, gain_replica), after=(input_grad,)
    )
    new_query, new_out, new_keyval = attn_adam(
        core_list,
        (own, replica, swap_core(own), swap_core(replica)),
        (w_query, moment_query, square_query),
        (w_out, moment_out, square_out),
        (w_keyval, moment_keyval, square_keyval),
        rate_wide,
        rate_out,
        after=(gain_own,),
    )
    new_gains = gain_adam(
        (gain_own, swap_core(gain_own), swap_tp(gain_own), swap_core_tp(gain_own)),
        (norm_gains, moment_gains, square_gains),
    )
    return (
        layer_out,
        input_grad,
        *new_query,
        *new_keyval,
        *new_out,
        *new_mlp,
        *new_gains,
    )


def solution(mesh):
    rows = P("rep", "grp", None)
    flat = P("grp", "tp")
    deep = P("grp", None, "tp")
    states = (flat,) * 3 + (deep,) * 3 + (flat,) * 3 + (deep,) * 3 + (flat,) * 3
    states += (P("grp", None),) * 3
    return jax.shard_map(
        on_device,
        mesh=mesh,
        in_specs=(rows, rows, P("rep", None)) + states,
        out_specs=(rows, rows) + states,
        check_vma=False,
    )
```

```python
import functools

import jax
import jax.numpy as jnp
from jax import lax
from jax.experimental import pallas as pl
from jax.experimental.layout import Layout, with_layout_constraint
from jax.experimental.pallas import tpu as pltpu
from jax.sharding import PartitionSpec as P

D = 2048
HEAD_DIM = 64
FF = 5632
LENGTH = 2048
STEP = 10
GROUP = 16
SPAN = 128
TILE = 256

norm_epsilon = 1e-05
rope_base = 10000.0
neg_large = -1e30
beta_first = 0.9
beta_second = 0.95
adam_epsilon = 1e-08
decay_rate = 0.1

bf16 = jnp.bfloat16
f32 = jnp.float32

VMEM_LIMIT = 63 * 1024 * 1024

CORE_SWAP = [(0, 1), (1, 0), (2, 3), (3, 2)]
REPLICA_SWAP = [(0, 2), (1, 3), (2, 0), (3, 1)]
BOTH_CORES_SWAP = [(0, 3), (1, 2), (2, 1), (3, 0)]
TP_SWAP = [(0, 1), (1, 0)]
CORE_TP_SWAP = [(2 * r + t, 2 * (r ^ 1) + (1 - t)) for r in range(4) for t in range(2)]
BOTH_SWAP = [(2 * r + t, 2 * (r ^ 2) + (1 - t)) for r in range(4) for t in range(2)]


def struct(shape, dtype):
    return jax.ShapeDtypeStruct(shape, dtype)


def kernel_call(
    kernel, *, name, out_shape, grid=(), in_specs=None, out_specs=None, scratch_shapes=(), prefetch=0,
    after=(),
):
    first = prefetch + len(in_specs)

    def body(*refs):
        kernel(*refs[:first], *refs[first + len(after) :])

    grid_spec = pltpu.PrefetchScalarGridSpec(
        num_scalar_prefetch=prefetch,
        grid=grid,
        in_specs=list(in_specs) + [pl.BlockSpec(memory_space=pl.ANY)] * len(after),
        out_specs=out_specs,
        scratch_shapes=list(scratch_shapes),
    )
    call = pl.pallas_call(
        body,
        grid_spec=grid_spec,
        out_shape=out_shape,
        compiler_params=pltpu.CompilerParams(vmem_limit_bytes=VMEM_LIMIT),
        name=name,
    )
    return lambda *args: call(*args, *after)


def dot_nn(left, right):
    return lax.dot_general(left, right, (((1,), (0,)), ((), ())), preferred_element_type=f32)


def dot_nt(left, right):
    return lax.dot_general(left, right, (((1,), (1,)), ((), ())), preferred_element_type=f32)


def dot_tn(left, right):
    return lax.dot_general(left, right, (((0,), (0,)), ((), ())), preferred_element_type=f32)


def adamw(weight, moment, square, grad, rate, decay):
    moment = beta_first * moment + (1.0 - beta_first) * grad
    square = beta_second * square + (1.0 - beta_second) * grad * grad
    fix_first = 1.0 - beta_first**STEP
    fix_second = 1.0 - beta_second**STEP
    update = moment / fix_first / (jnp.sqrt(square / fix_second) + adam_epsilon)
    return (weight * (1.0 - rate * decay) - rate * update, moment, square)


def norm_back(upstream, gain, normed, scale):
    weighted = upstream * gain
    return scale * (weighted - normed * jnp.mean(weighted * normed, axis=-1, keepdims=True))


def partner(values):
    lane = lax.broadcasted_iota(jnp.int32, values.shape, 1)
    up = pltpu.roll(values, 96, 1)
    down = pltpu.roll(values, 32, 1)
    return jnp.where(lane % HEAD_DIM < HEAD_DIM // 2, up, down)


def row_of(block):
    return jnp.concatenate([block[i : i + 1, :] for i in range(GROUP)], axis=1)


def rms_scale(values):
    return lax.rsqrt(jnp.mean(values * values, axis=-1, keepdims=True) + norm_epsilon)


def gain_row(gain_ref, index):
    return row_of(gain_ref[:, index, :].astype(f32))


GAIN_SPEC = pl.BlockSpec((GROUP, 16, 128), lambda *_: (0, 8, 0))
WQ_SPEC = pl.BlockSpec((D, 512), lambda *_: (0, 0))
WO_SPEC = pl.BlockSpec((D, 512), lambda *_: (0, 1))
WKV_SPEC = pl.BlockSpec((GROUP, 128, 128), lambda *_: (0, 0, 0))
ROWS_SPEC = pl.BlockSpec((SPAN, D), lambda *_: (0, 0))


def half_of(place, k):
    return place[1] if k == 0 else 1 - place[1]


STRIP = 128
STRIP_SPEC = pl.BlockSpec((STRIP, D), lambda i, *_: (i, 0))
HALF_SPEC = pl.BlockSpec((SPAN // 2, D), lambda i, *_: (i, 0))


def seq_strip(k):
    return pl.BlockSpec((1, STRIP, D), lambda i, *refs: (half_of(refs[-1], k), i, 0))


def seq_spec(k):
    return pl.BlockSpec((1, SPAN, D), lambda *ids: (half_of(ids[-1], k), 0, 0))


def turn_spec(k):
    return pl.BlockSpec((SPAN, 128), lambda i, *refs: (2 * half_of(refs[-1], k) + i, 0))


def whole_spec(shape):
    return pl.BlockSpec(shape, lambda *_: (0,) * len(shape))


def pack_attn_kernel(core_ref, wq_ref, wo_ref, wkv_ref, gain_ref, wide_ref, kv_ref, copies_ref):
    lane = lax.broadcasted_iota(jnp.int32, (128, 128), 1)
    low_half = lane < HEAD_DIM
    first_core = core_ref[0] == 0
    key = jnp.where(first_core, wkv_ref[:, 0, :], pltpu.roll(wkv_ref[:, 0, :], HEAD_DIM, 1))
    value = jnp.where(first_core, pltpu.roll(wkv_ref[:, 1, :], HEAD_DIM, 1), wkv_ref[:, 1, :])
    kv = jnp.where(low_half, key, value).astype(bf16)
    wide_ref[:, :512] = wq_ref[...].astype(bf16)
    wide_ref[:, 512:] = wo_ref[...].astype(bf16)
    kv_ref[...] = kv
    gains = jnp.concatenate([gain_ref[...], jnp.zeros((14, 128), f32)], axis=0).astype(bf16)
    for g in range(GROUP):
        copies_ref[g, :128, :] = kv
        copies_ref[g, 128:, :] = gains


def pack_attn(core, w_query, w_out, w_keyval, gains):
    rows = w_query.shape[0]
    half = pl.BlockSpec((rows, 512), lambda i, core: (0, core[0]))
    shapes = [(rows, 1024), (rows, 128), (GROUP, rows + 16, 128)]
    return kernel_call(
        pack_attn_kernel,
        prefetch=1,
        grid=(1,),
        in_specs=[half, half, whole_spec(w_keyval.shape), whole_spec(gains.shape)],
        out_specs=[whole_spec(shape) for shape in shapes],
        out_shape=[struct(shape, bf16) for shape in shapes],
        name="pack_attn",
    )(core, w_query, w_out, w_keyval, gains)


def project_kv_kernel(
    place_ref, own_ref, other_ref, wkv_ref, gain_ref, cos_ref, sin_ref, h_ref, turned_ref, kv_ref
):
    mine = pl.program_id(0) == 0
    x = jnp.where(mine, own_ref[0].astype(f32), other_ref[0].astype(f32))
    h = (x * rms_scale(x) * gain_row(gain_ref, 0)).astype(bf16)
    h_ref[...] = h
    low_half = lax.broadcasted_iota(jnp.int32, (SPAN, 128), 1) < HEAD_DIM
    keyval = dot_nn(h, wkv_ref[...].reshape(D, 128))
    turned = keyval * cos_ref[...] + partner(keyval) * sin_ref[...]
    kv = jnp.where(low_half, turned, keyval).astype(bf16)
    kv_ref[...] = jnp.broadcast_to(kv[None], (GROUP, SPAN, 128))
    turned_ref[...] = h.T


def project_kv(k, place, x_own, x_other, kv_full, cos, sin, after=()):
    return kernel_call(
        project_kv_kernel,
        prefetch=1,
        grid=(2,),
        in_specs=[seq_spec(k), seq_spec(k), WKV_SPEC, GAIN_SPEC, turn_spec(k), turn_spec(k)],
        out_specs=[
            pl.BlockSpec((SPAN, D), lambda i, *_: (i, 0)),
            pl.BlockSpec((D, SPAN), lambda i, *_: (0, i)),
            pl.BlockSpec((GROUP, SPAN, 128), lambda i, *_: (0, i, 0)),
        ],
        out_shape=[
            struct((2 * SPAN, D), bf16),
            struct((D, 2 * SPAN), bf16),
            struct((GROUP, 2 * SPAN, 128), bf16),
        ],
        after=after,
        name="project_kv",
    )(place, x_own, x_other, kv_full, kv_full, cos, sin)


def project_q_kernel(place_ref, h_ref, wq_ref, cos_ref, sin_ref, q_ref):
    cos = cos_ref[...]
    sin = sin_ref[...]
    low_half = lax.broadcasted_iota(jnp.int32, cos.shape, 1) < HEAD_DIM
    query = dot_nn(h_ref[...], wq_ref[...])
    for pair in range(4):
        block = query[:, pair * 128 : (pair + 1) * 128]
        turned = (block * cos + partner(block) * sin) * (HEAD_DIM**-0.5)
        q_ref[2 * pair] = jnp.where(low_half, turned, 0.0).astype(bf16)
        q_ref[2 * pair + 1] = jnp.where(
            low_half, pltpu.roll(turned, HEAD_DIM, 1), 0.0
        ).astype(bf16)


def project_q(k, place, h, wide_full, cos, sin, after=()):
    turn = pl.BlockSpec((2 * SPAN, 128), lambda i, place: (half_of(place, k), 0))
    return kernel_call(
        project_q_kernel,
        prefetch=1,
        grid=(1,),
        in_specs=[whole_spec((2 * SPAN, D)), WQ_SPEC, turn, turn],
        out_specs=whole_spec((8, 2 * SPAN, 128)),
        out_shape=struct((8, 2 * SPAN, 128), bf16),
        after=after,
        name="project_q",
    )(place, h, wide_full, cos, sin)


CHUNK = 512
BACK_CHUNK = 1024


def causal_offsets():
    key = lax.broadcasted_iota(jnp.int32, (128, 256), 0)
    query = lax.broadcasted_iota(jnp.int32, (128, 256), 1) % SPAN
    return key - query


def masked(raw, differ, own, off_ref, seq, c):
    parts = []
    blocks = raw.shape[0] // 128
    for j in range(blocks):
        allowed = differ <= own - off_ref[seq, blocks * c + j]
        parts.append(jnp.where(allowed, raw[j * 128 : (j + 1) * 128], neg_large))
    return jnp.concatenate(parts, axis=0)


def attend_kernel(
    off_ref, place_ref, q_ref, kv_ref, wo_ref, o_ref, lse_ref, own_ref, other_ref, kvt, scores, *, k
):
    step = pl.program_id(0)
    seq = 2 * half_of(place_ref, k) + step
    kvt[...] = kv_ref[...].reshape(LENGTH, 128).T
    own = off_ref[seq, place_ref[0]]
    differ = causal_offsets()
    blocks = CHUNK // 128

    for pair in range(4):
        q = q_ref[2 * pair : 2 * pair + 2].reshape(256, 128)
        top = jnp.full((1, 256), neg_large, f32)
        for c in range(LENGTH // CHUNK):
            raw = dot_nt(kv_ref[blocks * c : blocks * (c + 1)].reshape(CHUNK, 128), q)
            score = masked(raw, differ, own, off_ref, seq, c)
            scores[pair % 2, c * CHUNK : (c + 1) * CHUNK, :] = score
            top = jnp.maximum(top, jnp.max(score, axis=0, keepdims=True))
        total = jnp.zeros((1, 256), f32)
        mixed = jnp.zeros((128, 256), f32)
        for c in range(LENGTH // CHUNK):
            weight = jnp.exp(scores[pair % 2, c * CHUNK : (c + 1) * CHUNK, :] - top)
            total = total + jnp.sum(weight, axis=0, keepdims=True)
            mixed = mixed + dot_nn(kvt[:, c * CHUNK : (c + 1) * CHUNK], weight.astype(bf16))
        out = (mixed[HEAD_DIM:, :] / total).T
        o_ref[pair] = jnp.concatenate([out[:SPAN], out[SPAN:]], axis=1).astype(bf16)
        lse_ref[0, pair : pair + 1, :] = top + jnp.log(total)

    heads = jnp.concatenate([o_ref[i] for i in range(4)], axis=1)
    part = dot_nt(heads, wo_ref[...]).astype(bf16)

    @pl.when(step == 0)
    def _():
        own_ref[...] = part

    @pl.when(step == 1)
    def _():
        other_ref[...] = part


def attend(k, offsets, place, q, kv_all, wo_full, after=()):
    grid_spec = dict(
        prefetch=2,
        grid=(2,),
        in_specs=[
            pl.BlockSpec((8, SPAN, 128), lambda i, *_: (0, i, 0)),
            pl.BlockSpec((GROUP, SPAN, 128), lambda i, *_: (0, i, 0)),
            WO_SPEC,
        ],
        out_specs=[
            pl.BlockSpec((4, SPAN, 128), lambda i, *_: (0, i, 0)),
            pl.BlockSpec((1, 4, 256), lambda i, *_: (i, 0, 0)),
            ROWS_SPEC,
            ROWS_SPEC,
        ],
        scratch_shapes=[pltpu.VMEM((128, LENGTH), bf16), pltpu.VMEM((2, LENGTH, 256), f32)],
    )
    return kernel_call(
        functools.partial(attend_kernel, k=k),
        **grid_spec,
        out_shape=[
            struct((4, 2 * SPAN, 128), bf16),
            struct((2, 4, 256), f32),
            struct((SPAN, D), bf16),
            struct((SPAN, D), bf16),
        ],
        after=after,
        name="attend",
    )(offsets, place, q, kv_all, wo_full)


def share_kernel(own_ref, other_ref, out_ref):
    out_ref[...] = (own_ref[...].astype(f32) + other_ref[...].astype(f32)).astype(bf16)


def add_low(first, second, after=()):
    rows, width = first.shape
    block = pl.BlockSpec((128, width), lambda i: (i, 0))
    return kernel_call(
        share_kernel,
        grid=(rows // 128,),
        in_specs=[block, block],
        out_specs=block,
        out_shape=struct(first.shape, bf16),
        after=after,
        name="add_low",
    )(first, second)


def middle_kernel(place_ref, x_ref, one_ref, two_ref, gain_ref, mid_ref, h_ref):
    total = one_ref[...].astype(f32) + two_ref[...].astype(f32)
    mid = x_ref[0].astype(f32) + total
    mid_ref[...] = mid
    h_ref[...] = (mid * rms_scale(mid) * gain_row(gain_ref, 1)).astype(bf16)


def middle(place, x_own, one, two, attn_full):
    return kernel_call(
        middle_kernel,
        prefetch=1,
        grid=(SPAN // STRIP,),
        in_specs=[seq_strip(0), STRIP_SPEC, STRIP_SPEC, GAIN_SPEC],
        out_specs=[STRIP_SPEC, STRIP_SPEC],
        out_shape=[struct((SPAN, D), f32), struct((SPAN, D), bf16)],
        name="middle",
    )(place, x_own, one, two, attn_full)


def sum_rows(refs):
    return sum(ref[...].astype(f32) for ref in refs)


def middle_back_kernel(place_ref, p0, p1, p2, p3, mid_ref, dy_ref, gain_ref, da_ref):
    upstream = sum_rows((p0, p1, p2, p3))
    mid = mid_ref[...]
    scale = rms_scale(mid)
    d_norm = norm_back(upstream, gain_row(gain_ref, 1), mid * scale, scale)
    da_ref[...] = (dy_ref[0].astype(f32) + d_norm).astype(bf16)


def middle_back(place, parts, mid, dy_own, attn_full, after=()):
    return kernel_call(
        middle_back_kernel,
        prefetch=1,
        grid=(SPAN // STRIP,),
        in_specs=[STRIP_SPEC] * 5 + [seq_strip(0), GAIN_SPEC],
        out_specs=STRIP_SPEC,
        out_shape=struct((SPAN, D), bf16),
        after=after,
        name="middle_back",
    )(place, *parts, mid, dy_own, attn_full)


def layer_part_kernel(mid_ref, p0, p1, p2, p3, out_ref):
    out_ref[...] = (mid_ref[...] + sum_rows((p0, p1, p2, p3))).astype(bf16)


def layer_part(mid, parts, after=()):
    return kernel_call(
        layer_part_kernel,
        grid=(SPAN // STRIP,),
        in_specs=[STRIP_SPEC] * 5,
        out_specs=STRIP_SPEC,
        out_shape=struct((SPAN, D), bf16),
        after=after,
        name="layer_part",
    )(mid, *parts)


def row_outputs_kernel(
    place_ref, mine_ref, other_ref, da0, da1, s0, s1, r0, r1, x_ref, gain_ref, out_ref, layer_ref
):
    layer_ref[half_of(place_ref, 0)] = mine_ref[...]
    layer_ref[half_of(place_ref, 1)] = other_ref[...]
    gain = gain_row(gain_ref, 0)
    for k, (da_ref, share, received) in enumerate(((da0, s0, r1), (da1, s1, r0))):
        upstream = share[...].astype(f32) + received[...].astype(f32)
        m = half_of(place_ref, k)
        x = x_ref[m].astype(f32)
        scale = rms_scale(x)
        out_ref[m] = da_ref[...].astype(f32) + norm_back(upstream, gain, x * scale, scale)


def row_outputs(place, mine, other, das, share, received, x_own, kv_full, after=()):
    steps = 2
    rows = SPAN // steps
    block = pl.BlockSpec((rows, D), lambda i, *_: (i, 0))
    second = pl.BlockSpec((rows, D), lambda i, *_: (steps + i, 0))
    seqs = pl.BlockSpec((2, rows, D), lambda i, *_: (0, i, 0))
    return kernel_call(
        row_outputs_kernel,
        prefetch=1,
        grid=(steps,),
        in_specs=[block] * 5 + [second, block, second, seqs, GAIN_SPEC],
        out_specs=[seqs, seqs],
        out_shape=[struct((2, SPAN, D), f32), struct((2, SPAN, D), bf16)],
        after=after,
        name="row_outputs",
    )(place, mine, other, *das, share, share, received, received, x_own, kv_full)


PACK_ROWS = 16
ALL_ROWS = 8 * SPAN
SMALL = 128
WINDOW_TILES = 6
WIDTH = 3 * WINDOW_TILES * SMALL
WINDOW_STARTS = (0, 6, 11, 16)
FIRST_OWN = (0, 6, 12, 17, 22)


def window_start(quarter):
    return jnp.where(quarter < 2, 6 * quarter, 5 * quarter + 1)


def packed_column(tile, kind):
    return 3 * TILE * (tile // 2) + TILE * kind + SMALL * (tile % 2)


def transpose_kernel(place_ref, *refs):
    parts, out_ref = refs[:-1], refs[-1]
    for k in range(2):
        for i, ref in enumerate(parts):
            start = (len(parts) * k + i) * SPAN
            out_ref[:, start : start + SPAN] = ref[half_of(place_ref, k)].T


def transposed(place, parts, after=()):
    seqs = pl.BlockSpec((2, SPAN, 512), lambda i, *_: (0, 0, i))
    return kernel_call(
        transpose_kernel,
        prefetch=1,
        grid=(D // 512,),
        in_specs=[seqs] * 4,
        out_specs=pl.BlockSpec((512, ALL_ROWS), lambda i, *_: (i, 0)),
        out_shape=struct((D, ALL_ROWS), bf16),
        after=after,
        name="transposed",
    )(place, *parts)


def mlp_kernel(place_ref, *refs):
    h_parts, dy_parts, dyt_ref, w_ref = refs[:8], refs[8:12], refs[12], refs[13]
    side_ref, sum_ref, h, ht, dy, dyt, sems = refs[14:]
    step = pl.program_id(0)

    def part_copies():
        copies = []
        for i, ref in enumerate(h_parts):
            spot = h.at[i * SPAN : (i + 1) * SPAN]
            copies.append(pltpu.make_async_copy(ref, spot, sems.at[i]))
        for k in range(2):
            for i, ref in enumerate(dy_parts):
                number = 4 * k + i
                spot = dy.at[number * SPAN : (number + 1) * SPAN]
                source = ref.at[half_of(place_ref, k)]
                copies.append(pltpu.make_async_copy(source, spot, sems.at[8 + number]))
        return copies

    turned_copy = pltpu.make_async_copy(dyt_ref, dyt, sems.at[16])

    def work(start):
        rows = slice(start, start + 256)
        both = dot_nn(h[rows, :], w_ref[:, : 2 * TILE])
        upstream = dot_nn(dy[rows, :], w_ref[:, 2 * TILE :])
        gate = both[:, :TILE]
        up = both[:, TILE:]
        sigmoid = jax.nn.sigmoid(gate)
        active = gate * sigmoid
        side_ref[rows, :TILE] = (
            upstream * up * (sigmoid * (1.0 + gate * (1.0 - sigmoid)))
        ).astype(bf16)
        side_ref[rows, TILE : 2 * TILE] = (upstream * active).astype(bf16)
        side_ref[rows, 2 * TILE :] = (active * up).astype(bf16)

    @pl.when(step == 0)
    def _():
        copies = part_copies()
        for i in range(8):
            copies[i].start()
            copies[8 + i].start()
        turned_copy.start()
        for start in range(0, ALL_ROWS, 256):
            for i in range(start // SPAN, start // SPAN + 2):
                copies[i].wait()
                copies[8 + i].wait()
            work(start)
        ht[...] = h[...].T
        turned_copy.wait()

    @pl.when(step > 0)
    def _():
        for start in range(0, ALL_ROWS, 256):
            work(start)

    sum_ref[:, : 2 * TILE] = dot_nn(ht[...], side_ref[:, : 2 * TILE]).astype(bf16)
    sum_ref[:, 2 * TILE :] = dot_nn(dyt[...], side_ref[:, 2 * TILE :]).astype(bf16)


def mlp(place, h_parts, dy_parts, dy_t, w_full, after=()):
    width = 3 * TILE
    return kernel_call(
        mlp_kernel,
        prefetch=1,
        grid=(WIDTH // width,),
        in_specs=[pl.BlockSpec(memory_space=pl.ANY)] * 13
        + [pl.BlockSpec((D, width), lambda i, *_: (0, i))],
        out_specs=[
            pl.BlockSpec((ALL_ROWS, width), lambda i, *_: (0, i)),
            pl.BlockSpec((D, width), lambda i, *_: (0, i)),
        ],
        out_shape=[struct((ALL_ROWS, WIDTH), bf16), struct((D, WIDTH), bf16)],
        scratch_shapes=[
            pltpu.VMEM((ALL_ROWS, D), bf16),
            pltpu.VMEM((D, ALL_ROWS), bf16),
            pltpu.VMEM((ALL_ROWS, D), bf16),
            pltpu.VMEM((D, ALL_ROWS), bf16),
            pltpu.SemaphoreType.DMA((17,)),
        ],
        after=after,
        name="mlp",
    )(place, *h_parts, *dy_parts, dy_t, w_full)


def mlp_back_kernel(side_ref, w_ref, *outs, first, count):
    total = jnp.zeros((ALL_ROWS, w_ref.shape[0]), f32)
    for column in range(0, WIDTH, 3 * TILE):
        span = slice(column + first * TILE, column + (first + count) * TILE)
        total = total + dot_nt(side_ref[:, span], w_ref[:, span])
    for out, i in zip(outs, range(8)):
        out[...] = total[i * SPAN : (i + 1) * SPAN].astype(bf16)


def mlp_back(side, w_full, first, count, after=()):
    return kernel_call(
        functools.partial(mlp_back_kernel, first=first, count=count),
        grid=(D // 512,),
        in_specs=[whole_spec((ALL_ROWS, WIDTH)), pl.BlockSpec((512, WIDTH), lambda i: (i, 0))],
        out_specs=[pl.BlockSpec((SPAN, 512), lambda i: (0, i))] * 8,
        out_shape=[struct((SPAN, D), bf16)] * 8,
        after=after,
        name="mlp_back",
    )(side, w_full)


def quad_kernel(*refs):
    count = (len(refs) + 4) // 2
    inputs, outs = refs[:count], refs[count:]
    for i in range(4):
        total = inputs[2 * i][...].astype(f32) + inputs[2 * i + 1][...].astype(f32)
        outs[i][...] = total.astype(bf16)
    for source, target in zip(inputs[8:], outs[4:]):
        target[...] = source[...]


def add_quads(pairs, held=(), after=()):
    count = len(held)
    return kernel_call(
        quad_kernel,
        grid=(2,),
        in_specs=[HALF_SPEC] * (8 + count),
        out_specs=[HALF_SPEC] * (4 + count),
        out_shape=[struct((SPAN, D), bf16)] * (4 + count),
        after=after,
        name="add_quads",
    )(*[value for pair in pairs for value in pair], *held)


def attend_back_kernel(
    off_ref, place_ref, own_ref, other_ref, wo_ref, q_ref, kv_ref, o_ref, lse_ref, cos_ref,
    sin_ref, dq_ref, dkv_ref, kvt, d_heads, dkv, *, k,
):
    step = pl.program_id(0)
    seq = 2 * half_of(place_ref, k) + step
    kvt[...] = kv_ref[...].reshape(LENGTH, 128).T
    dkv[...] = jnp.zeros_like(dkv)
    d_out_rows = jnp.where(step == 0, own_ref[...].astype(f32), other_ref[...].astype(f32))
    d_all = dot_nn(d_out_rows.astype(bf16), wo_ref[...])
    for pair in range(4):
        d_heads[pair] = d_all[:, pair * 128 : (pair + 1) * 128].astype(bf16).astype(f32)
    own = off_ref[seq, place_ref[0]]
    differ = causal_offsets()
    lane = lax.broadcasted_iota(jnp.int32, (SPAN, 128), 1)
    high_half = lane >= HEAD_DIM
    cos = cos_ref[...]
    sin = sin_ref[...]
    blocks = BACK_CHUNK // 128

    for pair in range(4):
        q = q_ref[2 * pair : 2 * pair + 2].reshape(256, 128)
        d_out = d_heads[pair]
        first = jnp.where(high_half, pltpu.roll(d_out, HEAD_DIM, 1), 0.0).astype(bf16)
        second = jnp.where(high_half, d_out, 0.0).astype(bf16)
        d_o = jnp.concatenate([first, second], axis=0)
        dots = (d_out * o_ref[pair].astype(f32)).T
        inner = jnp.concatenate(
            [
                jnp.sum(dots[:HEAD_DIM], axis=0, keepdims=True),
                jnp.sum(dots[HEAD_DIM:], axis=0, keepdims=True),
            ],
            axis=1,
        )
        lse = lse_ref[0, pair : pair + 1, :]
        d_query = jnp.zeros((128, 256), f32)
        for c in range(LENGTH // BACK_CHUNK):
            kv = kv_ref[blocks * c : blocks * (c + 1)].reshape(BACK_CHUNK, 128)
            score = masked(dot_nt(kv, q), differ, own, off_ref, seq, c)
            prob = jnp.exp(score - lse)
            d_prob = dot_nt(kv, d_o)
            d_score = (prob * (d_prob - inner)).astype(bf16)
            span = slice(c * BACK_CHUNK, (c + 1) * BACK_CHUNK)
            dkv[span, :] += dot_nn(d_score, q) + dot_nn(prob.astype(bf16), d_o)
            d_query = d_query + dot_nn(kvt[:, span], d_score)
        turned = d_query[:HEAD_DIM, :].T
        block = jnp.concatenate([turned[:SPAN], turned[SPAN:]], axis=1)
        block = (block * cos - partner(block) * sin) * (HEAD_DIM**-0.5)
        dq_ref[pair] = block.astype(bf16)

    dkv_ref[...] = dkv[...].astype(bf16).reshape(GROUP, SPAN, 128)


def attend_back(k, offsets, place, da_own, da_other, wo_full, q, kv_all, o, lse, cos, sin, after=()):
    turn = turn_spec(k)
    heads = pl.BlockSpec((4, SPAN, 128), lambda i, *_: (0, i, 0))
    group = pl.BlockSpec((GROUP, SPAN, 128), lambda i, *_: (0, i, 0))
    grid_spec = dict(
        prefetch=2,
        grid=(2,),
        in_specs=[
            ROWS_SPEC,
            ROWS_SPEC,
            WO_SPEC,
            pl.BlockSpec((8, SPAN, 128), lambda i, *_: (0, i, 0)),
            group,
            heads,
            pl.BlockSpec((1, 4, 256), lambda i, *_: (i, 0, 0)),
            turn,
            turn,
        ],
        out_specs=[heads, group],
        scratch_shapes=[
            pltpu.VMEM((128, LENGTH), bf16),
            pltpu.VMEM((4, SPAN, 128), f32),
            pltpu.VMEM((LENGTH, 128), f32),
        ],
    )
    return kernel_call(
        functools.partial(attend_back_kernel, k=k),
        **grid_spec,
        out_shape=[
            struct((4, 2 * SPAN, 128), bf16),
            struct((GROUP, 2 * SPAN, 128), bf16),
        ],
        after=after,
        name="attend_back",
    )(offsets, place, da_own, da_other, wo_full, q, kv_all, o, lse, cos, sin)


def out_grads_kernel(a0, a1, a2, a3, o0_ref, o1_ref, out_ref):
    heads = jnp.concatenate(
        [jnp.concatenate([ref[i] for i in range(4)], axis=1) for ref in (o0_ref, o1_ref)],
        axis=0,
    )
    rows = jnp.concatenate([ref[...] for ref in (a0, a1, a2, a3)], axis=0)
    out_ref[...] = dot_tn(rows, heads).astype(bf16)


def out_grads(da_parts, o_parts, after=()):
    return kernel_call(
        out_grads_kernel,
        grid=(4,),
        in_specs=[pl.BlockSpec((SPAN, 512), lambda i: (0, i))] * 4
        + [whole_spec((4, 2 * SPAN, 128))] * 2,
        out_specs=pl.BlockSpec((512, 512), lambda i: (i, 0)),
        out_shape=struct((D, 512), bf16),
        after=after,
        name="out_grads",
    )(*da_parts, *o_parts)


def right_kernel(place_ref, dkv_ref, cos_ref, sin_ref, out_ref):
    lane = lax.broadcasted_iota(jnp.int32, (SPAN, 128), 1)
    total = jnp.sum(dkv_ref[...].astype(f32), axis=0)
    turned = total * cos_ref[...] - partner(total) * sin_ref[...]
    out_ref[...] = jnp.where(lane < HEAD_DIM, turned, total).astype(bf16)


def right_side(k, place, dkv, cos, sin, after=()):
    return kernel_call(
        right_kernel,
        prefetch=1,
        grid=(2,),
        in_specs=[
            pl.BlockSpec((GROUP, SPAN, 128), lambda i, *_: (0, i, 0)),
            turn_spec(k),
            turn_spec(k),
        ],
        out_specs=pl.BlockSpec((SPAN, 128), lambda i, *_: (i, 0)),
        out_shape=struct((2 * SPAN, 128), bf16),
        after=after,
        name="right_side",
    )(place, dkv, cos, sin)


def query_grads_kernel(place_ref, h0_ref, h1_ref, q0_ref, q1_ref, *outs):
    rights = [jnp.concatenate([ref[i] for i in range(4)], axis=1) for ref in (q0_ref, q1_ref)]
    for step in range(4):
        for z in range(4):
            owner = z * 4 + (place_ref[0] + step) % 4
            rows = pl.ds(pl.multiple_of(owner * 128, 128), 128)
            total = dot_nn(h0_ref[rows, :], rights[0]) + dot_nn(h1_ref[rows, :], rights[1])
            outs[step][z] = total.astype(bf16)


def query_grads(place, h_turned, dqs, after=()):
    args = (*h_turned, *dqs)
    shape = (4, 128, 512)
    return kernel_call(
        query_grads_kernel,
        prefetch=1,
        grid=(1,),
        in_specs=[whole_spec(arg.shape) for arg in args],
        out_specs=[whole_spec(shape)] * 4,
        out_shape=[struct(shape, bf16)] * 4,
        after=after,
        name="query_grads",
    )(place, *args)


def line_sum_kernel(place_ref, e0, e1, e2, e3, *outs):
    for step in range(4):
        z = (place_ref[0] // 4 + step) % 4
        outs[step][...] = sum(ref[z].astype(f32) for ref in (e0, e1, e2, e3)).astype(bf16)


def line_sums(place, terms, after=()):
    shape = terms[0].shape[1:]
    return kernel_call(
        line_sum_kernel,
        prefetch=1,
        grid=(1,),
        in_specs=[whole_spec(term.shape) for term in terms],
        out_specs=[whole_spec(shape)] * 4,
        out_shape=[struct(shape, bf16)] * 4,
        after=after,
        name="line_sums",
    )(place, *terms)


def final_sums_kernel(e0, e1, e2, e3, out_ref, kv_ref, sum_ref):
    sum_ref[:, :512] = sum_rows((e0, e1, e2, e3)).astype(bf16)
    sum_ref[:, 512:1024] = out_ref[...]
    sum_ref[:, 1024:] = jnp.sum(kv_ref[...].astype(f32), axis=0).astype(bf16)


def final_sums(q_terms, out_own, kv_terms, after=()):
    args = (*q_terms, out_own, kv_terms)
    return kernel_call(
        final_sums_kernel,
        grid=(1,),
        in_specs=[whole_spec(arg.shape) for arg in args],
        out_specs=whole_spec((128, 1152)),
        out_shape=struct((128, 1152), bf16),
        after=after,
        name="final_sums",
    )(*args)


def torus_shift(dz, dx):
    return [
        (z * 4 + x, ((z + dz) % 4) * 4 + (x + dx) % 4) for z in range(4) for x in range(4)
    ]


def along_x(values, step):
    return lax.ppermute(values, "grp", torus_shift(0, step))


def along_z(values, step):
    return lax.ppermute(values, "grp", torus_shift(step, 0))


def keyval_grads_kernel(
    place_ref, h0_ref, h1_ref, r0_ref, dkv_ref, cos_ref, sin_ref, out_ref, right_ref
):
    lane = lax.broadcasted_iota(jnp.int32, (SPAN, 128), 1)
    for i in range(2):
        rows = slice(i * SPAN, (i + 1) * SPAN)
        total = jnp.sum(dkv_ref[:, rows, :].astype(f32), axis=0)
        turned = total * cos_ref[rows, :] - partner(total) * sin_ref[rows, :]
        right_ref[rows, :] = jnp.where(lane < HEAD_DIM, turned, total).astype(bf16)
    total = dot_nn(h0_ref[...], r0_ref[...]) + dot_nn(h1_ref[...], right_ref[...])
    out_ref[...] = total.reshape(out_ref.shape)


def keyval_grads(place, h_turned, first_right, dkv, cos, sin, after=()):
    turn = pl.BlockSpec((2 * SPAN, 128), lambda i, place: (half_of(place, 1), 0))
    args = (*h_turned, first_right, dkv)
    return kernel_call(
        keyval_grads_kernel,
        prefetch=1,
        grid=(1,),
        in_specs=[whole_spec(arg.shape) for arg in args] + [turn, turn],
        out_specs=[whole_spec((GROUP, 128, 128)), whole_spec((2 * SPAN, 128))],
        out_shape=[struct((GROUP, 128, 128), f32), struct((2 * SPAN, 128), bf16)],
        after=after,
        name="keyval_grads",
    )(place, *args, cos, sin)


def project_back_kernel(q0_ref, q1_ref, r0_ref, r1_ref, wq_ref, wkv_ref, own_out, other_out):
    wq = wq_ref[...]
    wkv = wkv_ref[...].reshape(512, 128)
    for k, (q_ref, r_ref) in enumerate(((q0_ref, r0_ref), (q1_ref, r1_ref))):
        right = jnp.concatenate([q_ref[i] for i in range(4)], axis=1)
        d_h = (dot_nt(right, wq) + dot_nt(r_ref[...], wkv)).astype(bf16)
        spot = slice(k * SPAN, (k + 1) * SPAN)
        own_out[spot, :] = d_h[:SPAN]
        other_out[spot, :] = d_h[SPAN:]


def project_back(dqs, rights, wide_full, kv_full, after=()):
    args = (*dqs, *rights)
    out = pl.BlockSpec((2 * SPAN, 512), lambda i: (0, i))
    return kernel_call(
        project_back_kernel,
        grid=(4,),
        in_specs=[whole_spec(arg.shape) for arg in args]
        + [
            pl.BlockSpec((512, 512), lambda i: (i, 0)),
            pl.BlockSpec((4, 128, 128), lambda i: (i, 0, 0)),
        ],
        out_specs=[out, out],
        out_shape=[struct((2 * SPAN, D), bf16)] * 2,
        after=after,
        name="project_back",
    )(*args, wide_full, kv_full)


def as_rows(columns):
    return columns.T[:8, :]


def first_gain_kernel(wide_ref, kv_ref, own_ref, rep_ref, two_ref, two_rep, out_ref, copy_ref):
    grad = own_ref[...].astype(f32) + rep_ref[...].astype(f32)
    one = jnp.sum(wide_ref[...].astype(f32) * grad[:, :512], axis=1, keepdims=True)
    one = one + jnp.sum(kv_ref[...].astype(f32) * grad[:, 1024:], axis=1, keepdims=True)
    lane = lax.broadcasted_iota(jnp.int32, (128, 128), 1)
    out_ref[...] = as_rows(jnp.where(lane == 0, one, two_ref[...] + two_rep[...]))
    copy_ref[...] = rep_ref[...]


def gain_terms(wide_pack, kv_pack, sums, seconds, after=()):
    wide = pl.BlockSpec((128, 512), lambda i: (0, 0))
    args = (kv_pack, *sums, *seconds)
    return kernel_call(
        first_gain_kernel,
        grid=(1,),
        in_specs=[wide] + [whole_spec(arg.shape) for arg in args],
        out_specs=[whole_spec((8, 128)), whole_spec(sums[1].shape)],
        out_shape=[struct((8, 128), f32), struct(sums[1].shape, bf16)],
        after=after,
        name="gain_terms",
    )(wide_pack, *args)


def second_gain_kernel(pack_ref, sum_ref, held_ref, out_ref, copy_ref):
    total = jnp.zeros((pack_ref.shape[0], 1), f32)
    for column in range(0, WIDTH, 3 * TILE):
        span = slice(column, column + 2 * TILE)
        products = pack_ref[:, span].astype(f32) * sum_ref[:, span].astype(f32)
        total += jnp.sum(products, axis=1, keepdims=True)
    out_ref[...] = jnp.broadcast_to(total, out_ref.shape)
    copy_ref[...] = held_ref[...]


def second_gain_terms(mlp_pack, mlp_sum, held, after=()):
    args = (mlp_pack, mlp_sum, held)
    return kernel_call(
        second_gain_kernel,
        grid=(1,),
        in_specs=[whole_spec(arg.shape) for arg in args],
        out_specs=[whole_spec((128, 128)), whole_spec(held.shape)],
        out_shape=[struct((128, 128), f32), struct(held.shape, held.dtype)],
        after=after,
        name="second_gain_terms",
    )(*args)


def gain_adam_kernel(own, core, tp, both, w, m, s, w_o, m_o, s_o):
    total = (own[...] + core[...]) + (tp[...] + both[...])
    grad = total[:2, :] / w[...].astype(bf16).astype(f32)
    w_o[...], m_o[...], s_o[...] = adamw(w[...], m[...], s[...], grad, 1.0, 0.0)


def gain_adam(terms, states):
    args = (*terms, *[state.T for state in states])
    shape = args[-1].shape
    new = kernel_call(
        gain_adam_kernel,
        grid=(1,),
        in_specs=[whole_spec(arg.shape) for arg in args],
        out_specs=[whole_spec(shape)] * 3,
        out_shape=[struct(shape, f32)] * 3,
        name="gain_adam",
    )(*args)
    return [value.T for value in new]


def flat_view(values):
    rows, kinds, units = values.shape
    tiles = values.reshape(rows, kinds, units // SMALL, SMALL)
    tiles = with_layout_constraint(tiles, Layout(major_to_minor=(0, 2, 1, 3)))
    return tiles.transpose(0, 2, 1, 3).reshape(-1, SMALL)


def deep_view(values, shape):
    rows, kinds, units = shape
    tiles = values.reshape(rows, units // SMALL, kinds, SMALL).transpose(0, 2, 1, 3)
    tiles = with_layout_constraint(tiles, Layout(major_to_minor=(0, 2, 1, 3)))
    return tiles.reshape(shape)


def pack_kernel(quarter_ref, gu_ref, d_ref, out_ref):
    quarter = quarter_ref[0]
    start = window_start(quarter)
    stride = gu_ref.shape[0] // PACK_ROWS
    for tile in range(WINDOW_TILES):
        keep = jnp.where((quarter >= 2) & (tile == 0), 0.0, 1.0)
        for kind in range(3):
            if kind == 2:
                span = pl.ds(pl.multiple_of((start + tile) * SMALL, SMALL), SMALL)
                value = d_ref[:, span]
            else:
                value = gu_ref[pl.ds(2 * (start + tile) + kind, PACK_ROWS, stride), :]
            column = packed_column(tile, kind)
            out_ref[:, column : column + SMALL] = (value * keep).astype(bf16)


def pack_mlp(quarter, w_gateup, w_down, after=()):
    rows, units = w_down.shape
    per_row = 2 * units // SMALL
    return kernel_call(
        pack_kernel,
        prefetch=1,
        grid=(rows // PACK_ROWS,),
        in_specs=[
            pl.BlockSpec((PACK_ROWS * per_row, SMALL), lambda i, quarter: (i, 0)),
            pl.BlockSpec((PACK_ROWS, units), lambda i, quarter: (i, 0)),
        ],
        out_specs=pl.BlockSpec((PACK_ROWS, WIDTH), lambda i, quarter: (i, 0)),
        out_shape=struct((rows, WIDTH), bf16),
        after=after,
        name="pack_mlp",
    )(quarter, flat_view(w_gateup), w_down)


def mlp_adam_kernel(
    quarter_ref, own_ref, replica_ref, core_ref, both_ref, wg, mg, sg, wd, md, sd,
    wg_o, mg_o, sg_o, wd_o, md_o, sd_o, grads, *, rate_wide, rate_down,
):
    stride = wg.shape[0] // PACK_ROWS
    for part in range(4):
        same_core = quarter_ref[0] // 2 == part // 2
        same_replica = quarter_ref[0] % 2 == part % 2
        for tile in range(FIRST_OWN[part], FIRST_OWN[part + 1]):

            def grad(kind):
                column = packed_column(tile - WINDOW_STARTS[part], kind)
                spot = slice(column, column + SMALL)
                near = jnp.where(same_replica, own_ref[:, spot], replica_ref[:, spot])
                far = jnp.where(same_replica, core_ref[:, spot], both_ref[:, spot])
                return jnp.where(same_core, near, far).astype(f32)

            for kind in range(2):
                grads[pl.ds(2 * tile + kind, PACK_ROWS, stride), :] = grad(kind)
            span = slice(tile * SMALL, (tile + 1) * SMALL)
            wd_o[:, span], md_o[:, span], sd_o[:, span] = adamw(
                wd[:, span], md[:, span], sd[:, span], grad(2), rate_down, decay_rate
            )
    wg_o[...], mg_o[...], sg_o[...] = adamw(
        wg[...], mg[...], sg[...], grads[...], rate_wide, decay_rate
    )


def mlp_adam(quarter, sums, gateup, down, rate_wide, rate_down, after=()):
    rows, units = down[0].shape
    per_row = 2 * units // SMALL
    wide = pl.BlockSpec((PACK_ROWS * per_row, SMALL), lambda i, quarter: (i, 0))
    flat = pl.BlockSpec((PACK_ROWS, units), lambda i, quarter: (i, 0))
    grad = pl.BlockSpec((PACK_ROWS, WIDTH), lambda i, quarter: (i, 0))
    new = kernel_call(
        functools.partial(mlp_adam_kernel, rate_wide=rate_wide, rate_down=rate_down),
        prefetch=1,
        grid=(rows // PACK_ROWS,),
        in_specs=[grad] * 4 + [wide] * 3 + [flat] * 3,
        out_specs=[wide] * 3 + [flat] * 3,
        out_shape=[struct((rows * per_row, SMALL), f32)] * 3
        + [struct(down[0].shape, f32)] * 3,
        scratch_shapes=[pltpu.VMEM((PACK_ROWS * per_row, SMALL), f32)],
        after=after,
        name="mlp_adam",
    )(quarter, *sums, *[flat_view(state) for state in gateup], *down)
    return [deep_view(value, gateup[0].shape) for value in new[:3]] + list(new[3:])


def attn_adam_kernel(
    core_ref, own_ref, rep_ref, other_ref, both_ref, wq, mq, sq, wo, mo, so, wkv, mkv, skv,
    wq_o, mq_o, sq_o, wo_o, mo_o, so_o, wkv_o, mkv_o, skv_o, *, rate_wide, rate_out,
):
    mine = core_ref[0] == 0

    def halves(span):
        own = own_ref[:, span].astype(f32) + rep_ref[:, span].astype(f32)
        other = other_ref[:, span].astype(f32) + both_ref[:, span].astype(f32)
        return jnp.where(mine, own, other), jnp.where(mine, other, own)

    for i, grad in enumerate(halves(slice(0, 512))):
        span = slice(512 * i, 512 * (i + 1))
        wq_o[:, span], mq_o[:, span], sq_o[:, span] = adamw(
            wq[:, span], mq[:, span], sq[:, span], grad, rate_wide, decay_rate
        )
    for i, grad in enumerate(halves(slice(512, 1024))):
        span = slice(512 * i, 512 * (i + 1))
        wo_o[:, span], mo_o[:, span], so_o[:, span] = adamw(
            wo[:, span], mo[:, span], so[:, span], grad, rate_out, decay_rate
        )
    first, second = halves(slice(1024, 1152))
    low_half = lax.broadcasted_iota(jnp.int32, first.shape, 1) < HEAD_DIM
    grads = (
        jnp.where(low_half, first, pltpu.roll(second, HEAD_DIM, 1)),
        jnp.where(low_half, pltpu.roll(first, HEAD_DIM, 1), second),
    )
    for i, grad in enumerate(grads):
        wkv_o[:, i, :], mkv_o[:, i, :], skv_o[:, i, :] = adamw(
            wkv[:, i, :], mkv[:, i, :], skv[:, i, :], grad, rate_wide, decay_rate
        )


def attn_adam(core, sums, query, out, keyval, rate_wide, rate_out, after=()):
    rows = 32
    grad = pl.BlockSpec((rows, sums[0].shape[1]), lambda i, core: (i, 0))
    flat = pl.BlockSpec((rows, query[0].shape[1]), lambda i, core: (i, 0))
    deep = pl.BlockSpec((rows, *keyval[0].shape[1:]), lambda i, core: (i, 0, 0))
    new = kernel_call(
        functools.partial(attn_adam_kernel, rate_wide=rate_wide, rate_out=rate_out),
        prefetch=1,
        grid=(query[0].shape[0] // rows,),
        in_specs=[grad] * 4 + [flat] * 6 + [deep] * 3,
        out_specs=[flat] * 6 + [deep] * 3,
        out_shape=[struct(state.shape, f32) for state in (*query, *out, *keyval)],
        after=after,
        name="attn_adam",
    )(core, *sums, *query, *out, *keyval)
    return new[:3], new[3:6], new[6:]


def swap_core(values):
    return lax.ppermute(values, "rep", CORE_SWAP)


def swap_replica(values):
    return lax.ppermute(values, "rep", REPLICA_SWAP)


def swap_replica_core(values):
    return lax.ppermute(values, "rep", BOTH_CORES_SWAP)


def swap_tp(values):
    return lax.ppermute(values, "tp", TP_SWAP)


def swap_core_tp(values):
    return lax.ppermute(values, ("rep", "tp"), CORE_TP_SWAP)


def swap_both(values):
    return lax.ppermute(values, ("rep", "tp"), BOTH_SWAP)


def scatter_sums(parts, held=(), after=()):
    pairs = []
    for k in range(2):
        own, core, replica, both = parts[4 * k : 4 * k + 4]
        pairs += [(own, swap_core(core)), (replica, swap_core(both))]
    mine, replica, tp, both, *copies = add_quads(pairs, held=held, after=after)
    return mine, swap_replica(replica), swap_tp(tp), swap_both(both), *copies


def spread(values):
    return lax.all_to_all(values, "grp", 0, 0, tiled=False)


def on_device(
    tokens,
    cotangent,
    offsets,
    w_query,
    moment_query,
    square_query,
    w_keyval,
    moment_keyval,
    square_keyval,
    w_out,
    moment_out,
    square_out,
    w_gateup,
    moment_gateup,
    square_gateup,
    w_down,
    moment_down,
    square_down,
    norm_gains,
    moment_gains,
    square_gains,
):
    sequences, own_len, width = tokens.shape
    core = lax.axis_index("rep") % 2
    core_list = core.reshape(1).astype(jnp.int32)
    place = jnp.stack([lax.axis_index("grp"), lax.axis_index("tp")]).astype(jnp.int32)

    wide_pack, kv_pack, kv_copies = pack_attn(
        core_list, w_query, w_out, w_keyval, norm_gains.T
    )
    wide_full = lax.all_gather(wide_pack, "grp", axis=0, tiled=True)
    kv_full = spread(kv_copies)
    quarter = (2 * core + lax.axis_index("rep") // 2).reshape(1).astype(jnp.int32)
    x_other = swap_core(tokens)
    dy_replica = swap_replica(cotangent)
    dy_parts = (cotangent, swap_core(cotangent), dy_replica, swap_replica_core(cotangent))
    offsets_other = swap_core(offsets)
    offsets_all = jnp.stack([offsets, offsets_other], axis=1).reshape(2 * sequences, GROUP)
    steps_in = jnp.arange(own_len, dtype=jnp.int32)
    starts = lax.dynamic_slice_in_dim(offsets_all, place[0], 1, 1)
    positions = (starts + steps_in[None, :]).reshape(2 * sequences * own_len)
    half_dim = HEAD_DIM // 2
    inverse = rope_base ** (-2.0 * jnp.arange(half_dim, dtype=f32) / HEAD_DIM)
    angles = positions.astype(f32)[:, None] * inverse[None, :]
    cos_part = jnp.cos(angles)
    sin_part = jnp.sin(angles)
    cos = jnp.concatenate([cos_part] * 4, axis=1)
    sin = jnp.concatenate([-sin_part, sin_part] * 2, axis=1)

    kv_one = project_kv(1, place, tokens, x_other, kv_full, cos, sin)
    kv_zero = project_kv(
        0, place, tokens, x_other, kv_full, cos, sin, after=(kv_one[0], dy_replica)
    )
    h_turned = [kv_zero[1], kv_one[1]]
    kvs = {1: spread(kv_one[2])}
    kvs[0] = spread(kv_zero[2])
    dy_t = transposed(place, dy_parts, after=(kv_zero[0],))
    mlp_pack = pack_mlp(quarter, w_gateup, w_down, after=(kvs[1], dy_t))
    mlp_full = lax.all_gather(mlp_pack, "grp", axis=0, tiled=True)
    q_one = project_q(1, place, kv_one[0], wide_full, cos, sin, after=(mlp_pack,))
    one = attend(1, offsets_all, place, q_one, kvs[1], wide_full)
    one_share = add_low(one[2], swap_core(one[3]))
    q_zero = project_q(0, place, kv_zero[0], wide_full, cos, sin, after=(one[0],))
    qs = [q_zero, q_one]
    received = swap_tp(one_share)
    zero = attend(0, offsets_all, place, qs[0], kvs[0], wide_full, after=(one_share,))
    os_ = [zero[0], one[0]]
    lses = [zero[1], one[1]]
    zero_part = add_low(zero[2], received)
    mid, h_two = middle(place, tokens, zero_part, swap_core(zero[3]), kv_full)
    h_parts = []
    for first, second in ((h_two, swap_replica(h_two)), (swap_tp(h_two), swap_both(h_two))):
        h_parts += [first, swap_core(first), second, swap_core(second)]
    side, mlp_sums = mlp(place, h_parts, dy_parts, dy_t, mlp_full)
    mlp_own = lax.psum_scatter(mlp_sums, "grp", scatter_dimension=0, tiled=True)

    sums = scatter_sums(mlp_back(side, mlp_full, 0, 2))
    out_parts = mlp_back(side, mlp_full, 2, 1, after=(sums[0],))
    da = middle_back(place, sums, mid, cotangent, kv_full, after=(out_parts[0],))
    da_tp = swap_tp(da)
    da_parts = [da, swap_core(da)]

    def back_of(k, after=()):
        return attend_back(
            k, offsets_all, place, da_parts[2 * k], da_parts[2 * k + 1], wide_full, qs[k], kvs[k],
            os_[k], lses[k], cos, sin, after=after,
        )

    first_back = back_of(0)
    *out_shares, da_tp = scatter_sums(out_parts, held=(da_tp,), after=(first_back[0],))
    da_parts += [da_tp, swap_core(da_tp)]
    out_sums = out_grads(da_parts, os_, after=(out_shares[0],))
    out_own = lax.psum_scatter(out_sums, "grp", scatter_dimension=0, tiled=True)
    second_back = back_of(1, after=(out_sums,))
    dqs = [first_back[0], second_back[0]]
    gain_two, mlp_replica = second_gain_terms(
        mlp_pack, mlp_own, swap_replica(mlp_own), after=(second_back[0],)
    )
    first_right = right_side(0, place, spread(first_back[1]), cos, sin, after=(gain_two,))
    q_sums = query_grads(place, h_turned, dqs, after=(first_right,))
    rate_wide = 2.0 * D ** (-0.5)
    rate_out = 2.0 * max(1, 2 * D // LENGTH) ** (-0.5)
    rate_down = 2.0 * FF ** (-0.5)
    new_mlp = mlp_adam(
        quarter,
        (mlp_own, mlp_replica, swap_core(mlp_own), swap_core(mlp_replica)),
        (w_gateup, moment_gateup, square_gateup),
        (w_down, moment_down, square_down),
        rate_wide,
        rate_down,
        after=(q_sums[0],),
    )
    layer_mine = layer_part(mid, out_shares, after=(new_mlp[-1],))
    x_terms = [q_sums[0]] + [along_x(q_sums[i], i) for i in range(1, 4)]
    kv_sums, second_right = keyval_grads(
        place, h_turned, first_right, spread(second_back[1]), cos, sin, after=(layer_mine,)
    )
    layer_other = swap_tp(layer_mine)
    q_lines = line_sums(place, x_terms, after=(kv_sums, layer_other))
    rights = [first_right, second_right]
    gain_replica = swap_replica(gain_two)
    own_part, other_part = project_back(
        dqs, rights, wide_full, kv_full, after=(q_lines[0], gain_replica)
    )
    dh_share = add_low(own_part, swap_core(other_part))
    dh_received = swap_tp(dh_share)
    z_terms = [q_lines[0]] + [along_z(q_lines[i], i) for i in range(1, 4)]
    own = final_sums(z_terms, out_own, spread(kv_sums), after=(dh_share,))

    replica = swap_replica(own)
    input_grad, layer_out = row_outputs(
        place, layer_mine, layer_other, (da, da_parts[2]), dh_share, dh_received, tokens, kv_full,
        after=(own,),
    )
    gain_own, replica = gain_terms(
        wide_pack, kv_pack, (own, replica), (gain_two, gain_replica), after=(input_grad,)
    )
    new_query, new_out, new_keyval = attn_adam(
        core_list,
        (own, replica, swap_core(own), swap_core(replica)),
        (w_query, moment_query, square_query),
        (w_out, moment_out, square_out),
        (w_keyval, moment_keyval, square_keyval),
        rate_wide,
        rate_out,
        after=(gain_own,),
    )
    new_gains = gain_adam(
        (gain_own, swap_core(gain_own), swap_tp(gain_own), swap_core_tp(gain_own)),
        (norm_gains, moment_gains, square_gains),
    )
    return (
        layer_out,
        input_grad,
        *new_query,
        *new_keyval,
        *new_out,
        *new_mlp,
        *new_gains,
    )


def solution(mesh):
    rows = P("rep", "grp", None)
    flat = P("grp", "tp")
    deep = P("grp", None, "tp")
    states = (flat,) * 3 + (deep,) * 3 + (flat,) * 3 + (deep,) * 3 + (flat,) * 3
    states += (P("grp", None),) * 3
    return jax.shard_map(
        on_device,
        mesh=mesh,
        in_specs=(rows, rows, P("rep", None)) + states,
        out_specs=(rows, rows) + states,
        check_vma=False,
    )
```
